128 devices in a mesh: dp: 128 (over y, z, x, core).
Axes of the slice: x: 4, y: 4, z: 4, core: 2. Of those that a mesh axis runs over, the one named last changes fastest.
Arguments:
- embeddings: bfloat16 [16384, 1024], P('dp')
- positives: int32 [16384], P('dp'), may hold values from 0 to 16383, as said below
Outputs:
- loss: float32 [], replicated
- grad: float32 [16384, 1024], P('dp')
The draws below stay inside these ranges and needn't reach their ends.
Inputs may be any that keep to these rules, and one draw needn't show every extreme that they name: positives is a perfect matching of the rows: positives[positives[i]] = i and positives[i] != i.
All inputs are finite; a program needn't handle non-finite values.
Results may differ from the reference program's by a relative error of at most 0.002.
Values may be sent and summed in bfloat16 or wider, within the bound.
A program may use at most 128 MiB of HBM per device.

```python
import math
import jax
import jax.numpy as jnp
from jax import lax

D = 1024
ITERS = 3
ROWS = 16384


def pairing(key):
    order = jax.random.permutation(jax.random.fold_in(key, 5), ROWS).astype(jnp.int32)
    evens = order[0::2]
    odds = order[1::2]
    partner = jnp.zeros((ROWS,), jnp.int32)
    partner = partner.at[evens].set(odds)
    partner = partner.at[odds].set(evens)
    return partner


def mix_rows(shared, own, low, high):
    rowid = jnp.arange(ROWS).astype(jnp.float32)
    strength = low + (high - low) * rowid / (ROWS - 1)
    return strength[:, None] * shared + jnp.sqrt(1.0 - strength * strength)[:, None] * own


def draw_embeddings(key, part):
    partner = pairing(key)
    key = jax.random.fold_in(key, 11)
    first = jax.random.fold_in(key, 0)
    fourth = jax.random.fold_in(key, 3)
    rowid = jnp.arange(ROWS)
    image = jnp.minimum(rowid, partner)
    common = jax.random.normal(fourth, (ROWS, D))[image]
    own = jax.random.normal(first, (ROWS, D))
    values = jnp.clip(mix_rows(common, own, 0.15, 0.6), -6.0, 6.0)
    return values.astype(jnp.bfloat16)


def draw_positives(key, part):
    return pairing(key)


def setup_inputs(seed: int = 0) -> dict:
    arg_keys = jax.random.split(jax.random.key(seed), 3)
    embeddings = draw_embeddings(jax.random.fold_in(arg_keys[2], 71), 0)
    positives = draw_positives(jax.random.fold_in(arg_keys[2], 71), 0)
    return {"embeddings": embeddings, "positives": positives}


def reference(embeddings, positives):
    total = embeddings.shape[0]
    scale = 1.0 / math.sqrt(D)
    scores = jnp.dot(embeddings, embeddings.T, preferred_element_type=jnp.float32) * scale
    index = jnp.arange(total, dtype=jnp.int32)
    scores = jnp.where(index[:, None] == index[None, :], -30000.0, scores)
    potential = jnp.zeros((total,), scores.dtype)
    previous = []
    lse_list = []
    for step in range(ITERS):
        lse = jax.nn.logsumexp(scores + potential[None, :], axis=1)
        previous.append(potential)
        lse_list.append(lse)
        potential = (potential - lse) / 2
    picked = scores[index, positives]
    loss = -jnp.sum(picked + potential + potential[positives]) / total
    counts = jax.ops.segment_sum(jnp.ones((total,), scores.dtype), positives, total)
    cotangent = -(1.0 + counts)
    direct = -(index[None, :] == positives[:, None]).astype(scores.dtype)
    weights = direct + direct.T
    for step in reversed(range(ITERS)):
        pull = -cotangent / 2
        plan = jnp.exp(scores + previous[step][None, :] - lse_list[step][:, None])
        term = pull[:, None] * plan
        weights = weights + term + term.T
        cotangent = cotangent / 2 + lax.optimization_barrier(jnp.sum(term, axis=0))
    grad = jnp.dot(weights.astype(jnp.bfloat16), embeddings, preferred_element_type=jnp.float32) * scale
    return (loss, grad)
```

```python
import functools
import math

import jax
import jax.numpy as jnp
from jax import lax
from jax.experimental import pallas as pl
from jax.experimental.pallas import tpu as pltpu
from jax.sharding import PartitionSpec as P

SIDE = 4
PLANE = SIDE * SIDE
LINE = SIDE * 2
BLOCK = 128
WIDTH = 1024
RROWS = LINE * BLOCK
CCOLS = PLANE * BLOCK
TOTAL = PLANE * RROWS
LOG2E = math.log2(math.e)
LN2 = math.log(2.0)
MESH = pl.DeviceIdType.MESH
F32 = jnp.float32
BF16 = jnp.bfloat16
CH = 32
OFFS = (0, -1, 1, 2)


def fold(v, op):
    out = v[0:8]
    for r in range(8, v.shape[0], 8):
        out = op(out, v[r : r + 8])
    return out


def log2(v):
    return jnp.log(v) * LOG2E


def kernel(
    emb, pos, grad, loss,
    ec, er, s, w, wb, rvec, cvec, pr_ref, mr, accr, cmsg, crx, rmsg, rrx,
    gp, rb, xs2, xr2, xs1, xr1,
    lsem, psend, prsem, xsend, xrsem, csend, crecv, rsend, rrecv, gsend, grecv, hsend, hrecv,
):
    me = lax.axis_index("dp")
    a = me // LINE
    b = me % LINE
    y, z = a // SIDE, a % SIDE
    x, core = b // 2, b % 2

    def in_plane(k):
        return lax.rem(a + k, PLANE) * LINE + b

    def in_line(k):
        return a * LINE + lax.rem(b + k, LINE)

    barrier = pltpu.get_barrier_semaphore()

    def greet_plane(k, carry):
        pl.semaphore_signal(barrier, inc=1, device_id=(in_plane(k),), device_id_type=MESH)
        return carry

    def greet_line(k, carry):
        pl.semaphore_signal(barrier, inc=1, device_id=(in_line(k),), device_id_type=MESH)
        return carry

    lax.fori_loop(1, PLANE, greet_plane, 0)
    lax.fori_loop(1, LINE, greet_line, 0)
    own_c = pltpu.make_async_copy(emb, ec.at[a], lsem.at[0])
    own_r = pltpu.make_async_copy(emb, er.at[b], lsem.at[1])
    own_c.start()
    own_r.start()
    pl.semaphore_wait(barrier, PLANE - 1 + LINE - 1)

    def blk(h, op, oq):
        dy, dz = (oq, op) if h == 0 else (op, oq)
        return lax.rem(y + dy + SIDE, SIDE) * SIDE + lax.rem(z + dz + SIDE, SIDE)

    def send_plane(h, op, oq, lo, n, tp, tq, idx):
        k = blk(h, op, oq)
        rows = pl.ds(64 * h + lo, n)
        src = emb.at[rows] if (op, oq) == (0, 0) else ec.at[k, rows]
        pltpu.make_async_remote_copy(
            src_ref=src, dst_ref=ec.at[k, rows], send_sem=psend, recv_sem=prsem.at[h, idx],
            device_id=(blk(h, tp, tq) * LINE + b,), device_id_type=MESH,
        ).start()

    def wait_plane(h, op, oq, lo, n, idx):
        ref = ec.at[blk(h, op, oq), pl.ds(64 * h + lo, n)]
        pltpu.make_async_copy(ref, ref, prsem.at[h, idx]).wait()

    def xdev(dx):
        return a * LINE + lax.rem(x + dx + SIDE, SIDE) * 2 + core

    sibling = a * LINE + x * 2 + (1 - core)

    def xblk(dx):
        return lax.rem(x + dx + SIDE, SIDE) * 2 + core

    def send_line(dx, lo, n, device, idx):
        k = xblk(dx)
        rows = pl.ds(lo, n)
        src = emb.at[rows] if dx == 0 else er.at[k, rows]
        pltpu.make_async_remote_copy(
            src_ref=src, dst_ref=er.at[k, rows], send_sem=xsend, recv_sem=xrsem.at[idx],
            device_id=(device,), device_id_type=MESH,
        ).start()

    def wait_line(k, lo, n, idx):
        ref = er.at[k, pl.ds(lo, n)]
        pltpu.make_async_copy(ref, ref, xrsem.at[idx]).wait()

    for h in (0, 1):
        send_plane(h, 0, 0, 0, 64, 1, 0, 0)
        send_plane(h, 0, 0, 0, 64, -1, 0, 1)
    send_line(0, 0, 128, xdev(1), 0)
    send_line(0, 0, 128, xdev(-1), 1)
    send_line(0, 0, 128, sibling, 4)
    for h in (0, 1):
        send_plane(h, 0, 0, 0, 64, 0, 1, 4)
        send_plane(h, 0, 0, 0, 64, 0, -1, 5)
    for h in (0, 1):
        wait_plane(h, -1, 0, 0, 64, 0)
        send_plane(h, -1, 0, 0, 32, 1, 0, 2)
        wait_plane(h, 1, 0, 0, 64, 1)
        send_plane(h, 1, 0, 32, 32, -1, 0, 3)
    wait_line(xblk(-1), 0, 128, 0)
    send_line(-1, 0, 64, xdev(1), 2)
    send_line(-1, 0, 128, sibling, 5)
    wait_line(xblk(1), 0, 128, 1)
    send_line(1, 64, 64, xdev(-1), 3)
    send_line(1, 0, 128, sibling, 6)
    for h in (0, 1):
        for oi in (1, 2):
            send_plane(h, OFFS[oi], 0, 0, 64, 0, 1, 4 + 4 * oi)
            send_plane(h, OFFS[oi], 0, 0, 64, 0, -1, 5 + 4 * oi)
    for h in (0, 1):
        wait_plane(h, 0, -1, 0, 64, 4)
        send_plane(h, 0, -1, 0, 32, 0, 1, 6)
        wait_plane(h, 0, 1, 0, 64, 5)
        send_plane(h, 0, 1, 32, 32, 0, -1, 7)
    for h in (0, 1):
        wait_plane(h, 2, 0, 0, 32, 2)
        wait_plane(h, 2, 0, 32, 32, 3)
        send_plane(h, 2, 0, 0, 64, 0, 1, 16)
        send_plane(h, 2, 0, 0, 64, 0, -1, 17)
    wait_line(xblk(2), 0, 64, 2)
    wait_line(xblk(2), 64, 64, 3)
    send_line(2, 0, 128, sibling, 7)
    for oi in (1, 2, 3):
        o = OFFS[oi]
        for h in (0, 1):
            wait_plane(h, o, -1, 0, 64, 4 + 4 * oi)
            send_plane(h, o, -1, 0, 32, 0, 1, 6 + 4 * oi)
            wait_plane(h, o, 1, 0, 64, 5 + 4 * oi)
            send_plane(h, o, 1, 32, 32, 0, -1, 7 + 4 * oi)
    for i, dx in enumerate((0, -1, 1, 2)):
        wait_line(lax.rem(x + dx + SIDE, SIDE) * 2 + (1 - core), 0, 128, 4 + i)
    for oi in range(4):
        for h in (0, 1):
            wait_plane(h, OFFS[oi], 2, 0, 32, 6 + 4 * oi)
            wait_plane(h, OFFS[oi], 2, 32, 32, 7 + 4 * oi)
    own_c.wait()
    own_r.wait()

    score_scale = LOG2E / math.sqrt(WIDTH)

    def score_tile(t, carry):
        n, m = t // 4, t % 4
        left = er[pl.ds(2 * m, 2)].reshape(2 * BLOCK, WIDTH)
        right = ec[pl.ds(2 * n, 2)].reshape(2 * BLOCK, WIDTH)
        out = lax.dot_general(left, right, (((1,), (1,)), ((), ())), preferred_element_type=F32)
        s[pl.ds(pl.multiple_of(m * 256, 256), 256), pl.ds(pl.multiple_of(n * 256, 256), 256)] = out * score_scale
        return carry

    lax.fori_loop(0, 32, score_tile, 0)
    eye = lax.broadcasted_iota(jnp.int32, (BLOCK, BLOCK), 0) == lax.broadcasted_iota(jnp.int32, (BLOCK, BLOCK), 1)
    dr = pl.ds(pl.multiple_of(b * BLOCK, BLOCK), BLOCK)
    dc = pl.ds(pl.multiple_of(a * BLOCK, BLOCK), BLOCK)
    s[dr, dc] = jnp.where(eye, -30000.0 * LOG2E, s[dr, dc])

    def rows_at(i):
        return pl.ds(pl.multiple_of(i * CH, CH), CH)

    def lanes(k):
        return slice(k * BLOCK, (k + 1) * BLOCK)

    def to_rows(v, ref):
        for g in range(LINE):
            ref[pl.ds(g * BLOCK, BLOCK), :] = jnp.broadcast_to(v[g : g + 1], (BLOCK, BLOCK)).T

    def from_rows(ref):
        out = []
        for g in range(LINE):
            v = jnp.where(eye, ref[pl.ds(g * BLOCK, BLOCK), :], 0.0)
            out.append(jnp.sum(v, axis=0, keepdims=True))
        return jnp.concatenate(out, axis=0)

    def exchange(e):
        def to_plane(k, carry):
            pltpu.make_async_remote_copy(
                src_ref=cmsg.at[e], dst_ref=crx.at[e, a], send_sem=csend.at[e], recv_sem=crecv.at[e],
                device_id=(in_plane(k),), device_id_type=MESH,
            ).start()
            return carry

        def to_line(k, carry):
            pltpu.make_async_remote_copy(
                src_ref=rmsg.at[e], dst_ref=rrx.at[e, b], send_sem=rsend.at[e], recv_sem=rrecv.at[e],
                device_id=(in_line(k),), device_id_type=MESH,
            ).start()
            return carry

        lax.fori_loop(1, LINE, to_line, 0)
        lax.fori_loop(1, PLANE, to_plane, 0)
        crx[e, a] = cmsg[e]
        rrx[e, b] = rmsg[e]
        call = crx.at[e, pl.ds(0, PLANE - 1)]
        rall = rrx.at[e, pl.ds(0, LINE - 1)]
        pltpu.make_async_copy(rall, rall, rrecv.at[e]).wait()
        pltpu.make_async_copy(call, call, crecv.at[e]).wait()
        pltpu.make_async_copy(rall, rall, rsend.at[e]).wait()
        pltpu.make_async_copy(call, call, csend.at[e]).wait()

    def merge(v):
        top = jnp.max(v, axis=0)
        return top + log2(jnp.sum(jnp.exp2(v - top[None]), axis=0))

    def forward(t):
        pot_r, pot_c = rvec.at[t - 2], cvec.at[t - 2]

        def top_step(i, tops):
            rows = rows_at(i)
            if t > 1:
                pr = pot_r[rows, :]
            best = None
            out = []
            for k in range(PLANE):
                v = s[rows, lanes(k)]
                u = v + pot_c[k : k + 1, :] if t > 1 else v
                q = v + pr if t > 1 else v
                best = u if best is None else jnp.maximum(best, u)
                out.append(jnp.maximum(tops[k], fold(q, jnp.maximum)))
            mr[rows, :] = jnp.broadcast_to(jnp.max(best, axis=1, keepdims=True), (CH, BLOCK))
            return tuple(out)

        low = jnp.full((8, BLOCK), -jnp.inf, F32)
        tops = lax.fori_loop(0, RROWS // CH, top_step, (low,) * PLANE)
        ctop = jnp.concatenate([jnp.max(v, axis=0, keepdims=True) for v in tops], axis=0)
        cvec[7] = ctop

        def sum_step(i, sums):
            rows = rows_at(i)
            m = mr[rows, :]
            if t > 1:
                pr = pot_r[rows, :]
            acc = None
            out = []
            for k in range(PLANE):
                v = s[rows, lanes(k)]
                u = v + pot_c[k : k + 1, :] if t > 1 else v
                q = v + pr if t > 1 else v
                p = jnp.exp2(u - m)
                acc = p if acc is None else acc + p
                out.append(sums[k] + fold(jnp.exp2(q - cvec[7, k : k + 1, :]), jnp.add))
            total = jnp.sum(acc, axis=1, keepdims=True)
            accr[rows, :] = m + log2(jnp.broadcast_to(total, (CH, BLOCK)))
            return tuple(out)

        zero = jnp.zeros((8, BLOCK), F32)
        sums = lax.fori_loop(0, RROWS // CH, sum_step, (zero,) * PLANE)
        csum = jnp.concatenate([jnp.sum(v, axis=0, keepdims=True) for v in sums], axis=0)
        cmsg[t - 1, 0:PLANE, :] = ctop + log2(csum)
        rmsg[t - 1, 0:LINE, :] = from_rows(accr)
        if t == 1:
            rmsg[0, LINE : LINE + 8, :] = jnp.broadcast_to(pos[...].astype(F32), (8, BLOCK))
        exchange(t - 1)
        lse_c = merge(crx[t - 1, :, 0:PLANE, :])
        lse_r = merge(rrx[t - 1, :, 0:LINE, :])
        return lse_r, lse_c

    cmsg[...] = jnp.zeros_like(cmsg)
    rmsg[...] = jnp.zeros_like(rmsg)
    pot_r = jnp.zeros((LINE, BLOCK), F32)
    pot_c = jnp.zeros((PLANE, BLOCK), F32)
    for t in (1, 2, 3):
        lse_r, lse_c = forward(t)
        pot_r = (pot_r - lse_r) * 0.5
        pot_c = (pot_c - lse_c) * 0.5
        to_rows(lse_r, rvec.at[t + 1])
        cvec[t + 1] = lse_c
        if t < 3:
            to_rows(pot_r, rvec.at[t - 1])
            cvec[t - 1] = pot_c
        if t == 1:
            to_rows(jnp.concatenate([rrx[0, g, LINE : LINE + 1, :] for g in range(LINE)], axis=0), pr_ref)

    first_col = (lax.broadcasted_iota(jnp.int32, (8, BLOCK), 1) + b * BLOCK).astype(F32)
    first_col = jnp.broadcast_to(first_col[0:1], (CH, BLOCK))

    def backward(t):
        pot_rr, pot_cc = rvec.at[t - 2], cvec.at[t - 2]
        lse_rr, lse_cc = rvec.at[t + 1], cvec.at[t + 1]
        pull_rr, pull_cc = rvec.at[7 - t], cvec.at[7 - t]

        def step(i, carry):
            sums, picked = carry
            rows = rows_at(i)
            lr = lse_rr[rows, :]
            if t > 1:
                pr = pot_rr[rows, :]
            if t < 3:
                qr = pull_rr[rows, :]
            else:
                partner = pr_ref[rows, :] - first_col
            acc = None
            out = []
            for k in range(PLANE):
                v = s[rows, lanes(k)]
                u = v + pot_cc[k : k + 1, :] if t > 1 else v
                q = v + pr if t > 1 else v
                term = jnp.exp2(u - lr)
                mirror = jnp.exp2(q - lse_cc[k : k + 1, :])
                if t < 3:
                    term = term * qr
                    mirror = mirror * pull_cc[k : k + 1, :]
                    total = w[rows, lanes(k)] + (term + mirror)
                else:
                    hit = partner == float(k * RROWS)
                    picked = picked + fold(jnp.where(hit, v, 0.0), jnp.add)
                    total = jnp.where(hit, -2.0, 0.0) + (term + mirror)
                if t > 1:
                    w[rows, lanes(k)] = total
                    out.append(sums[k] + fold(term, jnp.add))
                    acc = mirror if acc is None else acc + mirror
                else:
                    wb[rows, lanes(k)] = total.astype(BF16)
            if t > 1:
                accr[rows, :] = jnp.broadcast_to(jnp.sum(acc, axis=1, keepdims=True), (CH, BLOCK))
            return tuple(out), picked

        zero = jnp.zeros((8, BLOCK), F32)
        sums, picked = lax.fori_loop(0, RROWS // CH, step, ((zero,) * (PLANE if t > 1 else 0), zero))
        if t == 1:
            return None
        e = 6 - t
        cmsg[e, 0:PLANE, :] = jnp.concatenate([jnp.sum(v, axis=0, keepdims=True) for v in sums], axis=0)
        rmsg[e, 0:LINE, :] = from_rows(accr)
        if t == 3:
            cmsg[e, PLANE : PLANE + 8, :] = picked
        return e

    e = backward(3)
    exchange(e)
    cot_r = -1.0 + jnp.sum(rrx[e, :, 0:LINE, :], axis=0)
    cot_c = -1.0 + jnp.sum(crx[e, :, 0:PLANE, :], axis=0)
    picked = jnp.sum(crx[e, :, PLANE : PLANE + 8, :], axis=0)
    to_rows(-0.5 * cot_r, rvec.at[5])
    cvec[5] = -0.5 * cot_c
    e = backward(2)
    rmsg[e, LINE : LINE + 8, :] = picked + 2.0 * (pot_c[0:8] + pot_c[8:16])
    exchange(e)
    cot_r = 0.5 * cot_r + jnp.sum(rrx[e, :, 0:LINE, :], axis=0)
    cot_c = 0.5 * cot_c + jnp.sum(crx[e, :, 0:PLANE, :], axis=0)
    whole = jnp.sum(rrx[e, :, LINE : LINE + 8, :], axis=0)
    loss[0, 0] = jnp.sum(whole) * (-LN2 / TOTAL)
    to_rows(-0.5 * cot_r, rvec.at[6])
    cvec[6] = -0.5 * cot_c
    backward(1)

    grad_scale = 1.0 / math.sqrt(WIDTH)

    def partial(d):
        xx = lax.rem(x + d, SIDE)
        rows = pl.ds(pl.multiple_of(xx * 256, 256), 256)

        def tile(n, carry):
            cols = pl.ds(pl.multiple_of(n * 256, 256), 256)
            right = ec[:, :, cols].reshape(CCOLS, 256)
            out = jnp.dot(wb[rows, :], right, preferred_element_type=F32) * grad_scale
            gp[d, :, :, cols] = out.reshape(2, BLOCK, 256)
            return carry

        lax.fori_loop(0, WIDTH // 256, tile, 0)
        pltpu.make_async_remote_copy(
            src_ref=gp.at[d, 1 - core], dst_ref=rb.at[d], send_sem=gsend.at[d], recv_sem=grecv.at[d],
            device_id=(sibling,), device_id_type=MESH,
        ).start()

    def chip_sum(d):
        pltpu.make_async_copy(rb.at[d], rb.at[d], grecv.at[d]).wait()
        return gp[d, core] + rb[d]

    def ring(src, dst, i, device):
        return pltpu.make_async_remote_copy(
            src_ref=src, dst_ref=dst, send_sem=hsend.at[i], recv_sem=hrecv.at[i],
            device_id=(device,), device_id_type=MESH,
        )

    half = WIDTH // 2
    far = [ring(xs2.at[i], xr2.at[i], i, xdev(dx)) for i, dx in ((0, 1), (1, -1))]
    near = [ring(xs1.at[i], xr1.at[i], 2 + i, xdev(dx)) for i, dx in ((0, 1), (1, -1))]
    partial(2)
    partial(1)
    v = chip_sum(2).astype(BF16)
    xs2[0] = v[:, :half]
    xs2[1] = v[:, half:]
    far[0].start()
    far[1].start()
    partial(3)
    v = chip_sum(1)
    far[0].wait_recv()
    xs1[0, :, :half] = (v[:, :half] + xr2[0].astype(F32)).astype(BF16)
    xs1[0, :, half:] = v[:, half:].astype(BF16)
    near[0].start()
    partial(0)
    v = chip_sum(3)
    far[1].wait_recv()
    xs1[1, :, :half] = v[:, :half].astype(BF16)
    xs1[1, :, half:] = (v[:, half:] + xr2[1].astype(F32)).astype(BF16)
    near[1].start()
    v = chip_sum(0)
    near[0].wait_recv()
    v = v + xr1[0].astype(F32)
    near[1].wait_recv()
    grad[...] = v + xr1[1].astype(F32)

    sent = ec.at[pl.ds(0, PLANE - 1)]
    pltpu.make_async_copy(sent, sent, psend).wait()
    sent = er.at[pl.ds(0, LINE - 1)]
    pltpu.make_async_copy(sent, sent, xsend).wait()
    for d in range(SIDE):
        pltpu.make_async_copy(rb.at[d], rb.at[d], gsend.at[d]).wait()
    for c in far + near:
        c.wait_send()


def shards(embeddings, positives):
    vec = pltpu.VMEM
    dma = pltpu.SemaphoreType.DMA
    grad, loss = pl.pallas_call(
        kernel,
        out_shape=(
            jax.ShapeDtypeStruct((BLOCK, WIDTH), F32),
            jax.ShapeDtypeStruct((1, 1), F32),
        ),
        in_specs=[pl.BlockSpec(memory_space=pl.ANY), pl.BlockSpec(memory_space=pltpu.VMEM)],
        out_specs=(pl.BlockSpec(memory_space=pltpu.VMEM), pl.BlockSpec(memory_space=pltpu.SMEM)),
        scratch_shapes=[
            vec((PLANE, BLOCK, WIDTH), BF16),
            vec((LINE, BLOCK, WIDTH), BF16),
            vec((RROWS, CCOLS), F32),
            vec((RROWS, CCOLS), F32),
            vec((RROWS, CCOLS), BF16),
            vec((7, RROWS, BLOCK), F32),
            vec((8, PLANE, BLOCK), F32),
            vec((RROWS, BLOCK), F32),
            vec((RROWS, BLOCK), F32),
            vec((RROWS, BLOCK), F32),
            vec((5, PLANE + 8, BLOCK), F32),
            vec((5, PLANE, PLANE + 8, BLOCK), F32),
            vec((5, LINE + 8, BLOCK), F32),
            vec((5, LINE, LINE + 8, BLOCK), F32),
            vec((SIDE, 2, BLOCK, WIDTH), F32),
            vec((SIDE, BLOCK, WIDTH), F32),
            vec((2, BLOCK, WIDTH // 2), BF16),
            vec((2, BLOCK, WIDTH // 2), BF16),
            vec((2, BLOCK, WIDTH), BF16),
            vec((2, BLOCK, WIDTH), BF16),
            dma((2,)),
            dma,
            dma((2, 20)),
            dma,
            dma((8,)),
            dma((5,)),
            dma((5,)),
            dma((5,)),
            dma((5,)),
            dma((SIDE,)),
            dma((SIDE,)),
            dma((4,)),
            dma((4,)),
        ],
        compiler_params=pltpu.CompilerParams(
            collective_id=0, has_side_effects=True, vmem_limit_bytes=56 * 1024 * 1024
        ),
    )(embeddings, positives.reshape(1, BLOCK))
    return loss.reshape(()), grad


def solution(mesh):
    placed = (P("dp", None), P("dp"))
    return jax.shard_map(
        shards, mesh=mesh, in_specs=placed, out_specs=(P(), P("dp", None)), check_vma=False
    )
```

```python
import functools
import math

import jax
import jax.numpy as jnp
from jax import lax
from jax.experimental import pallas as pl
from jax.experimental.pallas import tpu as pltpu
from jax.sharding import PartitionSpec as P

SIDE = 4
PLANE = SIDE * SIDE
LINE = SIDE * 2
BLOCK = 128
WIDTH = 1024
RROWS = LINE * BLOCK
CCOLS = PLANE * BLOCK
TOTAL = PLANE * RROWS
LOG2E = math.log2(math.e)
LN2 = math.log(2.0)
MESH = pl.DeviceIdType.MESH
F32 = jnp.float32
BF16 = jnp.bfloat16
SCORE_M = 4
CH = 32
OFFS = (0, -1, 1, 2)


def fold(v, op):
    out = v[0:8]
    for r in range(8, v.shape[0], 8):
        out = op(out, v[r : r + 8])
    return out


def log2(v):
    return jnp.log(v) * LOG2E


def kernel(
    emb, pos, grad, loss,
    ec, er, s, w, wb, rvec, cvec, pr_ref, mr, accr, cmsg, crx, rmsg, rrx,
    gp, rb, xs2, xr2, xs1, xr1,
    lsem, psend, prsem, xsend, xrsem, csend, crecv, rsend, rrecv, gsend, grecv, hsend, hrecv,
):
    me = lax.axis_index("dp")
    a = me // LINE
    b = me % LINE
    y, z = a // SIDE, a % SIDE
    x, core = b // 2, b % 2

    def in_plane(k):
        return lax.rem(a + k, PLANE) * LINE + b

    def in_line(k):
        return a * LINE + lax.rem(b + k, LINE)

    def dev_of(dy, dz, dx, c):
        yy, zz, xx = (lax.rem(v + d + SIDE, SIDE) for v, d in ((y, dy), (z, dz), (x, dx)))
        return ((yy * SIDE + zz) * SIDE + xx) * 2 + c

    barrier = pltpu.get_barrier_semaphore()

    near_by = (
        [dev_of(dy, dz, dx, core) for dy, dz, dx in ((1, 0, 0), (-1, 0, 0), (0, 1, 0), (0, -1, 0), (0, 0, 1), (0, 0, -1))]
        + [dev_of(0, 0, 0, 1 - core)]
    )
    for device in near_by:
        pl.semaphore_signal(barrier, inc=1, device_id=(device,), device_id_type=MESH)
    own_c = pltpu.make_async_copy(emb, ec.at[a], lsem.at[0])
    own_r = pltpu.make_async_copy(emb, er.at[b], lsem.at[1])
    own_c.start()
    own_r.start()
    pl.semaphore_wait(barrier, len(near_by))

    def blk(h, op, oq):
        dy, dz = (oq, op) if h == 0 else (op, oq)
        return lax.rem(y + dy + SIDE, SIDE) * SIDE + lax.rem(z + dz + SIDE, SIDE)

    def send_plane(h, op, oq, lo, n, tp, tq, idx):
        k = blk(h, op, oq)
        rows = pl.ds(64 * h + lo, n)
        src = emb.at[rows] if (op, oq) == (0, 0) else ec.at[k, rows]
        pltpu.make_async_remote_copy(
            src_ref=src, dst_ref=ec.at[k, rows], send_sem=psend, recv_sem=prsem.at[h, idx],
            device_id=(blk(h, tp, tq) * LINE + b,), device_id_type=MESH,
        ).start()

    def wait_plane(h, op, oq, lo, n, idx):
        ref = ec.at[blk(h, op, oq), pl.ds(64 * h + lo, n)]
        pltpu.make_async_copy(ref, ref, prsem.at[h, idx]).wait()

    def xdev(dx):
        return a * LINE + lax.rem(x + dx + SIDE, SIDE) * 2 + core

    sibling = a * LINE + x * 2 + (1 - core)

    def xblk(dx):
        return lax.rem(x + dx + SIDE, SIDE) * 2 + core

    def send_line(dx, lo, n, device, idx):
        k = xblk(dx)
        rows = pl.ds(lo, n)
        src = emb.at[rows] if dx == 0 else er.at[k, rows]
        pltpu.make_async_remote_copy(
            src_ref=src, dst_ref=er.at[k, rows], send_sem=xsend, recv_sem=xrsem.at[idx],
            device_id=(device,), device_id_type=MESH,
        ).start()

    def wait_line(k, lo, n, idx):
        ref = er.at[k, pl.ds(lo, n)]
        pltpu.make_async_copy(ref, ref, xrsem.at[idx]).wait()

    for h in (0, 1):
        send_plane(h, 0, 0, 0, 64, 1, 0, 0)
        send_plane(h, 0, 0, 0, 64, -1, 0, 1)
    send_line(0, 0, 128, xdev(1), 0)
    send_line(0, 0, 128, xdev(-1), 1)
    send_line(0, 0, 128, sibling, 4)
    for h in (0, 1):
        send_plane(h, 0, 0, 0, 64, 0, 1, 4)
        send_plane(h, 0, 0, 0, 64, 0, -1, 5)
    for h in (0, 1):
        wait_plane(h, -1, 0, 0, 64, 0)
        send_plane(h, -1, 0, 0, 32, 1, 0, 2)
        wait_plane(h, 1, 0, 0, 64, 1)
        send_plane(h, 1, 0, 32, 32, -1, 0, 3)
    wait_line(xblk(-1), 0, 128, 0)
    send_line(-1, 0, 64, xdev(1), 2)
    send_line(-1, 0, 128, sibling, 5)
    wait_line(xblk(1), 0, 128, 1)
    send_line(1, 64, 64, xdev(-1), 3)
    send_line(1, 0, 128, sibling, 6)
    for h in (0, 1):
        for oi in (1, 2):
            send_plane(h, OFFS[oi], 0, 0, 64, 0, 1, 4 + 4 * oi)
            send_plane(h, OFFS[oi], 0, 0, 64, 0, -1, 5 + 4 * oi)
    for h in (0, 1):
        wait_plane(h, 0, -1, 0, 64, 4)
        send_plane(h, 0, -1, 0, 32, 0, 1, 6)
        wait_plane(h, 0, 1, 0, 64, 5)
        send_plane(h, 0, 1, 32, 32, 0, -1, 7)
    for h in (0, 1):
        wait_plane(h, 2, 0, 0, 32, 2)
        wait_plane(h, 2, 0, 32, 32, 3)
        send_plane(h, 2, 0, 0, 64, 0, 1, 16)
        send_plane(h, 2, 0, 0, 64, 0, -1, 17)
    wait_line(xblk(2), 0, 64, 2)
    wait_line(xblk(2), 64, 64, 3)
    send_line(2, 0, 128, sibling, 7)
    for i, dx in enumerate((0, -1, 1, 2)):
        wait_line(lax.rem(x + dx + SIDE, SIDE) * 2 + (1 - core), 0, 128, 4 + i)
    own_c.wait()
    own_r.wait()

    score_scale = LOG2E / math.sqrt(WIDTH)

    def score_tile(dy, other):
        half = z // 2
        n = lax.rem(y + dy + SIDE, SIDE) * 2 + (1 - half if other else half)
        right = ec[pl.ds(2 * n, 2)].reshape(2 * BLOCK, WIDTH)
        cols = pl.ds(pl.multiple_of(n * 256, 256), 256)

        def part(m, carry):
            left = er[pl.ds(SCORE_M * m, SCORE_M)].reshape(SCORE_M * BLOCK, WIDTH)
            out = lax.dot_general(left, right, (((1,), (1,)), ((), ())), preferred_element_type=F32)
            s[pl.ds(pl.multiple_of(m * (SCORE_M * BLOCK), SCORE_M * BLOCK), SCORE_M * BLOCK), cols] = out * score_scale
            return carry

        lax.fori_loop(0, LINE // SCORE_M, part, 0)

    def wait_forwarded(h, oi):
        wait_plane(h, OFFS[oi], 2, 0, 32, 6 + 4 * oi)
        wait_plane(h, OFFS[oi], 2, 32, 32, 7 + 4 * oi)

    def second_stage(oi):
        o = OFFS[oi]
        for h in (0, 1):
            wait_plane(h, o, -1, 0, 64, 4 + 4 * oi)
            send_plane(h, o, -1, 0, 32, 0, 1, 6 + 4 * oi)
            wait_plane(h, o, 1, 0, 64, 5 + 4 * oi)
            send_plane(h, o, 1, 32, 32, 0, -1, 7 + 4 * oi)

    score_tile(0, False)
    second_stage(1)
    wait_forwarded(1, 0)
    score_tile(0, True)
    second_stage(2)
    score_tile(-1, False)
    score_tile(1, False)
    second_stage(3)
    wait_forwarded(1, 1)
    wait_forwarded(1, 2)
    score_tile(-1, True)
    score_tile(1, True)
    wait_forwarded(0, 0)
    wait_forwarded(0, 1)
    wait_forwarded(0, 2)
    score_tile(2, False)
    wait_forwarded(0, 3)
    wait_forwarded(1, 3)
    score_tile(2, True)
    eye = lax.broadcasted_iota(jnp.int32, (BLOCK, BLOCK), 0) == lax.broadcasted_iota(jnp.int32, (BLOCK, BLOCK), 1)
    dr = pl.ds(pl.multiple_of(b * BLOCK, BLOCK), BLOCK)
    dc = pl.ds(pl.multiple_of(a * BLOCK, BLOCK), BLOCK)
    s[dr, dc] = jnp.where(eye, -30000.0 * LOG2E, s[dr, dc])

    def rows_at(i):
        return pl.ds(pl.multiple_of(i * CH, CH), CH)

    def lanes(k):
        return slice(k * BLOCK, (k + 1) * BLOCK)

    def to_rows(v, ref):
        for g in range(LINE):
            ref[pl.ds(g * BLOCK, BLOCK), :] = jnp.broadcast_to(v[g : g + 1], (BLOCK, BLOCK)).T

    def from_rows(ref):
        out = []
        for g in range(LINE):
            v = jnp.where(eye, ref[pl.ds(g * BLOCK, BLOCK), :], 0.0)
            out.append(jnp.sum(v, axis=0, keepdims=True))
        return jnp.concatenate(out, axis=0)

    def send_cols(e):
        def to_plane(k, carry):
            pltpu.make_async_remote_copy(
                src_ref=cmsg.at[e], dst_ref=crx.at[e, a], send_sem=csend.at[e], recv_sem=crecv.at[e],
                device_id=(in_plane(k),), device_id_type=MESH,
            ).start()
            return carry

        lax.fori_loop(1, PLANE, to_plane, 0)
        crx[e, a] = cmsg[e]

    def send_rows(e):
        def to_line(k, carry):
            pltpu.make_async_remote_copy(
                src_ref=rmsg.at[e], dst_ref=rrx.at[e, b], send_sem=rsend.at[e], recv_sem=rrecv.at[e],
                device_id=(in_line(k),), device_id_type=MESH,
            ).start()
            return carry

        lax.fori_loop(1, LINE, to_line, 0)
        rrx[e, b] = rmsg[e]

    def wait_cols(e):
        every = crx.at[e, pl.ds(0, PLANE - 1)]
        pltpu.make_async_copy(every, every, crecv.at[e]).wait()

    def wait_rows(e):
        every = rrx.at[e, pl.ds(0, LINE - 1)]
        pltpu.make_async_copy(every, every, rrecv.at[e]).wait()

    def merge(v):
        top = jnp.max(v, axis=0)
        return top + log2(jnp.sum(jnp.exp2(v - top[None]), axis=0))

    low = jnp.full((8, BLOCK), -jnp.inf, F32)
    zero = jnp.zeros((8, BLOCK), F32)
    steps = RROWS // CH

    def row_lse(t):
        pot_c = cvec.at[t - 2]

        def step(i, carry):
            rows = rows_at(i)

            def value(k):
                v = s[rows, lanes(k)]
                return v + pot_c[k : k + 1, :] if t > 1 else v

            best = value(0)
            for k in range(1, PLANE):
                best = jnp.maximum(best, value(k))
            m = jnp.broadcast_to(jnp.max(best, axis=1, keepdims=True), (CH, BLOCK))
            acc = jnp.exp2(value(0) - m)
            for k in range(1, PLANE):
                acc = acc + jnp.exp2(value(k) - m)
            total = jnp.broadcast_to(jnp.sum(acc, axis=1, keepdims=True), (CH, BLOCK))
            accr[rows, :] = m + log2(total)
            return carry

        lax.fori_loop(0, steps, step, 0)
        rmsg[t - 1, 0:LINE, :] = from_rows(accr)
        if t == 1:
            rmsg[0, LINE : LINE + 8, :] = jnp.broadcast_to(pos[...].astype(F32), (8, BLOCK))
        send_rows(t - 1)

    def col_lse(t):
        pot_r = rvec.at[t - 2]

        def value(rows, k, pr):
            v = s[rows, lanes(k)]
            return v + pr if t > 1 else v

        def top_step(i, tops):
            rows = rows_at(i)
            pr = pot_r[rows, :] if t > 1 else None
            return tuple(jnp.maximum(tops[k], fold(value(rows, k, pr), jnp.maximum)) for k in range(PLANE))

        tops = lax.fori_loop(0, steps, top_step, (low,) * PLANE)
        ctop = jnp.concatenate([jnp.max(v, axis=0, keepdims=True) for v in tops], axis=0)
        cvec[7] = ctop

        def sum_step(i, sums):
            rows = rows_at(i)
            pr = pot_r[rows, :] if t > 1 else None
            return tuple(
                sums[k] + fold(jnp.exp2(value(rows, k, pr) - cvec[7, k : k + 1, :]), jnp.add) for k in range(PLANE)
            )

        sums = lax.fori_loop(0, steps, sum_step, (zero,) * PLANE)
        csum = jnp.concatenate([jnp.sum(v, axis=0, keepdims=True) for v in sums], axis=0)
        cmsg[t - 1, 0:PLANE, :] = ctop + log2(csum)
        send_cols(t - 1)

    cmsg[...] = jnp.zeros_like(cmsg)
    rmsg[...] = jnp.zeros_like(rmsg)
    row_lse(1)
    col_lse(1)
    wait_rows(0)
    to_rows(jnp.concatenate([rrx[0, g, LINE : LINE + 1, :] for g in range(LINE)], axis=0), pr_ref)
    pot_r = jnp.zeros((LINE, BLOCK), F32)
    pot_c = jnp.zeros((PLANE, BLOCK), F32)
    for t in (1, 2):
        if t > 1:
            wait_rows(t - 1)
        lse_r = merge(rrx[t - 1, :, 0:LINE, :])
        pot_r = (pot_r - lse_r) * 0.5
        to_rows(lse_r, rvec.at[t + 1])
        to_rows(pot_r, rvec.at[t - 1])
        col_lse(t + 1)
        wait_cols(t - 1)
        lse_c = merge(crx[t - 1, :, 0:PLANE, :])
        pot_c = (pot_c - lse_c) * 0.5
        cvec[t + 1] = lse_c
        cvec[t - 1] = pot_c
        row_lse(t + 1)

    first_col = (lax.broadcasted_iota(jnp.int32, (8, BLOCK), 1) + b * BLOCK).astype(F32)
    first_col = jnp.broadcast_to(first_col[0:1], (CH, BLOCK))

    def add_term(t):
        pot_cc, lse_rr, pull_rr = cvec.at[t - 2], rvec.at[t + 1], rvec.at[7 - t]

        def step(i, carry):
            sums, picked = carry
            rows = rows_at(i)
            lr = lse_rr[rows, :]
            if t < 3:
                qr = pull_rr[rows, :]
            else:
                partner = pr_ref[rows, :] - first_col
            out = []
            for k in range(PLANE):
                v = s[rows, lanes(k)]
                u = v + pot_cc[k : k + 1, :] if t > 1 else v
                term = jnp.exp2(u - lr)
                if t < 3:
                    term = term * qr
                    w[rows, lanes(k)] = w[rows, lanes(k)] + term
                else:
                    hit = partner == float(k * RROWS)
                    picked = picked + fold(jnp.where(hit, v, 0.0), jnp.add)
                    w[rows, lanes(k)] = jnp.where(hit, term - 2.0, term)
                if t > 1:
                    out.append(sums[k] + fold(term, jnp.add))
            return tuple(out), picked

        return lax.fori_loop(0, steps, step, ((zero,) * (PLANE if t > 1 else 0), zero))

    def add_mirror(t, start=0, count=steps):
        pot_rr, lse_cc, pull_cc = rvec.at[t - 2], cvec.at[t + 1], cvec.at[7 - t]

        def step(i, carry):
            rows = rows_at(start + i)
            if t > 1:
                pr = pot_rr[rows, :]
            acc = None
            for k in range(PLANE):
                v = s[rows, lanes(k)]
                q = v + pr if t > 1 else v
                mirror = jnp.exp2(q - lse_cc[k : k + 1, :])
                if t < 3:
                    mirror = mirror * pull_cc[k : k + 1, :]
                total = w[rows, lanes(k)] + mirror
                if t > 1:
                    w[rows, lanes(k)] = total
                    acc = mirror if acc is None else acc + mirror
                else:
                    wb[rows, lanes(k)] = total.astype(BF16)
            if t > 1:
                accr[rows, :] = jnp.broadcast_to(jnp.sum(acc, axis=1, keepdims=True), (CH, BLOCK))
            return carry

        lax.fori_loop(0, count, step, 0)

    def col_sums(e, sums):
        cmsg[e, 0:PLANE, :] = jnp.concatenate([jnp.sum(v, axis=0, keepdims=True) for v in sums], axis=0)
        send_cols(e)

    wait_rows(2)
    lse_r = merge(rrx[2, :, 0:LINE, :])
    to_rows(lse_r, rvec.at[4])
    sums, picked = add_term(3)
    cmsg[3, PLANE : PLANE + 8, :] = picked
    col_sums(3, sums)
    wait_cols(2)
    lse_c = merge(crx[2, :, 0:PLANE, :])
    cvec[4] = lse_c
    pot_c = (pot_c - lse_c) * 0.5
    add_mirror(3)
    rmsg[3, 0:LINE, :] = from_rows(accr)
    send_rows(3)
    wait_rows(3)
    cot_r = -1.0 + jnp.sum(rrx[3, :, 0:LINE, :], axis=0)
    to_rows(-0.5 * cot_r, rvec.at[5])
    sums, _ = add_term(2)
    col_sums(4, sums)
    wait_cols(3)
    cot_c = -1.0 + jnp.sum(crx[3, :, 0:PLANE, :], axis=0)
    cvec[5] = -0.5 * cot_c
    picked = jnp.sum(crx[3, :, PLANE : PLANE + 8, :], axis=0)
    rmsg[4, LINE : LINE + 8, :] = picked + 2.0 * (pot_c[0:8] + pot_c[8:16])
    add_mirror(2)
    rmsg[4, 0:LINE, :] = from_rows(accr)
    send_rows(4)
    wait_rows(4)
    cot_r = 0.5 * cot_r + jnp.sum(rrx[4, :, 0:LINE, :], axis=0)
    whole = jnp.sum(rrx[4, :, LINE : LINE + 8, :], axis=0)
    loss[0, 0] = jnp.sum(whole) * (-LN2 / TOTAL)
    to_rows(-0.5 * cot_r, rvec.at[6])
    add_term(1)
    wait_cols(4)
    cot_c = 0.5 * cot_c + jnp.sum(crx[4, :, 0:PLANE, :], axis=0)
    cvec[6] = -0.5 * cot_c

    grad_scale = 1.0 / math.sqrt(WIDTH)

    def partial(d):
        xx = lax.rem(x + d, SIDE)
        rows = pl.ds(pl.multiple_of(xx * 256, 256), 256)
        add_mirror(1, xx * (256 // CH), 256 // CH)

        def tile(n, carry):
            cols = pl.ds(pl.multiple_of(n * 256, 256), 256)
            right = ec[:, :, cols].reshape(CCOLS, 256)
            out = jnp.dot(wb[rows, :], right, preferred_element_type=F32) * grad_scale
            gp[d, :, :, cols] = out.reshape(2, BLOCK, 256)
            return carry

        lax.fori_loop(0, WIDTH // 256, tile, 0)
        pltpu.make_async_remote_copy(
            src_ref=gp.at[d, 1 - core], dst_ref=rb.at[d], send_sem=gsend.at[d], recv_sem=grecv.at[d],
            device_id=(sibling,), device_id_type=MESH,
        ).start()

    def chip_sum(d):
        pltpu.make_async_copy(rb.at[d], rb.at[d], grecv.at[d]).wait()
        return gp[d, core] + rb[d]

    def ring(src, dst, i, device):
        return pltpu.make_async_remote_copy(
            src_ref=src, dst_ref=dst, send_sem=hsend.at[i], recv_sem=hrecv.at[i],
            device_id=(device,), device_id_type=MESH,
        )

    half = WIDTH // 2
    far = [ring(xs2.at[i], xr2.at[i], i, xdev(dx)) for i, dx in ((0, 1), (1, -1))]
    near = [ring(xs1.at[i], xr1.at[i], 2 + i, xdev(dx)) for i, dx in ((0, 1), (1, -1))]
    partial(2)
    partial(1)
    v = chip_sum(2).astype(BF16)
    xs2[0] = v[:, :half]
    xs2[1] = v[:, half:]
    far[0].start()
    far[1].start()
    partial(3)
    v = chip_sum(1)
    far[0].wait_recv()
    xs1[0, :, :half] = (v[:, :half] + xr2[0].astype(F32)).astype(BF16)
    xs1[0, :, half:] = v[:, half:].astype(BF16)
    near[0].start()
    partial(0)
    v = chip_sum(3)
    far[1].wait_recv()
    xs1[1, :, :half] = v[:, :half].astype(BF16)
    xs1[1, :, half:] = (v[:, half:] + xr2[1].astype(F32)).astype(BF16)
    near[1].start()
    v = chip_sum(0)
    near[0].wait_recv()
    v = v + xr1[0].astype(F32)
    near[1].wait_recv()
    grad[...] = v + xr1[1].astype(F32)

    sent = ec.at[pl.ds(0, PLANE - 1)]
    pltpu.make_async_copy(sent, sent, psend).wait()
    sent = er.at[pl.ds(0, LINE - 1)]
    pltpu.make_async_copy(sent, sent, xsend).wait()
    for e in range(5):
        every = rrx.at[e, pl.ds(0, LINE - 1)]
        pltpu.make_async_copy(every, every, rsend.at[e]).wait()
        every = crx.at[e, pl.ds(0, PLANE - 1)]
        pltpu.make_async_copy(every, every, csend.at[e]).wait()
    for d in range(SIDE):
        pltpu.make_async_copy(rb.at[d], rb.at[d], gsend.at[d]).wait()
    for c in far + near:
        c.wait_send()


def shards(embeddings, positives):
    vec = pltpu.VMEM
    dma = pltpu.SemaphoreType.DMA
    grad, loss = pl.pallas_call(
        kernel,
        out_shape=(
            jax.ShapeDtypeStruct((BLOCK, WIDTH), F32),
            jax.ShapeDtypeStruct((1, 1), F32),
        ),
        in_specs=[pl.BlockSpec(memory_space=pl.ANY), pl.BlockSpec(memory_space=pltpu.VMEM)],
        out_specs=(pl.BlockSpec(memory_space=pltpu.VMEM), pl.BlockSpec(memory_space=pltpu.SMEM)),
        scratch_shapes=[
            vec((PLANE, BLOCK, WIDTH), BF16),
            vec((LINE, BLOCK, WIDTH), BF16),
            vec((RROWS, CCOLS), F32),
            vec((RROWS, CCOLS), F32),
            vec((RROWS, CCOLS), BF16),
            vec((7, RROWS, BLOCK), F32),
            vec((8, PLANE, BLOCK), F32),
            vec((RROWS, BLOCK), F32),
            vec((RROWS, BLOCK), F32),
            vec((RROWS, BLOCK), F32),
            vec((5, PLANE + 8, BLOCK), F32),
            vec((5, PLANE, PLANE + 8, BLOCK), F32),
            vec((5, LINE + 8, BLOCK), F32),
            vec((5, LINE, LINE + 8, BLOCK), F32),
            vec((SIDE, 2, BLOCK, WIDTH), F32),
            vec((SIDE, BLOCK, WIDTH), F32),
            vec((2, BLOCK, WIDTH // 2), BF16),
            vec((2, BLOCK, WIDTH // 2), BF16),
            vec((2, BLOCK, WIDTH), BF16),
            vec((2, BLOCK, WIDTH), BF16),
            dma((2,)),
            dma,
            dma((2, 20)),
            dma,
            dma((8,)),
            dma((5,)),
            dma((5,)),
            dma((5,)),
            dma((5,)),
            dma((SIDE,)),
            dma((SIDE,)),
            dma((4,)),
            dma((4,)),
        ],
        compiler_params=pltpu.CompilerParams(
            collective_id=0, has_side_effects=True, vmem_limit_bytes=56 * 1024 * 1024
        ),
    )(embeddings, positives.reshape(1, BLOCK))
    return loss.reshape(()), grad


def solution(mesh):
    placed = (P("dp", None), P("dp"))
    return jax.shard_map(
        shards, mesh=mesh, in_specs=placed, out_specs=(P(), P("dp", None)), check_vma=False
    )
```

```python
import functools
import math

import jax
import jax.numpy as jnp
from jax import lax
from jax.experimental import pallas as pl
from jax.experimental.pallas import tpu as pltpu
from jax.sharding import PartitionSpec as P

SIDE = 4
PLANE = SIDE * SIDE
LINE = SIDE * 2
BLOCK = 128
WIDTH = 1024
RROWS = LINE * BLOCK
CCOLS = PLANE * BLOCK
TOTAL = PLANE * RROWS
LOG2E = math.log2(math.e)
LN2 = math.log(2.0)
MESH = pl.DeviceIdType.MESH
F32 = jnp.float32
BF16 = jnp.bfloat16
TILE = 256
SCORE_M = 4
CH = 32
OFFS = (0, -1, 1, 2)
FAR_FIRST = sorted(
    ((dy, dz) for dy in OFFS for dz in OFFS if (dy, dz) != (0, 0)), key=lambda d: -abs(d[0]) - abs(d[1])
)


def fold(v, op):
    out = v[0:8]
    for r in range(8, v.shape[0], 8):
        out = op(out, v[r : r + 8])
    return out


def tree(v, op):
    while len(v) > 1:
        v = [op(*v[i : i + 2]) if i + 1 < len(v) else v[i] for i in range(0, len(v), 2)]
    return v[0]


def log2(v):
    return jnp.log(v) * LOG2E


def kernel(
    emb, pos, grad, loss,
    ec, er, s, w, wb, rvec, cvec, pr_ref, mr, accr, cmsg, crx, rmsg, rrx,
    gp, rb, xs2, xr2, xs1, xr1,
    lsem, psend, prsem, xsend, xrsem, csend, crecv, rsend, rrecv, gsend, grecv, hsend, hrecv,
):
    me = lax.axis_index("dp")
    a = me // LINE
    b = me % LINE
    y, z = a // SIDE, a % SIDE
    x, core = b // 2, b % 2

    def dev_of(dy, dz, dx, c):
        yy, zz, xx = (lax.rem(v + d + SIDE, SIDE) for v, d in ((y, dy), (z, dz), (x, dx)))
        return ((yy * SIDE + zz) * SIDE + xx) * 2 + c

    barrier = pltpu.get_barrier_semaphore()

    near_by = (
        [dev_of(dy, dz, dx, core) for dy, dz, dx in ((1, 0, 0), (-1, 0, 0), (0, 1, 0), (0, -1, 0), (0, 0, 1), (0, 0, -1))]
        + [dev_of(0, 0, 0, 1 - core)]
    )
    for device in near_by:
        pl.semaphore_signal(barrier, inc=1, device_id=(device,), device_id_type=MESH)
    own_c = pltpu.make_async_copy(emb, ec.at[a], lsem.at[0])
    own_r = pltpu.make_async_copy(emb, er.at[b], lsem.at[1])
    own_c.start()
    own_r.start()
    pl.semaphore_wait(barrier, len(near_by))

    def blk(h, op, oq):
        dy, dz = (oq, op) if h == 0 else (op, oq)
        return lax.rem(y + dy + SIDE, SIDE) * SIDE + lax.rem(z + dz + SIDE, SIDE)

    def send_plane(h, op, oq, lo, n, tp, tq, idx):
        k = blk(h, op, oq)
        rows = pl.ds(64 * h + lo, n)
        src = emb.at[rows] if (op, oq) == (0, 0) else ec.at[k, rows]
        pltpu.make_async_remote_copy(
            src_ref=src, dst_ref=ec.at[k, rows], send_sem=psend, recv_sem=prsem.at[h, idx],
            device_id=(blk(h, tp, tq) * LINE + b,), device_id_type=MESH,
        ).start()

    def wait_plane(h, op, oq, lo, n, idx):
        ref = ec.at[blk(h, op, oq), pl.ds(64 * h + lo, n)]
        pltpu.make_async_copy(ref, ref, prsem.at[h, idx]).wait()

    def xdev(dx):
        return a * LINE + lax.rem(x + dx + SIDE, SIDE) * 2 + core

    sibling = a * LINE + x * 2 + (1 - core)

    def xblk(dx):
        return lax.rem(x + dx + SIDE, SIDE) * 2 + core

    def send_line(dx, lo, n, device, idx):
        k = xblk(dx)
        rows = pl.ds(lo, n)
        src = emb.at[rows] if dx == 0 else er.at[k, rows]
        pltpu.make_async_remote_copy(
            src_ref=src, dst_ref=er.at[k, rows], send_sem=xsend, recv_sem=xrsem.at[idx],
            device_id=(device,), device_id_type=MESH,
        ).start()

    def wait_line(k, lo, n, idx):
        ref = er.at[k, pl.ds(lo, n)]
        pltpu.make_async_copy(ref, ref, xrsem.at[idx]).wait()

    for h in (0, 1):
        send_plane(h, 0, 0, 0, 64, 1, 0, 0)
        send_plane(h, 0, 0, 0, 64, -1, 0, 1)
    send_line(0, 0, 128, xdev(1), 0)
    send_line(0, 0, 128, xdev(-1), 1)
    send_line(0, 0, 128, sibling, 4)
    for h in (0, 1):
        send_plane(h, 0, 0, 0, 64, 0, 1, 4)
        send_plane(h, 0, 0, 0, 64, 0, -1, 5)
    for h in (0, 1):
        wait_plane(h, -1, 0, 0, 64, 0)
        send_plane(h, -1, 0, 0, 32, 1, 0, 2)
        wait_plane(h, 1, 0, 0, 64, 1)
        send_plane(h, 1, 0, 32, 32, -1, 0, 3)
    wait_line(xblk(-1), 0, 128, 0)
    send_line(-1, 0, 64, xdev(1), 2)
    send_line(-1, 0, 128, sibling, 5)
    wait_line(xblk(1), 0, 128, 1)
    send_line(1, 64, 64, xdev(-1), 3)
    send_line(1, 0, 128, sibling, 6)
    for h in (0, 1):
        for oi in (1, 2):
            send_plane(h, OFFS[oi], 0, 0, 64, 0, 1, 4 + 4 * oi)
            send_plane(h, OFFS[oi], 0, 0, 64, 0, -1, 5 + 4 * oi)
    for h in (0, 1):
        wait_plane(h, 0, -1, 0, 64, 4)
        send_plane(h, 0, -1, 0, 32, 0, 1, 6)
        wait_plane(h, 0, 1, 0, 64, 5)
        send_plane(h, 0, 1, 32, 32, 0, -1, 7)
    for h in (0, 1):
        wait_plane(h, 2, 0, 0, 32, 2)
        wait_plane(h, 2, 0, 32, 32, 3)
        send_plane(h, 2, 0, 0, 64, 0, 1, 16)
        send_plane(h, 2, 0, 0, 64, 0, -1, 17)
    wait_line(xblk(2), 0, 64, 2)
    wait_line(xblk(2), 64, 64, 3)
    send_line(2, 0, 128, sibling, 7)
    for i, dx in enumerate((0, -1, 1, 2)):
        wait_line(lax.rem(x + dx + SIDE, SIDE) * 2 + (1 - core), 0, 128, 4 + i)
    own_c.wait()
    own_r.wait()

    score_scale = LOG2E / math.sqrt(WIDTH)

    def score_tile(dy, other):
        half = z // 2
        n = lax.rem(y + dy + SIDE, SIDE) * 2 + (1 - half if other else half)
        right = ec[pl.ds(2 * n, 2)].reshape(2 * BLOCK, WIDTH)
        cols = pl.ds(pl.multiple_of(n * 256, 256), 256)

        def part(m, carry):
            left = er[pl.ds(SCORE_M * m, SCORE_M)].reshape(SCORE_M * BLOCK, WIDTH)
            out = lax.dot_general(left, right, (((1,), (1,)), ((), ())), preferred_element_type=F32)
            s[pl.ds(pl.multiple_of(m * (SCORE_M * BLOCK), SCORE_M * BLOCK), SCORE_M * BLOCK), cols] = out * score_scale
            return carry

        lax.fori_loop(0, LINE // SCORE_M, part, 0)

    def wait_forwarded(h, oi):
        wait_plane(h, OFFS[oi], 2, 0, 32, 6 + 4 * oi)
        wait_plane(h, OFFS[oi], 2, 32, 32, 7 + 4 * oi)

    def second_stage(oi):
        o = OFFS[oi]
        for h in (0, 1):
            wait_plane(h, o, -1, 0, 64, 4 + 4 * oi)
            send_plane(h, o, -1, 0, 32, 0, 1, 6 + 4 * oi)
            wait_plane(h, o, 1, 0, 64, 5 + 4 * oi)
            send_plane(h, o, 1, 32, 32, 0, -1, 7 + 4 * oi)

    score_tile(0, False)
    second_stage(1)
    wait_forwarded(1, 0)
    score_tile(0, True)
    second_stage(2)
    score_tile(-1, False)
    score_tile(1, False)
    second_stage(3)
    wait_forwarded(1, 1)
    wait_forwarded(1, 2)
    score_tile(-1, True)
    score_tile(1, True)
    wait_forwarded(0, 0)
    wait_forwarded(0, 1)
    wait_forwarded(0, 2)
    score_tile(2, False)
    wait_forwarded(0, 3)
    wait_forwarded(1, 3)
    score_tile(2, True)
    eye = lax.broadcasted_iota(jnp.int32, (BLOCK, BLOCK), 0) == lax.broadcasted_iota(jnp.int32, (BLOCK, BLOCK), 1)
    dr = pl.ds(pl.multiple_of(b * BLOCK, BLOCK), BLOCK)
    dc = pl.ds(pl.multiple_of(a * BLOCK, BLOCK), BLOCK)
    s[dr, dc] = jnp.where(eye, -30000.0 * LOG2E, s[dr, dc])

    def rows_at(i):
        return pl.ds(pl.multiple_of(i * CH, CH), CH)

    def lanes(k):
        return slice(k * BLOCK, (k + 1) * BLOCK)

    def to_rows(v, ref):
        for g in range(LINE):
            ref[pl.ds(g * BLOCK, BLOCK), :] = jnp.broadcast_to(v[g : g + 1], (BLOCK, BLOCK)).T

    def row_sums(ref):
        out = [jnp.sum(ref[pl.ds(g * BLOCK, BLOCK), :].T, axis=0, keepdims=True) for g in range(LINE)]
        return jnp.concatenate(out, axis=0)

    def send_cols(e):
        for dy, dz in FAR_FIRST:
            pltpu.make_async_remote_copy(
                src_ref=cmsg.at[e], dst_ref=crx.at[e, a], send_sem=csend.at[e], recv_sem=crecv.at[e],
                device_id=(dev_of(dy, dz, 0, core),), device_id_type=MESH,
            ).start()
        crx[e, a] = cmsg[e]

    def send_rows(e):
        for dx, other in ((2, 1), (2, 0), (1, 1), (-1, 1), (1, 0), (-1, 0), (0, 1)):
            pltpu.make_async_remote_copy(
                src_ref=rmsg.at[e], dst_ref=rrx.at[e, b], send_sem=rsend.at[e], recv_sem=rrecv.at[e],
                device_id=(dev_of(0, 0, dx, 1 - core if other else core),), device_id_type=MESH,
            ).start()
        rrx[e, b] = rmsg[e]

    def wait_cols(e):
        every = crx.at[e, pl.ds(0, PLANE - 1)]
        pltpu.make_async_copy(every, every, crecv.at[e]).wait()

    def wait_rows(e):
        every = rrx.at[e, pl.ds(0, LINE - 1)]
        pltpu.make_async_copy(every, every, rrecv.at[e]).wait()

    def merge(v):
        top = jnp.max(v, axis=0)
        return top + log2(jnp.sum(jnp.exp2(v - top[None]), axis=0))

    low = jnp.full((8, BLOCK), -jnp.inf, F32)
    zero = jnp.zeros((8, BLOCK), F32)
    steps = RROWS // CH

    def row_lse(t):
        pot_c = cvec.at[t - 2]

        def step(i, carry):
            rows = rows_at(i)
            v = [s[rows, lanes(k)] for k in range(PLANE)]
            if t > 1:
                v = [v[k] + pot_c[k : k + 1, :] for k in range(PLANE)]
            best = tree(v, jnp.maximum)
            mr[rows, :] = best
            accr[rows, :] = tree([jnp.exp2(u - best) for u in v], jnp.add)
            return carry

        lax.fori_loop(0, steps, step, 0)
        out = []
        for g in range(LINE):
            best = mr[pl.ds(g * BLOCK, BLOCK), :].T
            acc = accr[pl.ds(g * BLOCK, BLOCK), :].T
            top = jnp.max(best, axis=0, keepdims=True)
            out.append(top + log2(jnp.sum(acc * jnp.exp2(best - top), axis=0, keepdims=True)))
        rmsg[t - 1, 0:LINE, :] = jnp.concatenate(out, axis=0)
        if t == 1:
            rmsg[0, LINE : LINE + 8, :] = jnp.broadcast_to(pos[...].astype(F32), (8, BLOCK))
        send_rows(t - 1)

    def col_lse(t):
        pot_r = rvec.at[t - 2]

        def value(rows, k, pr):
            v = s[rows, lanes(k)]
            return v + pr if t > 1 else v

        def top_step(i, tops):
            rows = rows_at(i)
            pr = pot_r[rows, :] if t > 1 else None
            return tuple(jnp.maximum(tops[k], fold(value(rows, k, pr), jnp.maximum)) for k in range(PLANE))

        tops = lax.fori_loop(0, steps, top_step, (low,) * PLANE)
        ctop = jnp.concatenate([jnp.max(v, axis=0, keepdims=True) for v in tops], axis=0)
        cvec[7] = ctop

        def sum_step(i, sums):
            rows = rows_at(i)
            pr = pot_r[rows, :] if t > 1 else None
            return tuple(
                sums[k] + fold(jnp.exp2(value(rows, k, pr) - cvec[7, k : k + 1, :]), jnp.add) for k in range(PLANE)
            )

        sums = lax.fori_loop(0, steps, sum_step, (zero,) * PLANE)
        csum = jnp.concatenate([jnp.sum(v, axis=0, keepdims=True) for v in sums], axis=0)
        cmsg[t - 1, 0:PLANE, :] = ctop + log2(csum)
        send_cols(t - 1)

    cmsg[...] = jnp.zeros_like(cmsg)
    rmsg[...] = jnp.zeros_like(rmsg)
    row_lse(1)
    col_lse(1)
    wait_rows(0)
    to_rows(jnp.concatenate([rrx[0, g, LINE : LINE + 1, :] for g in range(LINE)], axis=0), pr_ref)
    pot_r = jnp.zeros((LINE, BLOCK), F32)
    pot_c = jnp.zeros((PLANE, BLOCK), F32)
    for t in (1, 2):
        if t > 1:
            wait_rows(t - 1)
        lse_r = merge(rrx[t - 1, :, 0:LINE, :])
        pot_r = (pot_r - lse_r) * 0.5
        to_rows(lse_r, rvec.at[t + 1])
        to_rows(pot_r, rvec.at[t - 1])
        col_lse(t + 1)
        wait_cols(t - 1)
        lse_c = merge(crx[t - 1, :, 0:PLANE, :])
        pot_c = (pot_c - lse_c) * 0.5
        cvec[t + 1] = lse_c
        cvec[t - 1] = pot_c
        row_lse(t + 1)

    first_col = (lax.broadcasted_iota(jnp.int32, (8, BLOCK), 1) + b * BLOCK).astype(F32)
    first_col = jnp.broadcast_to(first_col[0:1], (CH, BLOCK))

    def add_term(t):
        pot_cc, lse_rr, pull_rr = cvec.at[t - 2], rvec.at[t + 1], rvec.at[7 - t]

        def step(i, carry):
            sums, picked = carry
            rows = rows_at(i)
            lr = lse_rr[rows, :]
            if t < 3:
                qr = pull_rr[rows, :]
            else:
                partner = pr_ref[rows, :] - first_col
            out = []
            for k in range(PLANE):
                v = s[rows, lanes(k)]
                u = v + pot_cc[k : k + 1, :] if t > 1 else v
                term = jnp.exp2(u - lr)
                if t < 3:
                    term = term * qr
                    w[rows, lanes(k)] = w[rows, lanes(k)] + term
                else:
                    hit = partner == float(k * RROWS)
                    picked = picked + fold(jnp.where(hit, v, 0.0), jnp.add)
                    w[rows, lanes(k)] = jnp.where(hit, term - 2.0, term)
                if t > 1:
                    out.append(sums[k] + fold(term, jnp.add))
            return tuple(out), picked

        return lax.fori_loop(0, steps, step, ((zero,) * (PLANE if t > 1 else 0), zero))

    def add_mirror(t, start=0, count=steps):
        pot_rr, lse_cc, pull_cc = rvec.at[t - 2], cvec.at[t + 1], cvec.at[7 - t]

        def step(i, carry):
            rows = rows_at(start + i)
            if t > 1:
                pr = pot_rr[rows, :]
            acc = None
            for k in range(PLANE):
                v = s[rows, lanes(k)]
                q = v + pr if t > 1 else v
                mirror = jnp.exp2(q - lse_cc[k : k + 1, :])
                if t < 3:
                    mirror = mirror * pull_cc[k : k + 1, :]
                total = w[rows, lanes(k)] + mirror
                if t > 1:
                    w[rows, lanes(k)] = total
                    acc = mirror if acc is None else acc + mirror
                else:
                    wb[rows, lanes(k)] = total.astype(BF16)
            if t > 1:
                accr[rows, :] = acc
            return carry

        lax.fori_loop(0, count, step, 0)

    def col_sums(e, sums):
        cmsg[e, 0:PLANE, :] = jnp.concatenate([jnp.sum(v, axis=0, keepdims=True) for v in sums], axis=0)
        send_cols(e)

    wait_rows(2)
    lse_r = merge(rrx[2, :, 0:LINE, :])
    to_rows(lse_r, rvec.at[4])
    sums, picked = add_term(3)
    cmsg[3, PLANE : PLANE + 8, :] = picked
    col_sums(3, sums)
    wait_cols(2)
    lse_c = merge(crx[2, :, 0:PLANE, :])
    cvec[4] = lse_c
    pot_c = (pot_c - lse_c) * 0.5
    add_mirror(3)
    rmsg[3, 0:LINE, :] = row_sums(accr)
    send_rows(3)
    wait_rows(3)
    cot_r = -1.0 + jnp.sum(rrx[3, :, 0:LINE, :], axis=0)
    to_rows(-0.5 * cot_r, rvec.at[5])
    sums, _ = add_term(2)
    col_sums(4, sums)
    wait_cols(3)
    cot_c = -1.0 + jnp.sum(crx[3, :, 0:PLANE, :], axis=0)
    cvec[5] = -0.5 * cot_c
    picked = jnp.sum(crx[3, :, PLANE : PLANE + 8, :], axis=0)
    rmsg[4, LINE : LINE + 8, :] = picked + 2.0 * (pot_c[0:8] + pot_c[8:16])
    add_mirror(2)
    rmsg[4, 0:LINE, :] = row_sums(accr)
    send_rows(4)
    wait_rows(4)
    cot_r = 0.5 * cot_r + jnp.sum(rrx[4, :, 0:LINE, :], axis=0)
    whole = jnp.sum(rrx[4, :, LINE : LINE + 8, :], axis=0)
    loss[0, 0] = jnp.sum(whole) * (-LN2 / TOTAL)
    to_rows(-0.5 * cot_r, rvec.at[6])
    add_term(1)
    wait_cols(4)
    cot_c = 0.5 * cot_c + jnp.sum(crx[4, :, 0:PLANE, :], axis=0)
    cvec[6] = -0.5 * cot_c

    grad_scale = 1.0 / math.sqrt(WIDTH)

    add_mirror(1)

    def product(n):
        right = ec[:, :, pl.ds(n * TILE, TILE)].reshape(CCOLS, TILE)
        for m in range(2):
            out = jnp.dot(wb[pl.ds(m * 512, 512), :], right, preferred_element_type=F32) * grad_scale
            for g in range(4):
                block = 4 * m + g
                gp[n, block % 2, block // 2] = out[g * BLOCK : (g + 1) * BLOCK]
        pltpu.make_async_remote_copy(
            src_ref=gp.at[n, 1 - core], dst_ref=rb.at[n], send_sem=gsend.at[n], recv_sem=grecv.at[n],
            device_id=(sibling,), device_id_type=MESH,
        ).start()

    def ring(src, dst, i, dx):
        return pltpu.make_async_remote_copy(
            src_ref=src, dst_ref=dst, send_sem=hsend.at[i], recv_sem=hrecv.at[i],
            device_id=(xdev(dx),), device_id_type=MESH,
        )

    half = TILE // 2
    first = [[ring(xs1.at[n, i], xr1.at[n, i], 4 * n + i, dx) for i, dx in ((0, 1), (1, -1))] for n in range(SIDE)]
    second = [[ring(xs2.at[n, i], xr2.at[n, i], 4 * n + 2 + i, dx) for i, dx in ((0, 1), (1, -1))] for n in range(SIDE)]

    def chip_sum(n, d):
        xx = lax.rem(x + d, SIDE)
        return gp[n, core, xx] + rb[n, xx]

    def send_first(n):
        pltpu.make_async_copy(rb.at[n], rb.at[n], grecv.at[n]).wait()
        far = chip_sum(n, 2).astype(BF16)
        xs1[n, 0, :, :half] = far[:, :half]
        xs1[n, 0, :, half:] = chip_sum(n, 1)[:, half:].astype(BF16)
        first[n][0].start()
        xs1[n, 1, :, half:] = far[:, half:]
        xs1[n, 1, :, :half] = chip_sum(n, 3)[:, :half].astype(BF16)
        first[n][1].start()

    def send_second(n):
        first[n][0].wait_recv()
        xs2[n, 0] = (chip_sum(n, 1)[:, :half] + xr1[n, 0, :, :half].astype(F32)).astype(BF16)
        second[n][0].start()
        first[n][1].wait_recv()
        xs2[n, 1] = (chip_sum(n, 3)[:, half:] + xr1[n, 1, :, half:].astype(F32)).astype(BF16)
        second[n][1].start()

    def finish(n):
        own = chip_sum(n, 0)
        second[n][0].wait_recv()
        second[n][1].wait_recv()
        lo, mid = n * TILE, n * TILE + half
        grad[:, lo:mid] = own[:, :half] + xr2[n, 0].astype(F32) + xr1[n, 1, :, :half].astype(F32)
        grad[:, mid : mid + half] = own[:, half:] + xr2[n, 1].astype(F32) + xr1[n, 0, :, half:].astype(F32)

    for n in range(SIDE):
        product(n)
        if n >= 1:
            send_first(n - 1)
        if n >= 2:
            send_second(n - 2)
    send_first(3)
    send_second(2)
    finish(0)
    finish(1)
    send_second(3)
    finish(2)
    finish(3)

    sent = ec.at[pl.ds(0, PLANE - 1)]
    pltpu.make_async_copy(sent, sent, psend).wait()
    sent = er.at[pl.ds(0, LINE - 1)]
    pltpu.make_async_copy(sent, sent, xsend).wait()
    for e in range(5):
        every = rrx.at[e, pl.ds(0, LINE - 1)]
        pltpu.make_async_copy(every, every, rsend.at[e]).wait()
        every = crx.at[e, pl.ds(0, PLANE - 1)]
        pltpu.make_async_copy(every, every, csend.at[e]).wait()
    for d in range(SIDE):
        pltpu.make_async_copy(rb.at[d], rb.at[d], gsend.at[d]).wait()
    for c in sum(first + second, []):
        c.wait_send()


def shards(embeddings, positives):
    vec = pltpu.VMEM
    dma = pltpu.SemaphoreType.DMA
    grad, loss = pl.pallas_call(
        kernel,
        out_shape=(
            jax.ShapeDtypeStruct((BLOCK, WIDTH), F32),
            jax.ShapeDtypeStruct((1, 1), F32),
        ),
        in_specs=[pl.BlockSpec(memory_space=pl.ANY), pl.BlockSpec(memory_space=pltpu.VMEM)],
        out_specs=(pl.BlockSpec(memory_space=pltpu.VMEM), pl.BlockSpec(memory_space=pltpu.SMEM)),
        scratch_shapes=[
            vec((PLANE, BLOCK, WIDTH), BF16),
            vec((LINE, BLOCK, WIDTH), BF16),
            vec((RROWS, CCOLS), F32),
            vec((RROWS, CCOLS), F32),
            vec((RROWS, CCOLS), BF16),
            vec((7, RROWS, BLOCK), F32),
            vec((8, PLANE, BLOCK), F32),
            vec((RROWS, BLOCK), F32),
            vec((RROWS, BLOCK), F32),
            vec((RROWS, BLOCK), F32),
            vec((5, PLANE + 8, BLOCK), F32),
            vec((5, PLANE, PLANE + 8, BLOCK), F32),
            vec((5, LINE + 8, BLOCK), F32),
            vec((5, LINE, LINE + 8, BLOCK), F32),
            vec((SIDE, 2, SIDE, BLOCK, TILE), F32),
            vec((SIDE, SIDE, BLOCK, TILE), F32),
            vec((SIDE, 2, BLOCK, TILE // 2), BF16),
            vec((SIDE, 2, BLOCK, TILE // 2), BF16),
            vec((SIDE, 2, BLOCK, TILE), BF16),
            vec((SIDE, 2, BLOCK, TILE), BF16),
            dma((2,)),
            dma,
            dma((2, 20)),
            dma,
            dma((8,)),
            dma((5,)),
            dma((5,)),
            dma((5,)),
            dma((5,)),
            dma((SIDE,)),
            dma((SIDE,)),
            dma((16,)),
            dma((16,)),
        ],
        compiler_params=pltpu.CompilerParams(
            collective_id=0, has_side_effects=True, vmem_limit_bytes=56 * 1024 * 1024
        ),
    )(embeddings, positives.reshape(1, BLOCK))
    return loss.reshape(()), grad


def solution(mesh):
    placed = (P("dp", None), P("dp"))
    return jax.shard_map(
        shards, mesh=mesh, in_specs=placed, out_specs=(P(), P("dp", None)), check_vma=False
    )
```

```python
import functools
import math

import jax
import jax.numpy as jnp
from jax import lax
from jax.experimental import pallas as pl
from jax.experimental.pallas import tpu as pltpu
from jax.sharding import PartitionSpec as P

SIDE = 4
PLANE = SIDE * SIDE
LINE = SIDE * 2
BLOCK = 128
WIDTH = 1024
RROWS = LINE * BLOCK
CCOLS = PLANE * BLOCK
TOTAL = PLANE * RROWS
LOG2E = math.log2(math.e)
LN2 = math.log(2.0)
MESH = pl.DeviceIdType.MESH
F32 = jnp.float32
BF16 = jnp.bfloat16
TILE = 256
SCORE_M = 4
CH = 64
OFFS = (0, -1, 1, 2)
FAR_FIRST = sorted(
    ((dy, dz) for dy in OFFS for dz in OFFS if (dy, dz) != (0, 0)), key=lambda d: -abs(d[0]) - abs(d[1])
)


def fold(v, op):
    return tree([v[r : r + 8] for r in range(0, v.shape[0], 8)], op)


def tree(v, op):
    while len(v) > 1:
        v = [op(*v[i : i + 2]) if i + 1 < len(v) else v[i] for i in range(0, len(v), 2)]
    return v[0]


def log2(v):
    return jnp.log(v) * LOG2E


def kernel(
    emb, pos, grad, loss,
    ec, er, s, w, wb, rvec, cvec, pr_ref, mr, accr, cmsg, crx, rmsg, rrx,
    lmsg, lrx, gp, rb, xs2, xr2, xs1, xr1,
    lsem, psend, prsem, xsend, xrsem, csend, crecv, rsend, rrecv, losem, gsend, grecv, hsend, hrecv,
):
    me = lax.axis_index("dp")
    a = me // LINE
    b = me % LINE
    y, z = a // SIDE, a % SIDE
    x, core = b // 2, b % 2

    def dev_of(dy, dz, dx, c):
        yy, zz, xx = (lax.rem(v + d + SIDE, SIDE) for v, d in ((y, dy), (z, dz), (x, dx)))
        return ((yy * SIDE + zz) * SIDE + xx) * 2 + c

    barrier = pltpu.get_barrier_semaphore()

    near_by = (
        [dev_of(dy, dz, dx, core) for dy, dz, dx in ((1, 0, 0), (-1, 0, 0), (0, 1, 0), (0, -1, 0), (0, 0, 1), (0, 0, -1))]
        + [dev_of(0, 0, 0, 1 - core)]
    )
    for device in near_by:
        pl.semaphore_signal(barrier, inc=1, device_id=(device,), device_id_type=MESH)
    own_c = pltpu.make_async_copy(emb, ec.at[a], lsem.at[0])
    own_r = pltpu.make_async_copy(emb, er.at[b], lsem.at[1])
    own_c.start()
    own_r.start()
    pl.semaphore_wait(barrier, len(near_by))

    def blk(h, op, oq):
        dy, dz = (oq, op) if h == 0 else (op, oq)
        return lax.rem(y + dy + SIDE, SIDE) * SIDE + lax.rem(z + dz + SIDE, SIDE)

    def send_plane(h, op, oq, lo, n, tp, tq, idx):
        k = blk(h, op, oq)
        rows = pl.ds(64 * h + lo, n)
        src = emb.at[rows] if (op, oq) == (0, 0) else ec.at[k, rows]
        pltpu.make_async_remote_copy(
            src_ref=src, dst_ref=ec.at[k, rows], send_sem=psend, recv_sem=prsem.at[h, idx],
            device_id=(blk(h, tp, tq) * LINE + b,), device_id_type=MESH,
        ).start()

    def wait_plane(h, op, oq, lo, n, idx):
        ref = ec.at[blk(h, op, oq), pl.ds(64 * h + lo, n)]
        pltpu.make_async_copy(ref, ref, prsem.at[h, idx]).wait()

    def xdev(dx):
        return a * LINE + lax.rem(x + dx + SIDE, SIDE) * 2 + core

    sibling = a * LINE + x * 2 + (1 - core)

    def xblk(dx):
        return lax.rem(x + dx + SIDE, SIDE) * 2 + core

    def send_line(dx, lo, n, device, idx):
        k = xblk(dx)
        rows = pl.ds(lo, n)
        src = emb.at[rows] if dx == 0 else er.at[k, rows]
        pltpu.make_async_remote_copy(
            src_ref=src, dst_ref=er.at[k, rows], send_sem=xsend, recv_sem=xrsem.at[idx],
            device_id=(device,), device_id_type=MESH,
        ).start()

    def wait_line(k, lo, n, idx):
        ref = er.at[k, pl.ds(lo, n)]
        pltpu.make_async_copy(ref, ref, xrsem.at[idx]).wait()

    for h in (0, 1):
        send_plane(h, 0, 0, 0, 64, 1, 0, 0)
        send_plane(h, 0, 0, 0, 64, -1, 0, 1)
    send_line(0, 0, 128, xdev(1), 0)
    send_line(0, 0, 128, xdev(-1), 1)
    send_line(0, 0, 128, sibling, 4)
    for h in (0, 1):
        send_plane(h, 0, 0, 0, 64, 0, 1, 4)
        send_plane(h, 0, 0, 0, 64, 0, -1, 5)
    for h in (0, 1):
        wait_plane(h, -1, 0, 0, 64, 0)
        send_plane(h, -1, 0, 0, 32, 1, 0, 2)
        wait_plane(h, 1, 0, 0, 64, 1)
        send_plane(h, 1, 0, 32, 32, -1, 0, 3)
    wait_line(xblk(-1), 0, 128, 0)
    send_line(-1, 0, 64, xdev(1), 2)
    send_line(-1, 0, 128, sibling, 5)
    wait_line(xblk(1), 0, 128, 1)
    send_line(1, 64, 64, xdev(-1), 3)
    send_line(1, 0, 128, sibling, 6)
    for h in (0, 1):
        for oi in (1, 2):
            send_plane(h, OFFS[oi], 0, 0, 64, 0, 1, 4 + 4 * oi)
            send_plane(h, OFFS[oi], 0, 0, 64, 0, -1, 5 + 4 * oi)
    for h in (0, 1):
        wait_plane(h, 0, -1, 0, 64, 4)
        send_plane(h, 0, -1, 0, 32, 0, 1, 6)
        wait_plane(h, 0, 1, 0, 64, 5)
        send_plane(h, 0, 1, 32, 32, 0, -1, 7)
    for h in (0, 1):
        wait_plane(h, 2, 0, 0, 32, 2)
        wait_plane(h, 2, 0, 32, 32, 3)
        send_plane(h, 2, 0, 0, 64, 0, 1, 16)
        send_plane(h, 2, 0, 0, 64, 0, -1, 17)
    wait_line(xblk(2), 0, 64, 2)
    wait_line(xblk(2), 64, 64, 3)
    send_line(2, 0, 128, sibling, 7)
    for i, dx in enumerate((0, -1, 1, 2)):
        wait_line(lax.rem(x + dx + SIDE, SIDE) * 2 + (1 - core), 0, 128, 4 + i)
    own_c.wait()
    own_r.wait()

    eye = lax.broadcasted_iota(jnp.int32, (BLOCK, BLOCK), 0) == lax.broadcasted_iota(jnp.int32, (BLOCK, BLOCK), 1)
    low = jnp.full((8, BLOCK), -3e38, F32)
    zero = jnp.zeros((8, BLOCK), F32)
    steps = RROWS // CH

    def rows_at(i):
        return pl.ds(pl.multiple_of(i * CH, CH), CH)

    score_scale = LOG2E / math.sqrt(WIDTH)

    def score_tile(dy, other):
        half = z // 2
        n = lax.rem(y + dy + SIDE, SIDE) * 2 + (1 - half if other else half)
        right = ec[pl.ds(2 * n, 2)].reshape(2 * BLOCK, WIDTH)
        cols = pl.ds(pl.multiple_of(n * 256, 256), 256)

        def part(m, carry):
            left = er[pl.ds(SCORE_M * m, SCORE_M)].reshape(SCORE_M * BLOCK, WIDTH)
            out = lax.dot_general(left, right, (((1,), (1,)), ((), ())), preferred_element_type=F32)
            s[pl.ds(pl.multiple_of(m * (SCORE_M * BLOCK), SCORE_M * BLOCK), SCORE_M * BLOCK), cols] = out * score_scale
            return carry

        lax.fori_loop(0, LINE // SCORE_M, part, 0)
        if dy == 0 and not other:
            dr = pl.ds(pl.multiple_of(b * BLOCK, BLOCK), BLOCK)
            dc = pl.ds(pl.multiple_of(a * BLOCK, BLOCK), BLOCK)
            s[dr, dc] = jnp.where(eye, -30000.0 * LOG2E, s[dr, dc])
        first_sums(n, dy == 0 and not other)

    def first_sums(n, fresh):
        two = [pl.ds(pl.multiple_of(n * 256 + k * BLOCK, BLOCK), BLOCK) for k in range(2)]

        def step(i, carry):
            rows = rows_at(i)
            v = [s[rows, c] for c in two]
            top = jnp.maximum(v[0], v[1])
            if not fresh:
                old = mr[rows, :]
                top = jnp.maximum(top, old)
            acc = jnp.exp2(v[0] - top) + jnp.exp2(v[1] - top)
            if not fresh:
                acc = acc + accr[rows, :] * jnp.exp2(old - top)
            mr[rows, :] = top
            accr[rows, :] = acc
            out = []
            for k in range(2):
                old, acc = carry[k]
                top = jnp.maximum(old, fold(v[k], jnp.maximum))
                p = [jnp.exp2(v[k][r : r + 8] - top) for r in range(0, CH, 8)]
                out.append((top, acc * jnp.exp2(old - top) + tree(p, jnp.add)))
            return tuple(out)

        sums = lax.fori_loop(0, steps, step, ((low, zero),) * 2)
        for k in range(2):
            each, acc = sums[k]
            top = jnp.max(each, axis=0, keepdims=True)
            cmsg[0, pl.ds(2 * n + k, 1), :] = top + log2(jnp.sum(acc * jnp.exp2(each - top), axis=0, keepdims=True))

    def wait_forwarded(h, oi):
        wait_plane(h, OFFS[oi], 2, 0, 32, 6 + 4 * oi)
        wait_plane(h, OFFS[oi], 2, 32, 32, 7 + 4 * oi)

    def second_stage(oi):
        o = OFFS[oi]
        for h in (0, 1):
            wait_plane(h, o, -1, 0, 64, 4 + 4 * oi)
            send_plane(h, o, -1, 0, 32, 0, 1, 6 + 4 * oi)
            wait_plane(h, o, 1, 0, 64, 5 + 4 * oi)
            send_plane(h, o, 1, 32, 32, 0, -1, 7 + 4 * oi)

    score_tile(0, False)
    second_stage(1)
    wait_forwarded(1, 0)
    score_tile(0, True)
    second_stage(2)
    score_tile(-1, False)
    score_tile(1, False)
    second_stage(3)
    wait_forwarded(1, 1)
    wait_forwarded(1, 2)
    score_tile(-1, True)
    score_tile(1, True)
    wait_forwarded(0, 0)
    wait_forwarded(0, 1)
    wait_forwarded(0, 2)
    score_tile(2, False)
    wait_forwarded(0, 3)
    wait_forwarded(1, 3)
    score_tile(2, True)
    def lanes(k):
        return slice(k * BLOCK, (k + 1) * BLOCK)

    def to_rows(v, ref):
        for g in range(LINE):
            ref[pl.ds(g * BLOCK, BLOCK), :] = jnp.broadcast_to(v[g : g + 1], (BLOCK, BLOCK)).T

    def row_sums(ref):
        out = [jnp.sum(ref[pl.ds(g * BLOCK, BLOCK), :].T, axis=0, keepdims=True) for g in range(LINE)]
        return jnp.concatenate(out, axis=0)

    def send_cols(e):
        for dy, dz in FAR_FIRST:
            pltpu.make_async_remote_copy(
                src_ref=cmsg.at[e], dst_ref=crx.at[e, a], send_sem=csend.at[e], recv_sem=crecv.at[e],
                device_id=(dev_of(dy, dz, 0, core),), device_id_type=MESH,
            ).start()
        crx[e, a] = cmsg[e]

    def send_rows(e):
        for dx, other in ((2, 1), (2, 0), (1, 1), (-1, 1), (1, 0), (-1, 0), (0, 1)):
            pltpu.make_async_remote_copy(
                src_ref=rmsg.at[e], dst_ref=rrx.at[e, b], send_sem=rsend.at[e], recv_sem=rrecv.at[e],
                device_id=(dev_of(0, 0, dx, 1 - core if other else core),), device_id_type=MESH,
            ).start()
        rrx[e, b] = rmsg[e]

    def wait_cols(e):
        every = crx.at[e, pl.ds(0, PLANE - 1)]
        pltpu.make_async_copy(every, every, crecv.at[e]).wait()

    def wait_rows(e):
        every = rrx.at[e, pl.ds(0, LINE - 1)]
        pltpu.make_async_copy(every, every, rrecv.at[e]).wait()

    def send_loss():
        for dy, dz in FAR_FIRST:
            pltpu.make_async_remote_copy(
                src_ref=lmsg, dst_ref=lrx.at[a], send_sem=losem.at[0], recv_sem=losem.at[1],
                device_id=(dev_of(dy, dz, 0, core),), device_id_type=MESH,
            ).start()
        lrx[a] = lmsg[...]

    def merge(v):
        top = jnp.max(v, axis=0)
        return top + log2(jnp.sum(jnp.exp2(v - top[None]), axis=0))

    def row_lse(t):
        pot_c = cvec.at[t - 2]

        def step(i, carry):
            rows = rows_at(i)
            best = tree([s[rows, lanes(k)] + pot_c[k : k + 1, :] for k in range(PLANE)], jnp.maximum)
            mr[rows, :] = best
            acc = None
            for k in range(PLANE):
                p = jnp.exp2(s[rows, lanes(k)] + pot_c[k : k + 1, :] - best)
                acc = p if acc is None else acc + p
            accr[rows, :] = acc
            return carry

        lax.fori_loop(0, steps, step, 0)
        send_row_lse(t)

    def send_row_lse(t):
        out = []
        for g in range(LINE):
            best = mr[pl.ds(g * BLOCK, BLOCK), :].T
            acc = accr[pl.ds(g * BLOCK, BLOCK), :].T
            top = jnp.max(best, axis=0, keepdims=True)
            out.append(top + log2(jnp.sum(acc * jnp.exp2(best - top), axis=0, keepdims=True)))
        rmsg[t - 1, 0:LINE, :] = jnp.concatenate(out, axis=0)
        send_rows(t - 1)

    def col_lse(t):
        pot_r = rvec.at[t - 2]

        def value(rows, k, pr):
            return s[rows, lanes(k)] + pr

        def top_step(i, tops):
            rows = rows_at(i)
            pr = pot_r[rows, :]
            return tuple(jnp.maximum(tops[k], fold(value(rows, k, pr), jnp.maximum)) for k in range(PLANE))

        tops = lax.fori_loop(0, steps, top_step, (low,) * PLANE)
        ctop = jnp.concatenate([jnp.max(v, axis=0, keepdims=True) for v in tops], axis=0)
        cvec[7] = ctop

        def sum_step(i, sums):
            rows = rows_at(i)
            pr = pot_r[rows, :]
            return tuple(
                sums[k] + fold(jnp.exp2(value(rows, k, pr) - cvec[7, k : k + 1, :]), jnp.add) for k in range(PLANE)
            )

        sums = lax.fori_loop(0, steps, sum_step, (zero,) * PLANE)
        csum = jnp.concatenate([jnp.sum(v, axis=0, keepdims=True) for v in sums], axis=0)
        cmsg[t - 1] = ctop + log2(csum)
        send_cols(t - 1)

    def take_rows(e):
        wait_rows(e)
        return merge(rrx[e, :, 0:LINE, :])

    def take_cols(e):
        wait_cols(e)
        return merge(crx[e])

    rmsg[...] = jnp.zeros_like(rmsg)
    rmsg[0, LINE : LINE + 8, :] = jnp.broadcast_to(pos[...].astype(F32), (8, BLOCK))
    send_cols(0)
    send_row_lse(1)
    lse_r = take_rows(0)
    pot_r = -0.5 * lse_r
    to_rows(pot_r, rvec.at[0])
    col_lse(2)
    to_rows(lse_r, rvec.at[2])
    to_rows(jnp.concatenate([rrx[0, g, LINE : LINE + 1, :] for g in range(LINE)], axis=0), pr_ref)
    lse_c = take_cols(0)
    pot_c = -0.5 * lse_c
    cvec[2] = lse_c
    cvec[0] = pot_c
    row_lse(2)
    lse_c = take_cols(1)
    pot_c = (pot_c - lse_c) * 0.5
    cvec[3] = lse_c
    cvec[1] = pot_c
    row_lse(3)
    lse_r = take_rows(1)
    pot_r = (pot_r - lse_r) * 0.5
    to_rows(pot_r, rvec.at[1])
    col_lse(3)
    to_rows(lse_r, rvec.at[3])

    first_col = (lax.broadcasted_iota(jnp.int32, (8, BLOCK), 1) + b * BLOCK).astype(F32)
    first_col = jnp.broadcast_to(first_col[0:1], (CH, BLOCK))

    def add_term(t):
        pot_cc, lse_rr, pull_rr = cvec.at[t - 2], rvec.at[t + 1], rvec.at[7 - t]

        def step(i, carry):
            sums, picked = carry
            rows = rows_at(i)
            lr = lse_rr[rows, :]
            if t < 3:
                qr = pull_rr[rows, :]
            else:
                partner = pr_ref[rows, :] - first_col
            out = []
            for k in range(PLANE):
                v = s[rows, lanes(k)]
                u = v + pot_cc[k : k + 1, :] if t > 1 else v
                term = jnp.exp2(u - lr)
                if t < 3:
                    term = term * qr
                    w[rows, lanes(k)] = w[rows, lanes(k)] + term
                else:
                    hit = partner == float(k * RROWS)
                    picked = picked + fold(jnp.where(hit, v, 0.0), jnp.add)
                    w[rows, lanes(k)] = jnp.where(hit, term - 2.0, term)
                if t > 1:
                    out.append(sums[k] + fold(term, jnp.add))
            return tuple(out), picked

        return lax.fori_loop(0, steps, step, ((zero,) * (PLANE if t > 1 else 0), zero))

    def add_mirror(t, start=0, count=steps):
        pot_rr, lse_cc, pull_cc = rvec.at[t - 2], cvec.at[t + 1], cvec.at[7 - t]

        def step(i, carry):
            rows = rows_at(start + i)
            if t > 1:
                pr = pot_rr[rows, :]
            acc = None
            for k in range(PLANE):
                v = s[rows, lanes(k)]
                q = v + pr if t > 1 else v
                mirror = jnp.exp2(q - lse_cc[k : k + 1, :])
                if t < 3:
                    mirror = mirror * pull_cc[k : k + 1, :]
                total = w[rows, lanes(k)] + mirror
                if t > 1:
                    w[rows, lanes(k)] = total
                    acc = mirror if acc is None else acc + mirror
                else:
                    wb[rows, lanes(k)] = total.astype(BF16)
            if t > 1:
                accr[rows, :] = acc
            return carry

        lax.fori_loop(0, count, step, 0)

    def col_sums(e, sums):
        cmsg[e] = jnp.concatenate([jnp.sum(v, axis=0, keepdims=True) for v in sums], axis=0)
        send_cols(e)

    to_rows(take_rows(2), rvec.at[4])
    sums, picked = add_term(3)
    col_sums(3, sums)
    lse_c = take_cols(2)
    cvec[4] = lse_c
    pot_c = (pot_c - lse_c) * 0.5
    add_mirror(3)
    rmsg[3, 0:LINE, :] = row_sums(accr)
    rmsg[3, LINE : LINE + 8, :] = picked + (2.0 / PLANE) * (pot_c[0:8] + pot_c[8:16])
    send_rows(3)
    wait_cols(3)
    cot_c = -1.0 + jnp.sum(crx[3], axis=0)
    cvec[5] = -0.5 * cot_c
    add_mirror(2)
    rmsg[4, 0:LINE, :] = row_sums(accr)
    send_rows(4)
    wait_rows(3)
    cot_r = -1.0 + jnp.sum(rrx[3, :, 0:LINE, :], axis=0)
    to_rows(-0.5 * cot_r, rvec.at[5])
    sums, _ = add_term(2)
    col_sums(4, sums)
    lmsg[...] = jnp.sum(rrx[3, :, LINE : LINE + 8, :], axis=0)
    send_loss()
    wait_rows(4)
    cot_r = 0.5 * cot_r + jnp.sum(rrx[4, :, 0:LINE, :], axis=0)
    to_rows(-0.5 * cot_r, rvec.at[6])
    add_term(1)
    wait_cols(4)
    cot_c = 0.5 * cot_c + jnp.sum(crx[4], axis=0)
    cvec[6] = -0.5 * cot_c

    grad_scale = 1.0 / math.sqrt(WIDTH)

    add_mirror(1)

    def product(n):
        right = ec[:, :, pl.ds(n * TILE, TILE)].reshape(CCOLS, TILE)
        for m in range(2):
            out = jnp.dot(wb[pl.ds(m * 512, 512), :], right, preferred_element_type=F32) * grad_scale
            for g in range(4):
                block = 4 * m + g
                gp[n, block % 2, block // 2] = out[g * BLOCK : (g + 1) * BLOCK]
        pltpu.make_async_remote_copy(
            src_ref=gp.at[n, 1 - core], dst_ref=rb.at[n], send_sem=gsend.at[n], recv_sem=grecv.at[n],
            device_id=(sibling,), device_id_type=MESH,
        ).start()

    def ring(src, dst, i, dx):
        return pltpu.make_async_remote_copy(
            src_ref=src, dst_ref=dst, send_sem=hsend.at[i], recv_sem=hrecv.at[i],
            device_id=(xdev(dx),), device_id_type=MESH,
        )

    half = TILE // 2
    first = [[ring(xs1.at[n, i], xr1.at[n, i], 4 * n + i, dx) for i, dx in ((0, 1), (1, -1))] for n in range(SIDE)]
    second = [[ring(xs2.at[n, i], xr2.at[n, i], 4 * n + 2 + i, dx) for i, dx in ((0, 1), (1, -1))] for n in range(SIDE)]

    def chip_sum(n, d):
        xx = lax.rem(x + d, SIDE)
        return gp[n, core, xx] + rb[n, xx]

    def send_first(n):
        pltpu.make_async_copy(rb.at[n], rb.at[n], grecv.at[n]).wait()
        far = chip_sum(n, 2).astype(BF16)
        xs1[n, 0, :, :half] = far[:, :half]
        xs1[n, 0, :, half:] = chip_sum(n, 1)[:, half:].astype(BF16)
        first[n][0].start()
        xs1[n, 1, :, half:] = far[:, half:]
        xs1[n, 1, :, :half] = chip_sum(n, 3)[:, :half].astype(BF16)
        first[n][1].start()

    def send_second(n):
        first[n][0].wait_recv()
        xs2[n, 0] = (chip_sum(n, 1)[:, :half] + xr1[n, 0, :, :half].astype(F32)).astype(BF16)
        second[n][0].start()
        first[n][1].wait_recv()
        xs2[n, 1] = (chip_sum(n, 3)[:, half:] + xr1[n, 1, :, half:].astype(F32)).astype(BF16)
        second[n][1].start()

    def finish(n):
        own = chip_sum(n, 0)
        second[n][0].wait_recv()
        second[n][1].wait_recv()
        lo, mid = n * TILE, n * TILE + half
        grad[:, lo:mid] = own[:, :half] + xr2[n, 0].astype(F32) + xr1[n, 1, :, :half].astype(F32)
        grad[:, mid : mid + half] = own[:, half:] + xr2[n, 1].astype(F32) + xr1[n, 0, :, half:].astype(F32)

    for n in range(SIDE):
        product(n)
        if n >= 1:
            send_first(n - 1)
        if n >= 2:
            send_second(n - 2)
    send_first(3)
    send_second(2)
    finish(0)
    finish(1)
    send_second(3)
    finish(2)
    finish(3)

    every = lrx.at[pl.ds(0, PLANE - 1)]
    pltpu.make_async_copy(every, every, losem.at[1]).wait()
    loss[0, 0] = jnp.sum(lrx[...]) * (-LN2 / TOTAL)

    pltpu.make_async_copy(every, every, losem.at[0]).wait()
    sent = ec.at[pl.ds(0, PLANE - 1)]
    pltpu.make_async_copy(sent, sent, psend).wait()
    sent = er.at[pl.ds(0, LINE - 1)]
    pltpu.make_async_copy(sent, sent, xsend).wait()
    for e in range(5):
        every = rrx.at[e, pl.ds(0, LINE - 1)]
        pltpu.make_async_copy(every, every, rsend.at[e]).wait()
        every = crx.at[e, pl.ds(0, PLANE - 1)]
        pltpu.make_async_copy(every, every, csend.at[e]).wait()
    for d in range(SIDE):
        pltpu.make_async_copy(rb.at[d], rb.at[d], gsend.at[d]).wait()
    for c in sum(first + second, []):
        c.wait_send()


def shards(embeddings, positives):
    vec = pltpu.VMEM
    dma = pltpu.SemaphoreType.DMA
    grad, loss = pl.pallas_call(
        kernel,
        out_shape=(
            jax.ShapeDtypeStruct((BLOCK, WIDTH), F32),
            jax.ShapeDtypeStruct((1, 1), F32),
        ),
        in_specs=[pl.BlockSpec(memory_space=pl.ANY), pl.BlockSpec(memory_space=pltpu.VMEM)],
        out_specs=(pl.BlockSpec(memory_space=pltpu.VMEM), pl.BlockSpec(memory_space=pltpu.SMEM)),
        scratch_shapes=[
            vec((PLANE, BLOCK, WIDTH), BF16),
            vec((LINE, BLOCK, WIDTH), BF16),
            vec((RROWS, CCOLS), F32),
            vec((RROWS, CCOLS), F32),
            vec((RROWS, CCOLS), BF16),
            vec((7, RROWS, BLOCK), F32),
            vec((8, PLANE, BLOCK), F32),
            vec((RROWS, BLOCK), F32),
            vec((RROWS, BLOCK), F32),
            vec((RROWS, BLOCK), F32),
            vec((5, PLANE, BLOCK), F32),
            vec((5, PLANE, PLANE, BLOCK), F32),
            vec((5, LINE + 8, BLOCK), F32),
            vec((5, LINE, LINE + 8, BLOCK), F32),
            vec((8, BLOCK), F32),
            vec((PLANE, 8, BLOCK), F32),
            vec((SIDE, 2, SIDE, BLOCK, TILE), F32),
            vec((SIDE, SIDE, BLOCK, TILE), F32),
            vec((SIDE, 2, BLOCK, TILE // 2), BF16),
            vec((SIDE, 2, BLOCK, TILE // 2), BF16),
            vec((SIDE, 2, BLOCK, TILE), BF16),
            vec((SIDE, 2, BLOCK, TILE), BF16),
            dma((2,)),
            dma,
            dma((2, 20)),
            dma,
            dma((8,)),
            dma((5,)),
            dma((5,)),
            dma((5,)),
            dma((5,)),
            dma((2,)),
            dma((SIDE,)),
            dma((SIDE,)),
            dma((16,)),
            dma((16,)),
        ],
        compiler_params=pltpu.CompilerParams(
            collective_id=0, has_side_effects=True, vmem_limit_bytes=56 * 1024 * 1024
        ),
    )(embeddings, positives.reshape(1, BLOCK))
    return loss.reshape(()), grad


def solution(mesh):
    placed = (P("dp", None), P("dp"))
    return jax.shard_map(
        shards, mesh=mesh, in_specs=placed, out_specs=(P(), P("dp", None)), check_vma=False
    )
```

```python
import functools
import math

import jax
import jax.numpy as jnp
from jax import lax
from jax.experimental import pallas as pl
from jax.experimental.pallas import tpu as pltpu
from jax.sharding import PartitionSpec as P

SIDE = 4
PLANE = SIDE * SIDE
LINE = SIDE * 2
BLOCK = 128
WIDTH = 1024
RROWS = LINE * BLOCK
CCOLS = PLANE * BLOCK
TOTAL = PLANE * RROWS
LOG2E = math.log2(math.e)
LN2 = math.log(2.0)
MESH = pl.DeviceIdType.MESH
F32 = jnp.float32
BF16 = jnp.bfloat16
TILE = 256
SCORE_M = 8
CH = 64
OFFS = (0, -1, 1, 2)
FAR_FIRST = sorted(
    ((dy, dz) for dy in OFFS for dz in OFFS if (dy, dz) != (0, 0)), key=lambda d: -abs(d[0]) - abs(d[1])
)


def fold(v, op):
    return tree([v[r : r + 8] for r in range(0, v.shape[0], 8)], op)


def tree(v, op):
    while len(v) > 1:
        v = [op(*v[i : i + 2]) if i + 1 < len(v) else v[i] for i in range(0, len(v), 2)]
    return v[0]


def log2(v):
    return jnp.log(v) * LOG2E


def kernel(
    emb, pos, own, parts, loss,
    ec, er, s, w, wb, kept, term2, rvec, cvec, pr_ref, mr, accr, cmsg, crx, rmsg, rrx,
    lmsg, lrx, gp, rb, xs, xr,
    lsem, psend, prsem, xsend, xrsem, csend, crecv, rsend, rrecv, losem, gsend, grecv, hsend, hrecv,
):
    me = lax.axis_index("dp")
    a = me // LINE
    b = me % LINE
    y, z = a // SIDE, a % SIDE
    x, core = b // 2, b % 2

    def dev_of(dy, dz, dx, c):
        yy, zz, xx = (lax.rem(v + d + SIDE, SIDE) for v, d in ((y, dy), (z, dz), (x, dx)))
        return ((yy * SIDE + zz) * SIDE + xx) * 2 + c

    barrier = pltpu.get_barrier_semaphore()

    near_by = (
        [dev_of(dy, dz, dx, core) for dy, dz, dx in ((1, 0, 0), (-1, 0, 0), (0, 1, 0), (0, -1, 0), (0, 0, 1), (0, 0, -1))]
        + [dev_of(0, 0, 0, 1 - core)]
    )
    for device in near_by:
        pl.semaphore_signal(barrier, inc=1, device_id=(device,), device_id_type=MESH)
    own_c = pltpu.make_async_copy(emb, ec.at[a], lsem.at[0])
    own_r = pltpu.make_async_copy(emb, er.at[b], lsem.at[1])
    own_c.start()
    own_r.start()
    pl.semaphore_wait(barrier, len(near_by))

    def blk(h, op, oq):
        dy, dz = (oq, op) if h == 0 else (op, oq)
        return lax.rem(y + dy + SIDE, SIDE) * SIDE + lax.rem(z + dz + SIDE, SIDE)

    def send_plane(h, op, oq, lo, n, tp, tq, idx):
        k = blk(h, op, oq)
        rows = pl.ds(64 * h + lo, n)
        src = emb.at[rows] if (op, oq) == (0, 0) else ec.at[k, rows]
        pltpu.make_async_remote_copy(
            src_ref=src, dst_ref=ec.at[k, rows], send_sem=psend, recv_sem=prsem.at[h, idx],
            device_id=(blk(h, tp, tq) * LINE + b,), device_id_type=MESH,
        ).start()

    def wait_plane(h, op, oq, lo, n, idx):
        ref = ec.at[blk(h, op, oq), pl.ds(64 * h + lo, n)]
        pltpu.make_async_copy(ref, ref, prsem.at[h, idx]).wait()

    def xdev(dx):
        return a * LINE + lax.rem(x + dx + SIDE, SIDE) * 2 + core

    sibling = a * LINE + x * 2 + (1 - core)

    def xblk(dx):
        return lax.rem(x + dx + SIDE, SIDE) * 2 + core

    def send_line(dx, lo, n, device, idx):
        k = xblk(dx)
        rows = pl.ds(lo, n)
        src = emb.at[rows] if dx == 0 else er.at[k, rows]
        pltpu.make_async_remote_copy(
            src_ref=src, dst_ref=er.at[k, rows], send_sem=xsend, recv_sem=xrsem.at[idx],
            device_id=(device,), device_id_type=MESH,
        ).start()

    def wait_line(k, lo, n, idx):
        ref = er.at[k, pl.ds(lo, n)]
        pltpu.make_async_copy(ref, ref, xrsem.at[idx]).wait()

    for h in (0, 1):
        send_plane(h, 0, 0, 0, 64, 1, 0, 0)
        send_plane(h, 0, 0, 0, 64, -1, 0, 1)
    send_line(0, 0, 128, xdev(1), 0)
    send_line(0, 0, 128, xdev(-1), 1)
    send_line(0, 0, 128, sibling, 4)
    for h in (0, 1):
        send_plane(h, 0, 0, 0, 64, 0, 1, 4)
        send_plane(h, 0, 0, 0, 64, 0, -1, 5)
    for h in (0, 1):
        wait_plane(h, -1, 0, 0, 64, 0)
        send_plane(h, -1, 0, 0, 32, 1, 0, 2)
        wait_plane(h, 1, 0, 0, 64, 1)
        send_plane(h, 1, 0, 32, 32, -1, 0, 3)
    wait_line(xblk(-1), 0, 128, 0)
    send_line(-1, 0, 64, xdev(1), 2)
    send_line(-1, 0, 128, sibling, 5)
    wait_line(xblk(1), 0, 128, 1)
    send_line(1, 64, 64, xdev(-1), 3)
    send_line(1, 0, 128, sibling, 6)
    for h in (0, 1):
        for oi in (1, 2):
            send_plane(h, OFFS[oi], 0, 0, 64, 0, 1, 4 + 4 * oi)
            send_plane(h, OFFS[oi], 0, 0, 64, 0, -1, 5 + 4 * oi)
    for h in (0, 1):
        wait_plane(h, 0, -1, 0, 64, 4)
        send_plane(h, 0, -1, 0, 32, 0, 1, 6)
        wait_plane(h, 0, 1, 0, 64, 5)
        send_plane(h, 0, 1, 32, 32, 0, -1, 7)
    for h in (0, 1):
        wait_plane(h, 2, 0, 0, 32, 2)
        wait_plane(h, 2, 0, 32, 32, 3)
        send_plane(h, 2, 0, 0, 64, 0, 1, 16)
        send_plane(h, 2, 0, 0, 64, 0, -1, 17)
    wait_line(xblk(2), 0, 64, 2)
    wait_line(xblk(2), 64, 64, 3)
    send_line(2, 0, 128, sibling, 7)
    for i, dx in enumerate((0, -1, 1, 2)):
        wait_line(lax.rem(x + dx + SIDE, SIDE) * 2 + (1 - core), 0, 128, 4 + i)
    own_c.wait()
    own_r.wait()

    eye = lax.broadcasted_iota(jnp.int32, (BLOCK, BLOCK), 0) == lax.broadcasted_iota(jnp.int32, (BLOCK, BLOCK), 1)
    low = jnp.full((8, BLOCK), -3e38, F32)
    zero = jnp.zeros((8, BLOCK), F32)
    steps = RROWS // CH

    def rows_at(i):
        return pl.ds(pl.multiple_of(i * CH, CH), CH)

    score_scale = LOG2E / math.sqrt(WIDTH)

    def score_tile(n):
        right = ec[pl.ds(2 * n, 2)].reshape(2 * BLOCK, WIDTH)
        cols = pl.ds(pl.multiple_of(n * 256, 256), 256)
        for m in range(LINE // SCORE_M):
            left = er[pl.ds(SCORE_M * m, SCORE_M)].reshape(SCORE_M * BLOCK, WIDTH)
            out = lax.dot_general(left, right, (((1,), (1,)), ((), ())), preferred_element_type=F32)
            s[pl.ds(m * SCORE_M * BLOCK, SCORE_M * BLOCK), cols] = out * score_scale

    def first_sums(n):
        two = [pl.ds(pl.multiple_of(n * 256 + k * BLOCK, BLOCK), BLOCK) for k in range(2)]

        def step(i, carry):
            rows = rows_at(i)
            v = [s[rows, c] for c in two]
            old = mr[rows, :]
            top = jnp.maximum(jnp.maximum(v[0], v[1]), old)
            mr[rows, :] = top
            accr[rows, :] = accr[rows, :] * jnp.exp2(old - top) + (jnp.exp2(v[0] - top) + jnp.exp2(v[1] - top))
            out = []
            for k in range(2):
                old, acc = carry[k]
                top = jnp.maximum(old, fold(v[k], jnp.maximum))
                p = [jnp.exp2(v[k][r : r + 8] - top) for r in range(0, CH, 8)]
                out.append((top, acc * jnp.exp2(old - top) + tree(p, jnp.add)))
            return tuple(out)

        sums = lax.fori_loop(0, steps, step, ((low, zero),) * 2)
        for k in range(2):
            each, acc = sums[k]
            top = jnp.max(each, axis=0, keepdims=True)
            cmsg[0, pl.ds(2 * n + k, 1), :] = top + log2(jnp.sum(acc * jnp.exp2(each - top), axis=0, keepdims=True))

    def wait_forwarded(h, oi):
        wait_plane(h, OFFS[oi], 2, 0, 32, 6 + 4 * oi)
        wait_plane(h, OFFS[oi], 2, 32, 32, 7 + 4 * oi)

    def second_stage(oi):
        o = OFFS[oi]
        for h in (0, 1):
            wait_plane(h, o, -1, 0, 64, 4 + 4 * oi)
            send_plane(h, o, -1, 0, 32, 0, 1, 6 + 4 * oi)
            wait_plane(h, o, 1, 0, 64, 5 + 4 * oi)
            send_plane(h, o, 1, 32, 32, 0, -1, 7 + 4 * oi)

    def tile_step(i, carry):
        @pl.when(i == 1)
        def _():
            second_stage(1)
            wait_forwarded(1, 0)

        @pl.when(i == 2)
        def _():
            second_stage(2)

        @pl.when(i == 4)
        def _():
            second_stage(3)
            wait_forwarded(1, 1)
            wait_forwarded(1, 2)

        @pl.when(i == 6)
        def _():
            wait_forwarded(0, 0)
            wait_forwarded(0, 1)
            wait_forwarded(0, 2)

        @pl.when(i == 7)
        def _():
            wait_forwarded(0, 3)
            wait_forwarded(1, 3)

        def pick(values):
            out = values[0]
            for k in range(1, 8):
                out = jnp.where(i == k, values[k], out)
            return out

        half = z // 2
        other = pick((0, 1, 0, 0, 1, 1, 0, 1))
        n = lax.rem(y + pick((0, 0, 3, 1, 3, 1, 2, 2)), SIDE) * 2 + lax.rem(half + other, 2)
        score_tile(n)

        @pl.when(i == 0)
        def _():
            dr = pl.ds(pl.multiple_of(b * BLOCK, BLOCK), BLOCK)
            dc = pl.ds(pl.multiple_of(a * BLOCK, BLOCK), BLOCK)
            s[dr, dc] = jnp.where(eye, -30000.0 * LOG2E, s[dr, dc])

        first_sums(n)
        return carry

    mr[...] = jnp.full((RROWS, BLOCK), -3e38, F32)
    accr[...] = jnp.zeros((RROWS, BLOCK), F32)
    lax.fori_loop(0, 8, tile_step, 0)

    def lanes(k):
        return slice(k * BLOCK, (k + 1) * BLOCK)

    def to_rows(v, ref):
        for g in range(LINE):
            ref[pl.ds(g * BLOCK, BLOCK), :] = jnp.broadcast_to(v[g : g + 1], (BLOCK, BLOCK)).T

    def row_sums(ref):
        out = [jnp.sum(ref[pl.ds(g * BLOCK, BLOCK), :].T, axis=0, keepdims=True) for g in range(LINE)]
        return jnp.concatenate(out, axis=0)

    def send_cols(e):
        for dy, dz in FAR_FIRST:
            pltpu.make_async_remote_copy(
                src_ref=cmsg.at[e], dst_ref=crx.at[e, a], send_sem=csend.at[e], recv_sem=crecv.at[e],
                device_id=(dev_of(dy, dz, 0, core),), device_id_type=MESH,
            ).start()
        crx[e, a] = cmsg[e]

    def row_part(e):
        return pl.ds(0, LINE + 8 if e in (0, 3) else LINE)

    def send_rows(e):
        for dx, other in ((2, 1), (2, 0), (1, 1), (-1, 1), (1, 0), (-1, 0), (0, 1)):
            pltpu.make_async_remote_copy(
                src_ref=rmsg.at[e, row_part(e)], dst_ref=rrx.at[e, b, row_part(e)],
                send_sem=rsend.at[e], recv_sem=rrecv.at[e],
                device_id=(dev_of(0, 0, dx, 1 - core if other else core),), device_id_type=MESH,
            ).start()
        rrx[e, b] = rmsg[e]

    def wait_cols(e):
        every = crx.at[e, pl.ds(0, PLANE - 1)]
        pltpu.make_async_copy(every, every, crecv.at[e]).wait()

    def wait_rows(e):
        every = rrx.at[e, pl.ds(0, LINE - 1), row_part(e)]
        pltpu.make_async_copy(every, every, rrecv.at[e]).wait()

    def send_loss():
        for dy, dz in FAR_FIRST:
            pltpu.make_async_remote_copy(
                src_ref=lmsg, dst_ref=lrx.at[a], send_sem=losem.at[0], recv_sem=losem.at[1],
                device_id=(dev_of(dy, dz, 0, core),), device_id_type=MESH,
            ).start()
        lrx[a] = lmsg[...]

    def merge(v):
        top = jnp.max(v, axis=0)
        return top + log2(jnp.sum(jnp.exp2(v - top[None]), axis=0))

    def row_lse(t):
        pot_c = cvec.at[t - 2]

        def step(i, carry):
            rows = rows_at(i)
            best = tree([s[rows, lanes(k)] + pot_c[k : k + 1, :] for k in range(PLANE)], jnp.maximum)
            mr[rows, :] = best
            acc = None
            for k in range(PLANE):
                p = jnp.exp2(s[rows, lanes(k)] + pot_c[k : k + 1, :] - best)
                acc = p if acc is None else acc + p
            accr[rows, :] = acc
            return carry

        lax.fori_loop(0, steps, step, 0)
        send_row_lse(t)

    def send_row_lse(t):
        out = []
        for g in range(LINE):
            best = mr[pl.ds(g * BLOCK, BLOCK), :].T
            acc = accr[pl.ds(g * BLOCK, BLOCK), :].T
            top = jnp.max(best, axis=0, keepdims=True)
            out.append(top + log2(jnp.sum(acc * jnp.exp2(best - top), axis=0, keepdims=True)))
        rmsg[t - 1, 0:LINE, :] = jnp.concatenate(out, axis=0)
        send_rows(t - 1)

    def col_lse(t):
        pot_r = rvec.at[t - 2]

        def value(rows, k, pr):
            return s[rows, lanes(k)] + pr

        def top_step(i, tops):
            rows = rows_at(i)
            pr = pot_r[rows, :]
            return tuple(jnp.maximum(tops[k], fold(value(rows, k, pr), jnp.maximum)) for k in range(PLANE))

        tops = lax.fori_loop(0, steps, top_step, (low,) * PLANE)
        ctop = jnp.concatenate([jnp.max(v, axis=0, keepdims=True) for v in tops], axis=0)
        cvec[7] = ctop

        def sum_step(i, sums):
            rows = rows_at(i)
            pr = pot_r[rows, :]
            out = []
            for k in range(PLANE):
                p = jnp.exp2(value(rows, k, pr) - cvec[7, k : k + 1, :])
                if t == 3:
                    kept[rows, lanes(k)] = p
                out.append(sums[k] + fold(p, jnp.add))
            return tuple(out)

        sums = lax.fori_loop(0, steps, sum_step, (zero,) * PLANE)
        csum = jnp.concatenate([jnp.sum(v, axis=0, keepdims=True) for v in sums], axis=0)
        cmsg[t - 1] = ctop + log2(csum)
        send_cols(t - 1)

    def take_rows(e):
        wait_rows(e)
        return merge(rrx[e, :, 0:LINE, :])

    def take_cols(e):
        wait_cols(e)
        return merge(crx[e])

    rmsg[...] = jnp.zeros_like(rmsg)
    rmsg[0, LINE : LINE + 8, :] = jnp.broadcast_to(pos[...].astype(F32), (8, BLOCK))
    send_cols(0)
    send_row_lse(1)
    lse_r = take_rows(0)
    pot_r = -0.5 * lse_r
    to_rows(pot_r, rvec.at[0])
    col_lse(2)
    to_rows(lse_r, rvec.at[2])
    to_rows(jnp.concatenate([rrx[0, g, LINE : LINE + 1, :] for g in range(LINE)], axis=0), pr_ref)
    lse_c = take_cols(0)
    pot_c = -0.5 * lse_c
    cvec[2] = lse_c
    cvec[0] = pot_c
    row_lse(2)
    lse_c = take_cols(1)
    pot_c = (pot_c - lse_c) * 0.5
    cvec[3] = lse_c
    cvec[1] = pot_c
    row_lse(3)
    lse_r = take_rows(1)
    pot_r = (pot_r - lse_r) * 0.5
    to_rows(pot_r, rvec.at[1])
    col_lse(3)
    to_rows(lse_r, rvec.at[3])

    first_col = (lax.broadcasted_iota(jnp.int32, (8, BLOCK), 1) + b * BLOCK).astype(F32)
    first_col = jnp.broadcast_to(first_col[0:1], (CH, BLOCK))

    def add_term(t):
        def step(i, carry):
            sums, picked = carry
            rows = rows_at(i)
            if t < 3:
                qr = rvec[5, rows, :]
            else:
                lr = rvec[4, rows, :]
                partner = pr_ref[rows, :] - first_col
            out = []
            for k in range(PLANE):
                if t < 3:
                    term = term2[rows, lanes(k)] * qr
                    w[rows, lanes(k)] = w[rows, lanes(k)] + term
                else:
                    v = s[rows, lanes(k)]
                    term = jnp.exp2(v + cvec[1, k : k + 1, :] - lr)
                    hit = partner == float(k * RROWS)
                    picked = picked + fold(jnp.where(hit, v, 0.0), jnp.add)
                    w[rows, lanes(k)] = jnp.where(hit, term - 2.0, term)
                out.append(sums[k] + fold(term, jnp.add))
            return tuple(out), picked

        return lax.fori_loop(0, steps, step, ((zero,) * PLANE, zero))

    def add_mirror(factor):
        def step(i, carry):
            rows = rows_at(i)
            acc = None
            for k in range(PLANE):
                mirror = kept[rows, lanes(k)] * factor[k : k + 1, :]
                w[rows, lanes(k)] = w[rows, lanes(k)] + mirror
                acc = mirror if acc is None else acc + mirror
            accr[rows, :] = acc
            return carry

        lax.fori_loop(0, steps, step, 0)

    def keep_term():
        def step(i, carry):
            rows = rows_at(i)
            lr = rvec[3, rows, :]
            for k in range(PLANE):
                term2[rows, lanes(k)] = jnp.exp2(s[rows, lanes(k)] + cvec[0, k : k + 1, :] - lr)
            return carry

        lax.fori_loop(0, steps, step, 0)

    def keep_mirror(t):
        def step(i, carry):
            rows = rows_at(i)
            for k in range(PLANE):
                v = s[rows, lanes(k)]
                if t == 2:
                    v = v + rvec[0, rows, :]
                kept[rows, lanes(k)] = jnp.exp2(v - cvec[t + 1, k : k + 1, :])
            return carry

        lax.fori_loop(0, steps, step, 0)

    def add_first_term():
        def step(i, carry):
            rows = rows_at(i)
            lr = rvec[2, rows, :]
            qr = rvec[6, rows, :]
            for k in range(PLANE):
                w[rows, lanes(k)] = w[rows, lanes(k)] + jnp.exp2(s[rows, lanes(k)] - lr) * qr
            return carry

        lax.fori_loop(0, steps, step, 0)

    def round_weights(start, count):
        def step(i, carry):
            rows = rows_at(start + i)
            for k in range(PLANE):
                total = w[rows, lanes(k)] + kept[rows, lanes(k)] * cvec[6, k : k + 1, :]
                wb[rows, lanes(k)] = total.astype(BF16)
            return carry

        lax.fori_loop(0, count, step, 0)

    def col_sums(e, sums):
        cmsg[e] = jnp.concatenate([jnp.sum(v, axis=0, keepdims=True) for v in sums], axis=0)
        send_cols(e)

    to_rows(take_rows(2), rvec.at[4])
    sums, picked = add_term(3)
    col_sums(3, sums)
    keep_term()
    lse_c = take_cols(2)
    pot_c = (pot_c - lse_c) * 0.5
    cvec[4] = jnp.exp2(cvec[7] - lse_c)
    add_mirror(cvec.at[4])
    rmsg[3, 0:LINE, :] = row_sums(accr)
    rmsg[3, LINE : LINE + 8, :] = picked + (2.0 / PLANE) * (pot_c[0:8] + pot_c[8:16])
    send_rows(3)
    keep_mirror(2)
    wait_cols(3)
    cot_c = -1.0 + jnp.sum(crx[3], axis=0)
    cvec[5] = -0.5 * cot_c
    add_mirror(cvec.at[5])
    rmsg[4, 0:LINE, :] = row_sums(accr)
    send_rows(4)
    wait_rows(3)
    cot_r = -1.0 + jnp.sum(rrx[3, :, 0:LINE, :], axis=0)
    to_rows(-0.5 * cot_r, rvec.at[5])
    sums, _ = add_term(2)
    col_sums(4, sums)
    lmsg[...] = jnp.sum(rrx[3, :, LINE : LINE + 8, :], axis=0)
    send_loss()
    keep_mirror(1)
    wait_rows(4)
    cot_r = 0.5 * cot_r + jnp.sum(rrx[4, :, 0:LINE, :], axis=0)
    to_rows(-0.5 * cot_r, rvec.at[6])
    add_first_term()
    wait_cols(4)
    cot_c = 0.5 * cot_c + jnp.sum(crx[4], axis=0)
    cvec[6] = -0.5 * cot_c

    grad_scale = 1.0 / math.sqrt(WIDTH)

    def product(d):
        xx = lax.rem(x + d, SIDE)
        round_weights(xx * (2 * BLOCK // CH), 2 * BLOCK // CH)
        rows = pl.ds(pl.multiple_of(xx * 2 * BLOCK, 2 * BLOCK), 2 * BLOCK)
        left = wb[rows, :]
        for n in range(WIDTH // TILE):
            right = ec[:, :, pl.ds(n * TILE, TILE)].reshape(CCOLS, TILE)
            out = jnp.dot(left, right, preferred_element_type=F32) * grad_scale
            gp[d, :, :, n * TILE : (n + 1) * TILE] = out.reshape(2, BLOCK, TILE)
        pltpu.make_async_remote_copy(
            src_ref=gp.at[d, 1 - core], dst_ref=rb.at[d], send_sem=gsend.at[d], recv_sem=grecv.at[d],
            device_id=(sibling,), device_id_type=MESH,
        ).start()

    def chip_sum(d):
        pltpu.make_async_copy(rb.at[d], rb.at[d], grecv.at[d]).wait()
        return gp[d, core] + rb[d]

    def ring(n, i, dx):
        return pltpu.make_async_remote_copy(
            src_ref=xs.at[n, i], dst_ref=xr.at[i] if n == 0 else parts.at[n - 1, i],
            send_sem=hsend.at[2 * n + i], recv_sem=hrecv.at[2 * n + i],
            device_id=(xdev(dx),), device_id_type=MESH,
        )

    half = WIDTH // 2
    far, direct, near = [[ring(n, i, dx) for i, dx in ((0, 1), (1, -1))] for n in range(3)]

    def product_step(i, carry):
        product(jnp.where(i == 0, 2, jnp.where(i == 1, 1, jnp.where(i == 2, 3, 0))))

        @pl.when(i == 1)
        def _():
            v = chip_sum(2).astype(BF16)
            xs[0, 0] = v[:, :half]
            far[0].start()
            xs[0, 1] = v[:, half:]
            far[1].start()

        @pl.when(i == 2)
        def _():
            v = chip_sum(1)
            xs[1, 0] = v[:, half:].astype(BF16)
            direct[0].start()
            rb[1, :, :half] = v[:, :half]

        @pl.when(i == 3)
        def _():
            v = chip_sum(3)
            xs[1, 1] = v[:, :half].astype(BF16)
            direct[1].start()
            rb[3, :, half:] = v[:, half:]

        return carry

    lax.fori_loop(0, SIDE, product_step, 0)
    far[0].wait_recv()
    xs[2, 0] = (rb[1, :, :half] + xr[0].astype(F32)).astype(BF16)
    near[0].start()
    far[1].wait_recv()
    xs[2, 1] = (rb[3, :, half:] + xr[1].astype(F32)).astype(BF16)
    near[1].start()
    rb[0] = chip_sum(0)
    result = pltpu.make_async_copy(rb.at[0], own, lsem.at[2])
    result.start()
    for c in direct + near:
        c.wait_recv()
    result.wait()

    every = lrx.at[pl.ds(0, PLANE - 1)]
    pltpu.make_async_copy(every, every, losem.at[1]).wait()
    loss[0, 0] = jnp.sum(lrx[...]) * (-LN2 / TOTAL)

    pltpu.make_async_copy(every, every, losem.at[0]).wait()
    sent = ec.at[pl.ds(0, PLANE - 1)]
    pltpu.make_async_copy(sent, sent, psend).wait()
    sent = er.at[pl.ds(0, LINE - 1)]
    pltpu.make_async_copy(sent, sent, xsend).wait()
    for e in range(5):
        every = rrx.at[e, pl.ds(0, LINE - 1), row_part(e)]
        pltpu.make_async_copy(every, every, rsend.at[e]).wait()
        every = crx.at[e, pl.ds(0, PLANE - 1)]
        pltpu.make_async_copy(every, every, csend.at[e]).wait()
    for d in range(SIDE):
        pltpu.make_async_copy(rb.at[d], rb.at[d], gsend.at[d]).wait()
    for c in far + direct + near:
        c.wait_send()


def add_parts(own, parts, total, grad, loss):
    half = WIDTH // 2
    grad[:, :half] = own[:, :half] + parts[0, 1].astype(F32) + parts[1, 0].astype(F32)
    grad[:, half:] = own[:, half:] + parts[0, 0].astype(F32) + parts[1, 1].astype(F32)
    loss[0, 0] = total[0, 0]


def shards(embeddings, positives):
    vec = pltpu.VMEM
    dma = pltpu.SemaphoreType.DMA
    own, parts, total = pl.pallas_call(
        kernel,
        out_shape=(
            jax.ShapeDtypeStruct((BLOCK, WIDTH), F32),
            jax.ShapeDtypeStruct((2, 2, BLOCK, WIDTH // 2), BF16),
            jax.ShapeDtypeStruct((1, 1), F32),
        ),
        in_specs=[pl.BlockSpec(memory_space=pl.ANY), pl.BlockSpec(memory_space=pltpu.VMEM)],
        out_specs=(
            pl.BlockSpec(memory_space=pl.ANY),
            pl.BlockSpec(memory_space=pl.ANY),
            pl.BlockSpec(memory_space=pltpu.SMEM),
        ),
        scratch_shapes=[
            vec((PLANE, BLOCK, WIDTH), BF16),
            vec((LINE, BLOCK, WIDTH), BF16),
            vec((RROWS, CCOLS), F32),
            vec((RROWS, CCOLS), F32),
            vec((RROWS, CCOLS), BF16),
            vec((RROWS, CCOLS), F32),
            vec((RROWS, CCOLS), F32),
            vec((7, RROWS, BLOCK), F32),
            vec((8, PLANE, BLOCK), F32),
            vec((RROWS, BLOCK), F32),
            vec((RROWS, BLOCK), F32),
            vec((RROWS, BLOCK), F32),
            vec((5, PLANE, BLOCK), F32),
            vec((5, PLANE, PLANE, BLOCK), F32),
            vec((5, LINE + 8, BLOCK), F32),
            vec((5, LINE, LINE + 8, BLOCK), F32),
            vec((8, BLOCK), F32),
            vec((PLANE, 8, BLOCK), F32),
            vec((SIDE, 2, BLOCK, WIDTH), F32),
            vec((SIDE, BLOCK, WIDTH), F32),
            vec((3, 2, BLOCK, WIDTH // 2), BF16),
            vec((2, BLOCK, WIDTH // 2), BF16),
            dma((3,)),
            dma,
            dma((2, 20)),
            dma,
            dma((8,)),
            dma((5,)),
            dma((5,)),
            dma((5,)),
            dma((5,)),
            dma((2,)),
            dma((SIDE,)),
            dma((SIDE,)),
            dma((6,)),
            dma((6,)),
        ],
        compiler_params=pltpu.CompilerParams(
            collective_id=0, has_side_effects=True, vmem_limit_bytes=60 * 1024 * 1024
        ),
    )(embeddings, positives.reshape(1, BLOCK))
    grad, loss = pl.pallas_call(
        add_parts,
        out_shape=(jax.ShapeDtypeStruct((BLOCK, WIDTH), F32), jax.ShapeDtypeStruct((1, 1), F32)),
        grid=(2,),
        in_specs=[
            pl.BlockSpec((BLOCK // 2, WIDTH), lambda i: (i, 0)),
            pl.BlockSpec((2, 2, BLOCK // 2, WIDTH // 2), lambda i: (0, 0, i, 0)),
            pl.BlockSpec(memory_space=pltpu.SMEM),
        ],
        out_specs=(pl.BlockSpec((BLOCK // 2, WIDTH), lambda i: (i, 0)), pl.BlockSpec(memory_space=pltpu.SMEM)),
    )(own, parts, total)
    return loss.reshape(()), grad


def solution(mesh):
    placed = (P("dp", None), P("dp"))
    return jax.shard_map(
        shards, mesh=mesh, in_specs=placed, out_specs=(P(), P("dp", None)), check_vma=False
    )
```

```python
import functools
import math

import jax
import jax.numpy as jnp
from jax import lax
from jax.experimental import pallas as pl
from jax.experimental.pallas import tpu as pltpu
from jax.sharding import PartitionSpec as P

SIDE = 4
PLANE = SIDE * SIDE
LINE = SIDE * 2
BLOCK = 128
WIDTH = 1024
RROWS = LINE * BLOCK
CCOLS = PLANE * BLOCK
TOTAL = PLANE * RROWS
LOG2E = math.log2(math.e)
LN2 = math.log(2.0)
MESH = pl.DeviceIdType.MESH
F32 = jnp.float32
BF16 = jnp.bfloat16
TILE = 256
SCORE_M = 8
CH = 64
OFFS = (0, -1, 1, 2)
OWN_SLOTS = (1, 4, 5, 6)
FORWARD_SLOTS = (3, 7, 8, 9)
FAR_FIRST = sorted(
    ((dy, dz) for dy in OFFS for dz in OFFS if (dy, dz) != (0, 0)), key=lambda d: -abs(d[0]) - abs(d[1])
)


def fold(v, op):
    return tree([v[r : r + 8] for r in range(0, v.shape[0], 8)], op)


def tree(v, op):
    while len(v) > 1:
        v = [op(*v[i : i + 2]) if i + 1 < len(v) else v[i] for i in range(0, len(v), 2)]
    return v[0]


def log2(v):
    return jnp.log(v) * LOG2E


def kernel(
    emb, pos, own, parts, loss,
    ec, er, s, w, wb, kept, term2, rvec, cvec, pr_ref, mr, accr, cmsg, crx, rmsg, rrx,
    lmsg, lrx, gp, rb, xs, xr,
    lsem, psend, prsem, xsend, xrsem, csend, crecv, rsend, rrecv, losem, gsend, grecv, hsend, hrecv,
):
    me = lax.axis_index("dp")
    a = me // LINE
    b = me % LINE
    y, z = a // SIDE, a % SIDE
    x, core = b // 2, b % 2

    def dev_of(dy, dz, dx, c):
        yy, zz, xx = (lax.rem(v + d + SIDE, SIDE) for v, d in ((y, dy), (z, dz), (x, dx)))
        return ((yy * SIDE + zz) * SIDE + xx) * 2 + c

    barrier = pltpu.get_barrier_semaphore()

    near_by = (
        [dev_of(dy, dz, dx, core) for dy, dz, dx in ((1, 0, 0), (-1, 0, 0), (0, 1, 0), (0, -1, 0), (0, 0, 1), (0, 0, -1))]
        + [dev_of(0, 0, 0, 1 - core)]
    )
    for device in near_by:
        pl.semaphore_signal(barrier, inc=1, device_id=(device,), device_id_type=MESH)
    own_c = pltpu.make_async_copy(emb, ec.at[a], lsem.at[0])
    own_r = pltpu.make_async_copy(emb, er.at[b], lsem.at[1])
    own_c.start()
    own_r.start()
    pl.semaphore_wait(barrier, len(near_by))

    def blk(h, op, oq):
        dy, dz = (oq, op) if h == 0 else (op, oq)
        return lax.rem(y + dy + SIDE, SIDE) * SIDE + lax.rem(z + dz + SIDE, SIDE)

    def send_plane(h, op, oq, lo, n, tp, tq, idx, slot):
        k = blk(h, op, oq)
        rows = pl.ds(64 * h + lo, n)
        src = emb.at[rows] if (op, oq) == (0, 0) else ec.at[k, rows]
        pltpu.make_async_remote_copy(
            src_ref=src, dst_ref=ec.at[k, rows], send_sem=psend.at[slot], recv_sem=prsem.at[h, idx],
            device_id=(blk(h, tp, tq) * LINE + b,), device_id_type=MESH,
        ).start()

    def wait_plane(h, op, oq, lo, n, idx):
        ref = ec.at[blk(h, op, oq), pl.ds(64 * h + lo, n)]
        pltpu.make_async_copy(ref, ref, prsem.at[h, idx]).wait()

    def xdev(dx):
        return a * LINE + lax.rem(x + dx + SIDE, SIDE) * 2 + core

    sibling = a * LINE + x * 2 + (1 - core)

    def xblk(dx):
        return lax.rem(x + dx + SIDE, SIDE) * 2 + core

    def send_line(dx, lo, n, device, idx):
        k = xblk(dx)
        rows = pl.ds(lo, n)
        src = emb.at[rows] if dx == 0 else er.at[k, rows]
        pltpu.make_async_remote_copy(
            src_ref=src, dst_ref=er.at[k, rows], send_sem=xsend, recv_sem=xrsem.at[idx],
            device_id=(device,), device_id_type=MESH,
        ).start()

    def wait_line(k, lo, n, idx):
        ref = er.at[k, pl.ds(lo, n)]
        pltpu.make_async_copy(ref, ref, xrsem.at[idx]).wait()

    def issue(slot):
        for h in (0, 1):
            if slot == 0:
                send_plane(h, 0, 0, 0, 64, 1, 0, 0, slot)
                send_plane(h, 0, 0, 0, 64, -1, 0, 1, slot)
            elif slot == 2:
                send_plane(h, -1, 0, 0, 32, 1, 0, 2, slot)
                send_plane(h, 1, 0, 32, 32, -1, 0, 3, slot)
            elif slot in OWN_SLOTS:
                oi = OWN_SLOTS.index(slot)
                send_plane(h, OFFS[oi], 0, 0, 64, 0, 1, 4 + 4 * oi, slot)
                send_plane(h, OFFS[oi], 0, 0, 64, 0, -1, 5 + 4 * oi, slot)
            else:
                oi = FORWARD_SLOTS.index(slot)
                send_plane(h, OFFS[oi], -1, 0, 32, 0, 1, 6 + 4 * oi, slot)
                send_plane(h, OFFS[oi], 1, 32, 32, 0, -1, 7 + 4 * oi, slot)

    def sent(slot):
        ref = ec.at[pl.ds(0, 1 if slot == 2 or slot in FORWARD_SLOTS else 2)]
        pltpu.make_async_copy(ref, ref, psend.at[slot]).wait()

    def arrived(slot):
        for h in (0, 1):
            if slot == 0:
                wait_plane(h, -1, 0, 0, 64, 0)
                wait_plane(h, 1, 0, 0, 64, 1)
            elif slot == 2:
                wait_plane(h, 2, 0, 0, 32, 2)
                wait_plane(h, 2, 0, 32, 32, 3)
            elif slot in OWN_SLOTS:
                oi = OWN_SLOTS.index(slot)
                wait_plane(h, OFFS[oi], -1, 0, 64, 4 + 4 * oi)
                wait_plane(h, OFFS[oi], 1, 0, 64, 5 + 4 * oi)
            else:
                oi = FORWARD_SLOTS.index(slot)
                wait_plane(h, OFFS[oi], 2, 0, 32, 6 + 4 * oi)
                wait_plane(h, OFFS[oi], 2, 32, 32, 7 + 4 * oi)

    issue(0)
    send_line(0, 0, 128, xdev(1), 0)
    send_line(0, 0, 128, xdev(-1), 1)
    send_line(0, 0, 128, sibling, 4)
    issue(1)
    arrived(0)
    sent(0)
    issue(2)
    arrived(1)
    sent(1)
    issue(3)
    wait_line(xblk(-1), 0, 128, 0)
    send_line(-1, 0, 64, xdev(1), 2)
    send_line(-1, 0, 128, sibling, 5)
    wait_line(xblk(1), 0, 128, 1)
    send_line(1, 64, 64, xdev(-1), 3)
    send_line(1, 0, 128, sibling, 6)
    sent(2)
    issue(4)
    sent(3)
    issue(5)
    arrived(2)
    wait_line(xblk(2), 0, 64, 2)
    wait_line(xblk(2), 64, 64, 3)
    send_line(2, 0, 128, sibling, 7)
    for i, dx in enumerate((0, -1, 1, 2)):
        wait_line(lax.rem(x + dx + SIDE, SIDE) * 2 + (1 - core), 0, 128, 4 + i)
    own_c.wait()
    own_r.wait()
    sent(4)
    issue(6)

    eye = lax.broadcasted_iota(jnp.int32, (BLOCK, BLOCK), 0) == lax.broadcasted_iota(jnp.int32, (BLOCK, BLOCK), 1)
    low = jnp.full((8, BLOCK), -3e38, F32)
    zero = jnp.zeros((8, BLOCK), F32)
    steps = RROWS // CH

    def rows_at(i):
        return pl.ds(pl.multiple_of(i * CH, CH), CH)

    score_scale = LOG2E / math.sqrt(WIDTH)

    def score_tile(n):
        right = ec[pl.ds(2 * n, 2)].reshape(2 * BLOCK, WIDTH)
        cols = pl.ds(pl.multiple_of(n * 256, 256), 256)
        for m in range(LINE // SCORE_M):
            left = er[pl.ds(SCORE_M * m, SCORE_M)].reshape(SCORE_M * BLOCK, WIDTH)
            out = lax.dot_general(left, right, (((1,), (1,)), ((), ())), preferred_element_type=F32)
            s[pl.ds(m * SCORE_M * BLOCK, SCORE_M * BLOCK), cols] = out * score_scale

    def first_sums(n):
        two = [pl.ds(pl.multiple_of(n * 256 + k * BLOCK, BLOCK), BLOCK) for k in range(2)]

        def step(i, carry):
            rows = rows_at(i)
            v = [s[rows, c] for c in two]
            old = mr[rows, :]
            top = jnp.maximum(jnp.maximum(v[0], v[1]), old)
            mr[rows, :] = top
            accr[rows, :] = accr[rows, :] * jnp.exp2(old - top) + (jnp.exp2(v[0] - top) + jnp.exp2(v[1] - top))
            out = []
            for k in range(2):
                old, acc = carry[k]
                top = jnp.maximum(old, fold(v[k], jnp.maximum))
                p = [jnp.exp2(v[k][r : r + 8] - top) for r in range(0, CH, 8)]
                out.append((top, acc * jnp.exp2(old - top) + tree(p, jnp.add)))
            return tuple(out)

        sums = lax.fori_loop(0, steps, step, ((low, zero),) * 2)
        for k in range(2):
            each, acc = sums[k]
            top = jnp.max(each, axis=0, keepdims=True)
            cmsg[0, pl.ds(2 * n + k, 1), :] = top + log2(jnp.sum(acc * jnp.exp2(each - top), axis=0, keepdims=True))

    def tile_step(i, carry):
        @pl.when(i == 1)
        def _():
            arrived(3)

        @pl.when(i == 2)
        def _():
            arrived(4)
            sent(5)
            issue(7)
            arrived(5)

        @pl.when(i == 3)
        def _():
            sent(6)
            issue(8)

        @pl.when(i == 4)
        def _():
            arrived(6)
            sent(7)
            issue(9)
            arrived(7)

        @pl.when(i == 5)
        def _():
            arrived(8)

        @pl.when(i == 7)
        def _():
            arrived(9)

        def pick(values):
            out = values[0]
            for k in range(1, 8):
                out = jnp.where(i == k, values[k], out)
            return out

        half = z // 2
        other = pick((0, 1, 0, 0, 1, 1, 0, 1))
        n = lax.rem(y + pick((0, 0, 3, 1, 3, 1, 2, 2)), SIDE) * 2 + lax.rem(half + other, 2)
        score_tile(n)

        @pl.when(i == 0)
        def _():
            dr = pl.ds(pl.multiple_of(b * BLOCK, BLOCK), BLOCK)
            dc = pl.ds(pl.multiple_of(a * BLOCK, BLOCK), BLOCK)
            s[dr, dc] = jnp.where(eye, -30000.0 * LOG2E, s[dr, dc])

        first_sums(n)
        return carry

    mr[...] = jnp.full((RROWS, BLOCK), -3e38, F32)
    accr[...] = jnp.zeros((RROWS, BLOCK), F32)
    lax.fori_loop(0, 8, tile_step, 0)

    def lanes(k):
        return slice(k * BLOCK, (k + 1) * BLOCK)

    def to_rows(v, ref):
        for g in range(LINE):
            ref[pl.ds(g * BLOCK, BLOCK), :] = jnp.broadcast_to(v[g : g + 1], (BLOCK, BLOCK)).T

    def row_sums(ref):
        out = [jnp.sum(ref[pl.ds(g * BLOCK, BLOCK), :].T, axis=0, keepdims=True) for g in range(LINE)]
        return jnp.concatenate(out, axis=0)

    def send_cols(e):
        for dy, dz in FAR_FIRST:
            pltpu.make_async_remote_copy(
                src_ref=cmsg.at[e], dst_ref=crx.at[e, a], send_sem=csend.at[e], recv_sem=crecv.at[e],
                device_id=(dev_of(dy, dz, 0, core),), device_id_type=MESH,
            ).start()
        crx[e, a] = cmsg[e]

    def row_part(e):
        return pl.ds(0, LINE + 8 if e in (0, 3) else LINE)

    def send_rows(e):
        for dx, other in ((2, 1), (2, 0), (1, 1), (-1, 1), (1, 0), (-1, 0), (0, 1)):
            pltpu.make_async_remote_copy(
                src_ref=rmsg.at[e, row_part(e)], dst_ref=rrx.at[e, b, row_part(e)],
                send_sem=rsend.at[e], recv_sem=rrecv.at[e],
                device_id=(dev_of(0, 0, dx, 1 - core if other else core),), device_id_type=MESH,
            ).start()
        rrx[e, b] = rmsg[e]

    def wait_cols(e):
        every = crx.at[e, pl.ds(0, PLANE - 1)]
        pltpu.make_async_copy(every, every, crecv.at[e]).wait()

    def wait_rows(e):
        every = rrx.at[e, pl.ds(0, LINE - 1), row_part(e)]
        pltpu.make_async_copy(every, every, rrecv.at[e]).wait()

    def send_loss():
        for dy, dz in FAR_FIRST:
            pltpu.make_async_remote_copy(
                src_ref=lmsg, dst_ref=lrx.at[a], send_sem=losem.at[0], recv_sem=losem.at[1],
                device_id=(dev_of(dy, dz, 0, core),), device_id_type=MESH,
            ).start()
        lrx[a] = lmsg[...]

    def merge(v):
        top = jnp.max(v, axis=0)
        return top + log2(jnp.sum(jnp.exp2(v - top[None]), axis=0))

    def row_lse(t):
        pot_c = cvec.at[t - 2]

        def step(i, carry):
            rows = rows_at(i)
            best = tree([s[rows, lanes(k)] + pot_c[k : k + 1, :] for k in range(PLANE)], jnp.maximum)
            mr[rows, :] = best
            acc = None
            for k in range(PLANE):
                p = jnp.exp2(s[rows, lanes(k)] + pot_c[k : k + 1, :] - best)
                acc = p if acc is None else acc + p
            accr[rows, :] = acc
            return carry

        lax.fori_loop(0, steps, step, 0)
        send_row_lse(t)

    def send_row_lse(t):
        out = []
        for g in range(LINE):
            best = mr[pl.ds(g * BLOCK, BLOCK), :].T
            acc = accr[pl.ds(g * BLOCK, BLOCK), :].T
            top = jnp.max(best, axis=0, keepdims=True)
            out.append(top + log2(jnp.sum(acc * jnp.exp2(best - top), axis=0, keepdims=True)))
        rmsg[t - 1, 0:LINE, :] = jnp.concatenate(out, axis=0)
        send_rows(t - 1)

    def col_lse(t):
        pot_r = rvec.at[t - 2]

        def value(rows, k, pr):
            return s[rows, lanes(k)] + pr

        def top_step(i, tops):
            rows = rows_at(i)
            pr = pot_r[rows, :]
            return tuple(jnp.maximum(tops[k], fold(value(rows, k, pr), jnp.maximum)) for k in range(PLANE))

        tops = lax.fori_loop(0, steps, top_step, (low,) * PLANE)
        ctop = jnp.concatenate([jnp.max(v, axis=0, keepdims=True) for v in tops], axis=0)
        cvec[7] = ctop

        def sum_step(i, sums):
            rows = rows_at(i)
            pr = pot_r[rows, :]
            out = []
            for k in range(PLANE):
                p = jnp.exp2(value(rows, k, pr) - cvec[7, k : k + 1, :])
                if t == 3:
                    kept[rows, lanes(k)] = p
                out.append(sums[k] + fold(p, jnp.add))
            return tuple(out)

        sums = lax.fori_loop(0, steps, sum_step, (zero,) * PLANE)
        csum = jnp.concatenate([jnp.sum(v, axis=0, keepdims=True) for v in sums], axis=0)
        cmsg[t - 1] = ctop + log2(csum)
        send_cols(t - 1)

    def take_rows(e):
        wait_rows(e)
        return merge(rrx[e, :, 0:LINE, :])

    def take_cols(e):
        wait_cols(e)
        return merge(crx[e])

    rmsg[...] = jnp.zeros_like(rmsg)
    rmsg[0, LINE : LINE + 8, :] = jnp.broadcast_to(pos[...].astype(F32), (8, BLOCK))
    send_cols(0)
    send_row_lse(1)
    lse_r = take_rows(0)
    pot_r = -0.5 * lse_r
    to_rows(pot_r, rvec.at[0])
    col_lse(2)
    to_rows(lse_r, rvec.at[2])
    to_rows(jnp.concatenate([rrx[0, g, LINE : LINE + 1, :] for g in range(LINE)], axis=0), pr_ref)
    lse_c = take_cols(0)
    pot_c = -0.5 * lse_c
    cvec[2] = lse_c
    cvec[0] = pot_c
    row_lse(2)
    lse_c = take_cols(1)
    pot_c = (pot_c - lse_c) * 0.5
    cvec[3] = lse_c
    cvec[1] = pot_c
    row_lse(3)
    lse_r = take_rows(1)
    pot_r = (pot_r - lse_r) * 0.5
    to_rows(pot_r, rvec.at[1])
    col_lse(3)
    to_rows(lse_r, rvec.at[3])

    first_col = (lax.broadcasted_iota(jnp.int32, (8, BLOCK), 1) + b * BLOCK).astype(F32)
    first_col = jnp.broadcast_to(first_col[0:1], (CH, BLOCK))

    def add_term(t):
        def step(i, carry):
            sums, picked = carry
            rows = rows_at(i)
            if t < 3:
                qr = rvec[5, rows, :]
            else:
                lr = rvec[4, rows, :]
                partner = pr_ref[rows, :] - first_col
            out = []
            for k in range(PLANE):
                if t < 3:
                    term = term2[rows, lanes(k)] * qr
                    w[rows, lanes(k)] = w[rows, lanes(k)] + term
                else:
                    v = s[rows, lanes(k)]
                    term = jnp.exp2(v + cvec[1, k : k + 1, :] - lr)
                    hit = partner == float(k * RROWS)
                    picked = picked + fold(jnp.where(hit, v, 0.0), jnp.add)
                    w[rows, lanes(k)] = jnp.where(hit, term - 2.0, term)
                out.append(sums[k] + fold(term, jnp.add))
            return tuple(out), picked

        return lax.fori_loop(0, steps, step, ((zero,) * PLANE, zero))

    def add_mirror(factor):
        def step(i, carry):
            rows = rows_at(i)
            acc = None
            for k in range(PLANE):
                mirror = kept[rows, lanes(k)] * factor[k : k + 1, :]
                w[rows, lanes(k)] = w[rows, lanes(k)] + mirror
                acc = mirror if acc is None else acc + mirror
            accr[rows, :] = acc
            return carry

        lax.fori_loop(0, steps, step, 0)

    def keep_term():
        def step(i, carry):
            rows = rows_at(i)
            lr = rvec[3, rows, :]
            for k in range(PLANE):
                term2[rows, lanes(k)] = jnp.exp2(s[rows, lanes(k)] + cvec[0, k : k + 1, :] - lr)
            return carry

        lax.fori_loop(0, steps, step, 0)

    def keep_mirror(t):
        def step(i, carry):
            rows = rows_at(i)
            for k in range(PLANE):
                v = s[rows, lanes(k)]
                if t == 2:
                    v = v + rvec[0, rows, :]
                kept[rows, lanes(k)] = jnp.exp2(v - cvec[t + 1, k : k + 1, :])
            return carry

        lax.fori_loop(0, steps, step, 0)

    def add_first_term():
        def step(i, carry):
            rows = rows_at(i)
            lr = rvec[2, rows, :]
            qr = rvec[6, rows, :]
            for k in range(PLANE):
                w[rows, lanes(k)] = w[rows, lanes(k)] + jnp.exp2(s[rows, lanes(k)] - lr) * qr
            return carry

        lax.fori_loop(0, steps, step, 0)

    def round_weights(start, count):
        def step(i, carry):
            rows = rows_at(start + i)
            for k in range(PLANE):
                total = w[rows, lanes(k)] + kept[rows, lanes(k)] * cvec[6, k : k + 1, :]
                wb[rows, lanes(k)] = total.astype(BF16)
            return carry

        lax.fori_loop(0, count, step, 0)

    def col_sums(e, sums):
        cmsg[e] = jnp.concatenate([jnp.sum(v, axis=0, keepdims=True) for v in sums], axis=0)
        send_cols(e)

    to_rows(take_rows(2), rvec.at[4])
    sums, picked = add_term(3)
    col_sums(3, sums)
    keep_term()
    lse_c = take_cols(2)
    pot_c = (pot_c - lse_c) * 0.5
    cvec[4] = jnp.exp2(cvec[7] - lse_c)
    add_mirror(cvec.at[4])
    rmsg[3, 0:LINE, :] = row_sums(accr)
    rmsg[3, LINE : LINE + 8, :] = picked + (2.0 / PLANE) * (pot_c[0:8] + pot_c[8:16])
    send_rows(3)
    keep_mirror(2)
    wait_cols(3)
    cot_c = -1.0 + jnp.sum(crx[3], axis=0)
    cvec[5] = -0.5 * cot_c
    add_mirror(cvec.at[5])
    rmsg[4, 0:LINE, :] = row_sums(accr)
    send_rows(4)
    wait_rows(3)
    cot_r = -1.0 + jnp.sum(rrx[3, :, 0:LINE, :], axis=0)
    to_rows(-0.5 * cot_r, rvec.at[5])
    sums, _ = add_term(2)
    col_sums(4, sums)
    lmsg[...] = jnp.sum(rrx[3, :, LINE : LINE + 8, :], axis=0)
    send_loss()
    keep_mirror(1)
    wait_rows(4)
    cot_r = 0.5 * cot_r + jnp.sum(rrx[4, :, 0:LINE, :], axis=0)
    to_rows(-0.5 * cot_r, rvec.at[6])
    add_first_term()
    wait_cols(4)
    cot_c = 0.5 * cot_c + jnp.sum(crx[4], axis=0)
    cvec[6] = -0.5 * cot_c

    grad_scale = 1.0 / math.sqrt(WIDTH)

    def product(d):
        xx = lax.rem(x + d, SIDE)
        round_weights(xx * (2 * BLOCK // CH), 2 * BLOCK // CH)
        rows = pl.ds(pl.multiple_of(xx * 2 * BLOCK, 2 * BLOCK), 2 * BLOCK)
        left = wb[rows, :]
        for n in range(WIDTH // TILE):
            right = ec[:, :, pl.ds(n * TILE, TILE)].reshape(CCOLS, TILE)
            out = jnp.dot(left, right, preferred_element_type=F32) * grad_scale
            gp[d, :, :, n * TILE : (n + 1) * TILE] = out.reshape(2, BLOCK, TILE)
        pltpu.make_async_remote_copy(
            src_ref=gp.at[d, 1 - core], dst_ref=rb.at[d], send_sem=gsend.at[d], recv_sem=grecv.at[d],
            device_id=(sibling,), device_id_type=MESH,
        ).start()

    def chip_sum(d):
        pltpu.make_async_copy(rb.at[d], rb.at[d], grecv.at[d]).wait()
        return gp[d, core] + rb[d]

    def ring(n, i, dx):
        return pltpu.make_async_remote_copy(
            src_ref=xs.at[n, i], dst_ref=xr.at[i] if n == 0 else parts.at[n - 1, i],
            send_sem=hsend.at[2 * n + i], recv_sem=hrecv.at[2 * n + i],
            device_id=(xdev(dx),), device_id_type=MESH,
        )

    half = WIDTH // 2
    far, direct, near = [[ring(n, i, dx) for i, dx in ((0, 1), (1, -1))] for n in range(3)]

    def product_step(i, carry):
        product(jnp.where(i == 0, 2, jnp.where(i == 1, 1, jnp.where(i == 2, 3, 0))))

        @pl.when(i == 1)
        def _():
            v = chip_sum(2).astype(BF16)
            xs[0, 0] = v[:, :half]
            far[0].start()
            xs[0, 1] = v[:, half:]
            far[1].start()

        @pl.when(i == 2)
        def _():
            v = chip_sum(1)
            xs[1, 0] = v[:, half:].astype(BF16)
            direct[0].start()
            rb[1, :, :half] = v[:, :half]

        @pl.when(i == 3)
        def _():
            v = chip_sum(3)
            xs[1, 1] = v[:, :half].astype(BF16)
            direct[1].start()
            rb[3, :, half:] = v[:, half:]

        return carry

    lax.fori_loop(0, SIDE, product_step, 0)
    far[0].wait_recv()
    xs[2, 0] = (rb[1, :, :half] + xr[0].astype(F32)).astype(BF16)
    near[0].start()
    far[1].wait_recv()
    xs[2, 1] = (rb[3, :, half:] + xr[1].astype(F32)).astype(BF16)
    near[1].start()
    rb[0] = chip_sum(0)
    result = pltpu.make_async_copy(rb.at[0], own, lsem.at[2])
    result.start()
    for c in direct + near:
        c.wait_recv()
    result.wait()

    every = lrx.at[pl.ds(0, PLANE - 1)]
    pltpu.make_async_copy(every, every, losem.at[1]).wait()
    loss[0, 0] = jnp.sum(lrx[...]) * (-LN2 / TOTAL)

    pltpu.make_async_copy(every, every, losem.at[0]).wait()
    sent(8)
    sent(9)
    every = er.at[pl.ds(0, LINE - 1)]
    pltpu.make_async_copy(every, every, xsend).wait()
    for e in range(5):
        every = rrx.at[e, pl.ds(0, LINE - 1), row_part(e)]
        pltpu.make_async_copy(every, every, rsend.at[e]).wait()
        every = crx.at[e, pl.ds(0, PLANE - 1)]
        pltpu.make_async_copy(every, every, csend.at[e]).wait()
    for d in range(SIDE):
        pltpu.make_async_copy(rb.at[d], rb.at[d], gsend.at[d]).wait()
    for c in far + direct + near:
        c.wait_send()


def add_parts(own, parts, total, grad, loss):
    half = WIDTH // 2
    grad[:, :half] = own[:, :half] + parts[0, 1].astype(F32) + parts[1, 0].astype(F32)
    grad[:, half:] = own[:, half:] + parts[0, 0].astype(F32) + parts[1, 1].astype(F32)
    loss[0, 0] = total[0, 0]


def shards(embeddings, positives):
    vec = pltpu.VMEM
    dma = pltpu.SemaphoreType.DMA
    own, parts, total = pl.pallas_call(
        kernel,
        out_shape=(
            jax.ShapeDtypeStruct((BLOCK, WIDTH), F32),
            jax.ShapeDtypeStruct((2, 2, BLOCK, WIDTH // 2), BF16),
            jax.ShapeDtypeStruct((1, 1), F32),
        ),
        in_specs=[pl.BlockSpec(memory_space=pl.ANY), pl.BlockSpec(memory_space=pltpu.VMEM)],
        out_specs=(
            pl.BlockSpec(memory_space=pl.ANY),
            pl.BlockSpec(memory_space=pl.ANY),
            pl.BlockSpec(memory_space=pltpu.SMEM),
        ),
        scratch_shapes=[
            vec((PLANE, BLOCK, WIDTH), BF16),
            vec((LINE, BLOCK, WIDTH), BF16),
            vec((RROWS, CCOLS), F32),
            vec((RROWS, CCOLS), F32),
            vec((RROWS, CCOLS), BF16),
            vec((RROWS, CCOLS), F32),
            vec((RROWS, CCOLS), F32),
            vec((7, RROWS, BLOCK), F32),
            vec((8, PLANE, BLOCK), F32),
            vec((RROWS, BLOCK), F32),
            vec((RROWS, BLOCK), F32),
            vec((RROWS, BLOCK), F32),
            vec((5, PLANE, BLOCK), F32),
            vec((5, PLANE, PLANE, BLOCK), F32),
            vec((5, LINE + 8, BLOCK), F32),
            vec((5, LINE, LINE + 8, BLOCK), F32),
            vec((8, BLOCK), F32),
            vec((PLANE, 8, BLOCK), F32),
            vec((SIDE, 2, BLOCK, WIDTH), F32),
            vec((SIDE, BLOCK, WIDTH), F32),
            vec((3, 2, BLOCK, WIDTH // 2), BF16),
            vec((2, BLOCK, WIDTH // 2), BF16),
            dma((3,)),
            dma((10,)),
            dma((2, 20)),
            dma,
            dma((8,)),
            dma((5,)),
            dma((5,)),
            dma((5,)),
            dma((5,)),
            dma((2,)),
            dma((SIDE,)),
            dma((SIDE,)),
            dma((6,)),
            dma((6,)),
        ],
        compiler_params=pltpu.CompilerParams(
            collective_id=0, has_side_effects=True, vmem_limit_bytes=60 * 1024 * 1024
        ),
    )(embeddings, positives.reshape(1, BLOCK))
    grad, loss = pl.pallas_call(
        add_parts,
        out_shape=(jax.ShapeDtypeStruct((BLOCK, WIDTH), F32), jax.ShapeDtypeStruct((1, 1), F32)),
        grid=(2,),
        in_specs=[
            pl.BlockSpec((BLOCK // 2, WIDTH), lambda i: (i, 0)),
            pl.BlockSpec((2, 2, BLOCK // 2, WIDTH // 2), lambda i: (0, 0, i, 0)),
            pl.BlockSpec(memory_space=pltpu.SMEM),
        ],
        out_specs=(pl.BlockSpec((BLOCK // 2, WIDTH), lambda i: (i, 0)), pl.BlockSpec(memory_space=pltpu.SMEM)),
    )(own, parts, total)
    return loss.reshape(()), grad


def solution(mesh):
    placed = (P("dp", None), P("dp"))
    return jax.shard_map(
        shards, mesh=mesh, in_specs=placed, out_specs=(P(), P("dp", None)), check_vma=False
    )
```

```python
import functools
import math

import jax
import jax.numpy as jnp
from jax import lax
from jax.experimental import pallas as pl
from jax.experimental.pallas import tpu as pltpu
from jax.sharding import PartitionSpec as P

SIDE = 4
PLANE = SIDE * SIDE
LINE = SIDE * 2
BLOCK = 128
WIDTH = 1024
RROWS = LINE * BLOCK
CCOLS = PLANE * BLOCK
TOTAL = PLANE * RROWS
LOG2E = math.log2(math.e)
LN2 = math.log(2.0)
MESH = pl.DeviceIdType.MESH
F32 = jnp.float32
BF16 = jnp.bfloat16
TILE = 256
SCORE_M = 8
CH = 64
OFFS = (0, -1, 1, 2)
OWN_SLOTS = (1, 4, 5, 6)
FORWARD_SLOTS = (3, 7, 8, 9)
FAR_FIRST = sorted(
    ((dy, dz) for dy in OFFS for dz in OFFS if (dy, dz) != (0, 0)), key=lambda d: -abs(d[0]) - abs(d[1])
)


def fold(v, op):
    return tree([v[r : r + 8] for r in range(0, v.shape[0], 8)], op)


def tree(v, op):
    while len(v) > 1:
        v = [op(*v[i : i + 2]) if i + 1 < len(v) else v[i] for i in range(0, len(v), 2)]
    return v[0]


def log2(v):
    return jnp.log(v) * LOG2E


def kernel(
    emb, pos, own, parts, loss,
    ec, er, s, w, wb, kept, term2, rvec, cvec, pr_ref, mr, accr, cmsg, crx, rmsg, rrx,
    lmsg, lrx, gp, rb, xs, xr,
    lsem, psend, prsem, xsend, xrsem, csend, crecv, rsend, rrecv, losem, gsend, grecv, hsend, hrecv,
):
    me = lax.axis_index("dp")
    a = me // LINE
    b = me % LINE
    y, z = a // SIDE, a % SIDE
    x, core = b // 2, b % 2

    def dev_of(dy, dz, dx, c):
        yy, zz, xx = (lax.rem(v + d + SIDE, SIDE) for v, d in ((y, dy), (z, dz), (x, dx)))
        return ((yy * SIDE + zz) * SIDE + xx) * 2 + c

    barrier = pltpu.get_barrier_semaphore()

    near_by = (
        [dev_of(dy, dz, dx, core) for dy, dz, dx in ((1, 0, 0), (-1, 0, 0), (0, 1, 0), (0, -1, 0), (0, 0, 1), (0, 0, -1))]
        + [dev_of(0, 0, 0, 1 - core)]
    )
    for device in near_by:
        pl.semaphore_signal(barrier, inc=1, device_id=(device,), device_id_type=MESH)
    own_c = pltpu.make_async_copy(emb, ec.at[a], lsem.at[0])
    own_r = pltpu.make_async_copy(emb, er.at[b], lsem.at[1])
    own_c.start()
    own_r.start()
    pl.semaphore_wait(barrier, len(near_by))

    def blk(h, op, oq):
        dy, dz = (oq, op) if h == 0 else (op, oq)
        return lax.rem(y + dy + SIDE, SIDE) * SIDE + lax.rem(z + dz + SIDE, SIDE)

    def send_plane(h, op, oq, lo, n, tp, tq, idx, slot):
        k = blk(h, op, oq)
        rows = pl.ds(64 * h + lo, n)
        src = emb.at[rows] if (op, oq) == (0, 0) else ec.at[k, rows]
        pltpu.make_async_remote_copy(
            src_ref=src, dst_ref=ec.at[k, rows], send_sem=psend.at[slot], recv_sem=prsem.at[h, idx],
            device_id=(blk(h, tp, tq) * LINE + b,), device_id_type=MESH,
        ).start()

    def wait_plane(h, op, oq, lo, n, idx):
        ref = ec.at[blk(h, op, oq), pl.ds(64 * h + lo, n)]
        pltpu.make_async_copy(ref, ref, prsem.at[h, idx]).wait()

    def xdev(dx):
        return a * LINE + lax.rem(x + dx + SIDE, SIDE) * 2 + core

    sibling = a * LINE + x * 2 + (1 - core)

    def xblk(dx):
        return lax.rem(x + dx + SIDE, SIDE) * 2 + core

    def send_line(dx, lo, n, device, idx):
        k = xblk(dx)
        rows = pl.ds(lo, n)
        src = emb.at[rows] if dx == 0 else er.at[k, rows]
        pltpu.make_async_remote_copy(
            src_ref=src, dst_ref=er.at[k, rows], send_sem=xsend, recv_sem=xrsem.at[idx],
            device_id=(device,), device_id_type=MESH,
        ).start()

    def wait_line(k, lo, n, idx):
        ref = er.at[k, pl.ds(lo, n)]
        pltpu.make_async_copy(ref, ref, xrsem.at[idx]).wait()

    def issue(slot):
        for h in (0, 1):
            if slot == 0:
                send_plane(h, 0, 0, 0, 64, 1, 0, 0, slot)
                send_plane(h, 0, 0, 0, 64, -1, 0, 1, slot)
            elif slot == 2:
                send_plane(h, -1, 0, 0, 32, 1, 0, 2, slot)
                send_plane(h, 1, 0, 32, 32, -1, 0, 3, slot)
            elif slot in OWN_SLOTS:
                oi = OWN_SLOTS.index(slot)
                send_plane(h, OFFS[oi], 0, 0, 64, 0, 1, 4 + 4 * oi, slot)
                send_plane(h, OFFS[oi], 0, 0, 64, 0, -1, 5 + 4 * oi, slot)
            else:
                oi = FORWARD_SLOTS.index(slot)
                send_plane(h, OFFS[oi], -1, 0, 32, 0, 1, 6 + 4 * oi, slot)
                send_plane(h, OFFS[oi], 1, 32, 32, 0, -1, 7 + 4 * oi, slot)

    def sent(slot):
        ref = ec.at[pl.ds(0, 1 if slot == 2 or slot in FORWARD_SLOTS else 2)]
        pltpu.make_async_copy(ref, ref, psend.at[slot]).wait()

    def arrived(slot):
        for h in (0, 1):
            if slot == 0:
                wait_plane(h, -1, 0, 0, 64, 0)
                wait_plane(h, 1, 0, 0, 64, 1)
            elif slot == 2:
                wait_plane(h, 2, 0, 0, 32, 2)
                wait_plane(h, 2, 0, 32, 32, 3)
            elif slot in OWN_SLOTS:
                oi = OWN_SLOTS.index(slot)
                wait_plane(h, OFFS[oi], -1, 0, 64, 4 + 4 * oi)
                wait_plane(h, OFFS[oi], 1, 0, 64, 5 + 4 * oi)
            else:
                oi = FORWARD_SLOTS.index(slot)
                wait_plane(h, OFFS[oi], 2, 0, 32, 6 + 4 * oi)
                wait_plane(h, OFFS[oi], 2, 32, 32, 7 + 4 * oi)

    issue(0)
    send_line(0, 0, 128, xdev(1), 0)
    send_line(0, 0, 128, xdev(-1), 1)
    send_line(0, 0, 128, sibling, 4)
    issue(1)
    arrived(0)
    sent(0)
    issue(2)
    arrived(1)
    sent(1)
    issue(3)
    wait_line(xblk(-1), 0, 128, 0)
    send_line(-1, 0, 64, xdev(1), 2)
    send_line(-1, 0, 128, sibling, 5)
    wait_line(xblk(1), 0, 128, 1)
    send_line(1, 64, 64, xdev(-1), 3)
    send_line(1, 0, 128, sibling, 6)
    sent(2)
    issue(4)
    sent(3)
    issue(5)
    arrived(2)
    wait_line(xblk(2), 0, 64, 2)
    wait_line(xblk(2), 64, 64, 3)
    send_line(2, 0, 128, sibling, 7)
    for i, dx in enumerate((0, -1, 1, 2)):
        wait_line(lax.rem(x + dx + SIDE, SIDE) * 2 + (1 - core), 0, 128, 4 + i)
    own_c.wait()
    own_r.wait()
    sent(4)
    issue(6)

    eye = lax.broadcasted_iota(jnp.int32, (BLOCK, BLOCK), 0) == lax.broadcasted_iota(jnp.int32, (BLOCK, BLOCK), 1)
    low = jnp.full((8, BLOCK), -3e38, F32)
    zero = jnp.zeros((8, BLOCK), F32)
    steps = RROWS // CH

    def rows_at(i):
        return pl.ds(pl.multiple_of(i * CH, CH), CH)

    score_scale = LOG2E / math.sqrt(WIDTH)

    def score_tile(n):
        right = ec[pl.ds(2 * n, 2)].reshape(2 * BLOCK, WIDTH)
        cols = pl.ds(pl.multiple_of(n * 256, 256), 256)
        for m in range(LINE // SCORE_M):
            left = er[pl.ds(SCORE_M * m, SCORE_M)].reshape(SCORE_M * BLOCK, WIDTH)
            out = lax.dot_general(left, right, (((1,), (1,)), ((), ())), preferred_element_type=F32)
            s[pl.ds(m * SCORE_M * BLOCK, SCORE_M * BLOCK), cols] = out * score_scale

    def first_sums(n):
        two = [pl.ds(pl.multiple_of(n * 256 + k * BLOCK, BLOCK), BLOCK) for k in range(2)]

        def step(i, carry):
            rows = rows_at(i)
            v = [s[rows, c] for c in two]
            old = mr[rows, :]
            top = jnp.maximum(jnp.maximum(v[0], v[1]), old)
            mr[rows, :] = top
            accr[rows, :] = accr[rows, :] * jnp.exp2(old - top) + (jnp.exp2(v[0] - top) + jnp.exp2(v[1] - top))
            out = []
            for k in range(2):
                old, acc = carry[k]
                top = jnp.maximum(old, fold(v[k], jnp.maximum))
                p = [jnp.exp2(v[k][r : r + 8] - top) for r in range(0, CH, 8)]
                out.append((top, acc * jnp.exp2(old - top) + tree(p, jnp.add)))
            return tuple(out)

        sums = lax.fori_loop(0, steps, step, ((low, zero),) * 2)
        for k in range(2):
            each, acc = sums[k]
            top = jnp.max(each, axis=0, keepdims=True)
            cmsg[0, pl.ds(2 * n + k, 1), :] = top + log2(jnp.sum(acc * jnp.exp2(each - top), axis=0, keepdims=True))

    def tile_step(i, carry):
        @pl.when(i == 1)
        def _():
            arrived(3)

        @pl.when(i == 2)
        def _():
            arrived(4)
            sent(5)
            issue(7)
            arrived(5)

        @pl.when(i == 3)
        def _():
            sent(6)
            issue(8)

        @pl.when(i == 4)
        def _():
            arrived(6)
            sent(7)
            issue(9)
            arrived(7)

        @pl.when(i == 5)
        def _():
            arrived(8)

        @pl.when(i == 7)
        def _():
            arrived(9)

        def pick(values):
            out = values[0]
            for k in range(1, 8):
                out = jnp.where(i == k, values[k], out)
            return out

        half = z // 2
        other = pick((0, 1, 0, 0, 1, 1, 0, 1))
        n = lax.rem(y + pick((0, 0, 3, 1, 3, 1, 2, 2)), SIDE) * 2 + lax.rem(half + other, 2)
        score_tile(n)

        @pl.when(i == 0)
        def _():
            dr = pl.ds(pl.multiple_of(b * BLOCK, BLOCK), BLOCK)
            dc = pl.ds(pl.multiple_of(a * BLOCK, BLOCK), BLOCK)
            s[dr, dc] = jnp.where(eye, -30000.0 * LOG2E, s[dr, dc])

        first_sums(n)
        return carry

    mr[...] = jnp.full((RROWS, BLOCK), -3e38, F32)
    accr[...] = jnp.zeros((RROWS, BLOCK), F32)
    lax.fori_loop(0, 8, tile_step, 0)

    def lanes(k):
        return slice(k * BLOCK, (k + 1) * BLOCK)

    def to_rows(v, ref):
        for g in range(LINE):
            ref[pl.ds(g * BLOCK, BLOCK), :] = jnp.broadcast_to(v[g : g + 1], (BLOCK, BLOCK)).T

    def row_sums(ref):
        out = [jnp.sum(ref[pl.ds(g * BLOCK, BLOCK), :].T, axis=0, keepdims=True) for g in range(LINE)]
        return jnp.concatenate(out, axis=0)

    plane_ids = [dev_of(dy, dz, 0, core) for dy, dz in FAR_FIRST]
    line_ids = [
        dev_of(0, 0, dx, 1 - core if other else core)
        for dx, other in ((2, 1), (2, 0), (1, 1), (-1, 1), (1, 0), (-1, 0), (0, 1))
    ]

    def send_cols(e):
        for device in plane_ids:
            pltpu.make_async_remote_copy(
                src_ref=cmsg.at[e], dst_ref=crx.at[e, a], send_sem=csend.at[e], recv_sem=crecv.at[e],
                device_id=(device,), device_id_type=MESH,
            ).start()
        crx[e, a] = cmsg[e]

    def row_part(e):
        return pl.ds(0, LINE + 8 if e in (0, 3) else LINE)

    def send_rows(e):
        for device in line_ids:
            pltpu.make_async_remote_copy(
                src_ref=rmsg.at[e, row_part(e)], dst_ref=rrx.at[e, b, row_part(e)],
                send_sem=rsend.at[e], recv_sem=rrecv.at[e],
                device_id=(device,), device_id_type=MESH,
            ).start()
        rrx[e, b] = rmsg[e]

    def wait_cols(e):
        every = crx.at[e, pl.ds(0, PLANE - 1)]
        pltpu.make_async_copy(every, every, crecv.at[e]).wait()

    def wait_rows(e):
        every = rrx.at[e, pl.ds(0, LINE - 1), row_part(e)]
        pltpu.make_async_copy(every, every, rrecv.at[e]).wait()

    def send_loss():
        for device in plane_ids:
            pltpu.make_async_remote_copy(
                src_ref=lmsg, dst_ref=lrx.at[a], send_sem=losem.at[0], recv_sem=losem.at[1],
                device_id=(device,), device_id_type=MESH,
            ).start()
        lrx[a] = lmsg[...]

    def merge(v):
        top = jnp.max(v, axis=0)
        return top + log2(jnp.sum(jnp.exp2(v - top[None]), axis=0))

    def row_lse(t):
        pot_c = cvec.at[t - 2]

        def step(i, carry):
            rows = rows_at(i)
            best = tree([s[rows, lanes(k)] + pot_c[k : k + 1, :] for k in range(PLANE)], jnp.maximum)
            mr[rows, :] = best
            acc = None
            for k in range(PLANE):
                p = jnp.exp2(s[rows, lanes(k)] + pot_c[k : k + 1, :] - best)
                acc = p if acc is None else acc + p
            accr[rows, :] = acc
            return carry

        lax.fori_loop(0, steps, step, 0)
        send_row_lse(t)

    def send_row_lse(t):
        out = []
        for g in range(LINE):
            best = mr[pl.ds(g * BLOCK, BLOCK), :].T
            acc = accr[pl.ds(g * BLOCK, BLOCK), :].T
            top = jnp.max(best, axis=0, keepdims=True)
            out.append(top + log2(jnp.sum(acc * jnp.exp2(best - top), axis=0, keepdims=True)))
        rmsg[t - 1, 0:LINE, :] = jnp.concatenate(out, axis=0)
        send_rows(t - 1)

    def col_lse(t):
        pot_r = rvec.at[t - 2]

        def value(rows, k, pr):
            return s[rows, lanes(k)] + pr

        def top_step(i, tops):
            rows = rows_at(i)
            pr = pot_r[rows, :]
            return tuple(jnp.maximum(tops[k], fold(value(rows, k, pr), jnp.maximum)) for k in range(PLANE))

        tops = lax.fori_loop(0, steps, top_step, (low,) * PLANE)
        ctop = jnp.concatenate([jnp.max(v, axis=0, keepdims=True) for v in tops], axis=0)
        cvec[7] = ctop

        def sum_step(i, sums):
            rows = rows_at(i)
            pr = pot_r[rows, :]
            out = []
            for k in range(PLANE):
                p = jnp.exp2(value(rows, k, pr) - cvec[7, k : k + 1, :])
                if t == 3:
                    kept[rows, lanes(k)] = p
                out.append(sums[k] + fold(p, jnp.add))
            return tuple(out)

        sums = lax.fori_loop(0, steps, sum_step, (zero,) * PLANE)
        csum = jnp.concatenate([jnp.sum(v, axis=0, keepdims=True) for v in sums], axis=0)
        cmsg[t - 1] = ctop + log2(csum)
        send_cols(t - 1)

    def take_rows(e):
        wait_rows(e)
        return merge(rrx[e, :, 0:LINE, :])

    def take_cols(e):
        wait_cols(e)
        return merge(crx[e])

    rmsg[...] = jnp.zeros_like(rmsg)
    rmsg[0, LINE : LINE + 8, :] = jnp.broadcast_to(pos[...].astype(F32), (8, BLOCK))
    send_cols(0)
    send_row_lse(1)
    lse_r = take_rows(0)
    pot_r = -0.5 * lse_r
    to_rows(pot_r, rvec.at[0])
    col_lse(2)
    to_rows(lse_r, rvec.at[2])
    to_rows(jnp.concatenate([rrx[0, g, LINE : LINE + 1, :] for g in range(LINE)], axis=0), pr_ref)
    lse_c = take_cols(0)
    pot_c = -0.5 * lse_c
    cvec[2] = lse_c
    cvec[0] = pot_c
    row_lse(2)
    lse_c = take_cols(1)
    pot_c = (pot_c - lse_c) * 0.5
    cvec[3] = lse_c
    cvec[1] = pot_c
    row_lse(3)
    lse_r = take_rows(1)
    pot_r = (pot_r - lse_r) * 0.5
    to_rows(pot_r, rvec.at[1])
    col_lse(3)
    to_rows(lse_r, rvec.at[3])

    first_col = (lax.broadcasted_iota(jnp.int32, (8, BLOCK), 1) + b * BLOCK).astype(F32)
    first_col = jnp.broadcast_to(first_col[0:1], (CH, BLOCK))

    def add_term(t):
        def step(i, carry):
            sums, picked = carry
            rows = rows_at(i)
            if t < 3:
                qr = rvec[5, rows, :]
            else:
                lr = rvec[4, rows, :]
                partner = pr_ref[rows, :] - first_col
            out = []
            for k in range(PLANE):
                if t < 3:
                    term = term2[rows, lanes(k)] * qr
                    w[rows, lanes(k)] = w[rows, lanes(k)] + term
                else:
                    v = s[rows, lanes(k)]
                    term = jnp.exp2(v + cvec[1, k : k + 1, :] - lr)
                    hit = partner == float(k * RROWS)
                    picked = picked + fold(jnp.where(hit, v, 0.0), jnp.add)
                    w[rows, lanes(k)] = jnp.where(hit, term - 2.0, term)
                out.append(sums[k] + fold(term, jnp.add))
            return tuple(out), picked

        return lax.fori_loop(0, steps, step, ((zero,) * PLANE, zero))

    def add_mirror(factor):
        def step(i, carry):
            rows = rows_at(i)
            acc = None
            for k in range(PLANE):
                mirror = kept[rows, lanes(k)] * factor[k : k + 1, :]
                w[rows, lanes(k)] = w[rows, lanes(k)] + mirror
                acc = mirror if acc is None else acc + mirror
            accr[rows, :] = acc
            return carry

        lax.fori_loop(0, steps, step, 0)

    def keep_term():
        def step(i, carry):
            rows = rows_at(i)
            lr = rvec[3, rows, :]
            for k in range(PLANE):
                term2[rows, lanes(k)] = jnp.exp2(s[rows, lanes(k)] + cvec[0, k : k + 1, :] - lr)
            return carry

        lax.fori_loop(0, steps, step, 0)

    def keep_mirror(t):
        def step(i, carry):
            rows = rows_at(i)
            for k in range(PLANE):
                v = s[rows, lanes(k)]
                if t == 2:
                    v = v + rvec[0, rows, :]
                kept[rows, lanes(k)] = jnp.exp2(v - cvec[t + 1, k : k + 1, :])
            return carry

        lax.fori_loop(0, steps, step, 0)

    def keep_first_term():
        def step(i, carry):
            rows = rows_at(i)
            lr = rvec[2, rows, :]
            for k in range(PLANE):
                s[rows, lanes(k)] = jnp.exp2(s[rows, lanes(k)] - lr)
            return carry

        lax.fori_loop(0, steps, step, 0)

    def round_weights(start, count):
        def step(i, carry):
            rows = rows_at(start + i)
            qr = rvec[6, rows, :]
            for k in range(PLANE):
                total = w[rows, lanes(k)] + kept[rows, lanes(k)] * cvec[6, k : k + 1, :] + s[rows, lanes(k)] * qr
                wb[rows, lanes(k)] = total.astype(BF16)
            return carry

        lax.fori_loop(0, count, step, 0)

    def col_sums(e, sums):
        cmsg[e] = jnp.concatenate([jnp.sum(v, axis=0, keepdims=True) for v in sums], axis=0)
        send_cols(e)

    to_rows(take_rows(2), rvec.at[4])
    sums, picked = add_term(3)
    col_sums(3, sums)
    keep_term()
    lse_c = take_cols(2)
    pot_c = (pot_c - lse_c) * 0.5
    cvec[4] = jnp.exp2(cvec[7] - lse_c)
    add_mirror(cvec.at[4])
    rmsg[3, 0:LINE, :] = row_sums(accr)
    rmsg[3, LINE : LINE + 8, :] = picked + (2.0 / PLANE) * (pot_c[0:8] + pot_c[8:16])
    send_rows(3)
    keep_mirror(2)
    wait_cols(3)
    cot_c = -1.0 + jnp.sum(crx[3], axis=0)
    cvec[5] = -0.5 * cot_c
    add_mirror(cvec.at[5])
    rmsg[4, 0:LINE, :] = row_sums(accr)
    send_rows(4)
    wait_rows(3)
    cot_r = -1.0 + jnp.sum(rrx[3, :, 0:LINE, :], axis=0)
    to_rows(-0.5 * cot_r, rvec.at[5])
    sums, _ = add_term(2)
    col_sums(4, sums)
    lmsg[...] = jnp.sum(rrx[3, :, LINE : LINE + 8, :], axis=0)
    send_loss()
    keep_mirror(1)
    keep_first_term()
    wait_rows(4)
    cot_r = 0.5 * cot_r + jnp.sum(rrx[4, :, 0:LINE, :], axis=0)
    to_rows(-0.5 * cot_r, rvec.at[6])
    wait_cols(4)
    cot_c = 0.5 * cot_c + jnp.sum(crx[4], axis=0)
    cvec[6] = -0.5 * cot_c

    grad_scale = 1.0 / math.sqrt(WIDTH)

    def product(d, half_of):
        block = lax.rem(x + d, SIDE) * 2 + half_of
        round_weights(block * (BLOCK // CH), BLOCK // CH)
        left = wb[pl.ds(pl.multiple_of(block * BLOCK, BLOCK), BLOCK), :]
        for n in range(WIDTH // TILE):
            right = ec[:, :, pl.ds(n * TILE, TILE)].reshape(CCOLS, TILE)
            out = jnp.dot(left, right, preferred_element_type=F32) * grad_scale
            gp[d, half_of, :, n * TILE : (n + 1) * TILE] = out

    def chip_sum(d):
        pltpu.make_async_copy(rb.at[d], rb.at[d], grecv.at[d]).wait()
        return gp[d, core] + rb[d]

    def ring(n, i, dx):
        return pltpu.make_async_remote_copy(
            src_ref=xs.at[n, i], dst_ref=xr.at[i] if n == 0 else parts.at[n - 1, i],
            send_sem=hsend.at[2 * n + i], recv_sem=hrecv.at[2 * n + i],
            device_id=(xdev(dx),), device_id_type=MESH,
        )

    half = WIDTH // 2
    far, direct, near = [[ring(n, i, dx) for i, dx in ((0, 1), (1, -1))] for n in range(3)]

    def product_step(i, carry):
        step = i // 2
        d = jnp.where(step == 0, 2, jnp.where(step == 1, 1, jnp.where(step == 2, 3, 0)))
        product(d, lax.rem(i + 1 + core, 2))

        @pl.when(lax.rem(i, 2) == 0)
        def _():
            pltpu.make_async_remote_copy(
                src_ref=gp.at[d, 1 - core], dst_ref=rb.at[d], send_sem=gsend.at[d], recv_sem=grecv.at[d],
                device_id=(sibling,), device_id_type=MESH,
            ).start()

        @pl.when(i == 2)
        def _():
            v = chip_sum(2).astype(BF16)
            xs[0, 0] = v[:, :half]
            far[0].start()
            xs[0, 1] = v[:, half:]
            far[1].start()

        @pl.when(i == 4)
        def _():
            v = chip_sum(1)
            xs[1, 0] = v[:, half:].astype(BF16)
            direct[0].start()
            rb[1, :, :half] = v[:, :half]

        @pl.when(i == 6)
        def _():
            v = chip_sum(3)
            xs[1, 1] = v[:, :half].astype(BF16)
            direct[1].start()
            rb[3, :, half:] = v[:, half:]

        return carry

    lax.fori_loop(0, 2 * SIDE, product_step, 0)
    far[0].wait_recv()
    xs[2, 0] = (rb[1, :, :half] + xr[0].astype(F32)).astype(BF16)
    near[0].start()
    far[1].wait_recv()
    xs[2, 1] = (rb[3, :, half:] + xr[1].astype(F32)).astype(BF16)
    near[1].start()
    rb[0] = chip_sum(0)
    result = pltpu.make_async_copy(rb.at[0], own, lsem.at[2])
    result.start()
    for c in direct + near:
        c.wait_recv()
    result.wait()

    every = lrx.at[pl.ds(0, PLANE - 1)]
    pltpu.make_async_copy(every, every, losem.at[1]).wait()
    loss[0, 0] = jnp.sum(lrx[...]) * (-LN2 / TOTAL)

    pltpu.make_async_copy(every, every, losem.at[0]).wait()
    sent(8)
    sent(9)
    every = er.at[pl.ds(0, LINE - 1)]
    pltpu.make_async_copy(every, every, xsend).wait()
    for e in range(5):
        every = rrx.at[e, pl.ds(0, LINE - 1), row_part(e)]
        pltpu.make_async_copy(every, every, rsend.at[e]).wait()
        every = crx.at[e, pl.ds(0, PLANE - 1)]
        pltpu.make_async_copy(every, every, csend.at[e]).wait()
    for d in range(SIDE):
        pltpu.make_async_copy(rb.at[d], rb.at[d], gsend.at[d]).wait()
    for c in far + direct + near:
        c.wait_send()


def add_parts(own, parts, total, grad, loss):
    half = WIDTH // 2
    grad[:, :half] = own[:, :half] + parts[0, 1].astype(F32) + parts[1, 0].astype(F32)
    grad[:, half:] = own[:, half:] + parts[0, 0].astype(F32) + parts[1, 1].astype(F32)
    loss[0, 0] = total[0, 0]


def shards(embeddings, positives):
    vec = pltpu.VMEM
    dma = pltpu.SemaphoreType.DMA
    own, parts, total = pl.pallas_call(
        kernel,
        out_shape=(
            jax.ShapeDtypeStruct((BLOCK, WIDTH), F32),
            jax.ShapeDtypeStruct((2, 2, BLOCK, WIDTH // 2), BF16),
            jax.ShapeDtypeStruct((1, 1), F32),
        ),
        in_specs=[pl.BlockSpec(memory_space=pl.ANY), pl.BlockSpec(memory_space=pltpu.VMEM)],
        out_specs=(
            pl.BlockSpec(memory_space=pl.ANY),
            pl.BlockSpec(memory_space=pl.ANY),
            pl.BlockSpec(memory_space=pltpu.SMEM),
        ),
        scratch_shapes=[
            vec((PLANE, BLOCK, WIDTH), BF16),
            vec((LINE, BLOCK, WIDTH), BF16),
            vec((RROWS, CCOLS), F32),
            vec((RROWS, CCOLS), F32),
            vec((RROWS, CCOLS), BF16),
            vec((RROWS, CCOLS), F32),
            vec((RROWS, CCOLS), F32),
            vec((7, RROWS, BLOCK), F32),
            vec((8, PLANE, BLOCK), F32),
            vec((RROWS, BLOCK), F32),
            vec((RROWS, BLOCK), F32),
            vec((RROWS, BLOCK), F32),
            vec((5, PLANE, BLOCK), F32),
            vec((5, PLANE, PLANE, BLOCK), F32),
            vec((5, LINE + 8, BLOCK), F32),
            vec((5, LINE, LINE + 8, BLOCK), F32),
            vec((8, BLOCK), F32),
            vec((PLANE, 8, BLOCK), F32),
            vec((SIDE, 2, BLOCK, WIDTH), F32),
            vec((SIDE, BLOCK, WIDTH), F32),
            vec((3, 2, BLOCK, WIDTH // 2), BF16),
            vec((2, BLOCK, WIDTH // 2), BF16),
            dma((3,)),
            dma((10,)),
            dma((2, 20)),
            dma,
            dma((8,)),
            dma((5,)),
            dma((5,)),
            dma((5,)),
            dma((5,)),
            dma((2,)),
            dma((SIDE,)),
            dma((SIDE,)),
            dma((6,)),
            dma((6,)),
        ],
        compiler_params=pltpu.CompilerParams(
            collective_id=0, has_side_effects=True, vmem_limit_bytes=60 * 1024 * 1024
        ),
    )(embeddings, positives.reshape(1, BLOCK))
    grad, loss = pl.pallas_call(
        add_parts,
        out_shape=(jax.ShapeDtypeStruct((BLOCK, WIDTH), F32), jax.ShapeDtypeStruct((1, 1), F32)),
        grid=(2,),
        in_specs=[
            pl.BlockSpec((BLOCK // 2, WIDTH), lambda i: (i, 0)),
            pl.BlockSpec((2, 2, BLOCK // 2, WIDTH // 2), lambda i: (0, 0, i, 0)),
            pl.BlockSpec(memory_space=pltpu.SMEM),
        ],
        out_specs=(pl.BlockSpec((BLOCK // 2, WIDTH), lambda i: (i, 0)), pl.BlockSpec(memory_space=pltpu.SMEM)),
    )(own, parts, total)
    return loss.reshape(()), grad


def solution(mesh):
    placed = (P("dp", None), P("dp"))
    return jax.shard_map(
        shards, mesh=mesh, in_specs=placed, out_specs=(P(), P("dp", None)), check_vma=False
    )
```

```python
import functools
import math

import jax
import jax.numpy as jnp
from jax import lax
from jax.experimental import pallas as pl
from jax.experimental.pallas import tpu as pltpu
from jax.sharding import PartitionSpec as P

SIDE = 4
PLANE = SIDE * SIDE
LINE = SIDE * 2
BLOCK = 128
WIDTH = 1024
RROWS = LINE * BLOCK
CCOLS = PLANE * BLOCK
TOTAL = PLANE * RROWS
LOG2E = math.log2(math.e)
LN2 = math.log(2.0)
MESH = pl.DeviceIdType.MESH
F32 = jnp.float32
BF16 = jnp.bfloat16
TILE = 256
SCORE_M = 8
CH = 64
OFFS = (0, -1, 1, 2)
OWN_SLOTS = (1, 4, 5, 6)
FORWARD_SLOTS = (3, 7, 8, 9)
FAR_FIRST = sorted(
    ((dy, dz) for dy in OFFS for dz in OFFS if (dy, dz) != (0, 0)), key=lambda d: -abs(d[0]) - abs(d[1])
)


def fold(v, op):
    return tree([v[r : r + 8] for r in range(0, v.shape[0], 8)], op)


def tree(v, op):
    while len(v) > 1:
        v = [op(*v[i : i + 2]) if i + 1 < len(v) else v[i] for i in range(0, len(v), 2)]
    return v[0]


def log2(v):
    return jnp.log(v) * LOG2E


def kernel(
    emb, pos, own, parts, loss,
    ec, er, s, w, wb, kept, term2, rvec, cvec, pr_ref, mr, accr, cmsg, crx, rmsg, rrx,
    lmsg, lrx, gp, rb, xs, xr,
    lsem, psend, prsem, xsend, xrsem, csend, crecv, rsend, rrecv, losem, gsend, grecv, hsend, hrecv,
):
    me = lax.axis_index("dp")
    a = me // LINE
    b = me % LINE
    y, z = a // SIDE, a % SIDE
    x, core = b // 2, b % 2

    def dev_of(dy, dz, dx, c):
        yy, zz, xx = (lax.rem(v + d + SIDE, SIDE) for v, d in ((y, dy), (z, dz), (x, dx)))
        return ((yy * SIDE + zz) * SIDE + xx) * 2 + c

    barrier = pltpu.get_barrier_semaphore()

    near_by = (
        [dev_of(dy, dz, dx, core) for dy, dz, dx in ((1, 0, 0), (-1, 0, 0), (0, 1, 0), (0, -1, 0), (0, 0, 1), (0, 0, -1))]
        + [dev_of(0, 0, 0, 1 - core)]
    )
    for device in near_by:
        pl.semaphore_signal(barrier, inc=1, device_id=(device,), device_id_type=MESH)
    own_c = pltpu.make_async_copy(emb, ec.at[a], lsem.at[0])
    own_r = pltpu.make_async_copy(emb, er.at[b], lsem.at[1])
    own_c.start()
    own_r.start()
    pl.semaphore_wait(barrier, len(near_by))

    def blk(h, op, oq):
        dy, dz = (oq, op) if h == 0 else (op, oq)
        return lax.rem(y + dy + SIDE, SIDE) * SIDE + lax.rem(z + dz + SIDE, SIDE)

    def send_plane(h, op, oq, lo, n, tp, tq, idx, slot):
        k = blk(h, op, oq)
        rows = pl.ds(64 * h + lo, n)
        src = emb.at[rows] if (op, oq) == (0, 0) else ec.at[k, rows]
        pltpu.make_async_remote_copy(
            src_ref=src, dst_ref=ec.at[k, rows], send_sem=psend.at[slot], recv_sem=prsem.at[h, idx],
            device_id=(blk(h, tp, tq) * LINE + b,), device_id_type=MESH,
        ).start()

    def wait_plane(h, op, oq, lo, n, idx):
        ref = ec.at[blk(h, op, oq), pl.ds(64 * h + lo, n)]
        pltpu.make_async_copy(ref, ref, prsem.at[h, idx]).wait()

    def xdev(dx):
        return a * LINE + lax.rem(x + dx + SIDE, SIDE) * 2 + core

    sibling = a * LINE + x * 2 + (1 - core)

    def xblk(dx):
        return lax.rem(x + dx + SIDE, SIDE) * 2 + core

    def send_line(dx, lo, n, device, idx):
        k = xblk(dx)
        rows = pl.ds(lo, n)
        src = emb.at[rows] if dx == 0 else er.at[k, rows]
        pltpu.make_async_remote_copy(
            src_ref=src, dst_ref=er.at[k, rows], send_sem=xsend, recv_sem=xrsem.at[idx],
            device_id=(device,), device_id_type=MESH,
        ).start()

    def wait_line(k, lo, n, idx):
        ref = er.at[k, pl.ds(lo, n)]
        pltpu.make_async_copy(ref, ref, xrsem.at[idx]).wait()

    def issue(slot):
        for h in (0, 1):
            if slot == 0:
                send_plane(h, 0, 0, 0, 64, 1, 0, 0, slot)
                send_plane(h, 0, 0, 0, 64, -1, 0, 1, slot)
            elif slot == 2:
                send_plane(h, -1, 0, 0, 32, 1, 0, 2, slot)
                send_plane(h, 1, 0, 32, 32, -1, 0, 3, slot)
            elif slot in OWN_SLOTS:
                oi = OWN_SLOTS.index(slot)
                send_plane(h, OFFS[oi], 0, 0, 64, 0, 1, 4 + 4 * oi, slot)
                send_plane(h, OFFS[oi], 0, 0, 64, 0, -1, 5 + 4 * oi, slot)
            else:
                oi = FORWARD_SLOTS.index(slot)
                send_plane(h, OFFS[oi], -1, 0, 32, 0, 1, 6 + 4 * oi, slot)
                send_plane(h, OFFS[oi], 1, 32, 32, 0, -1, 7 + 4 * oi, slot)

    def sent(slot):
        ref = ec.at[pl.ds(0, 1 if slot == 2 or slot in FORWARD_SLOTS else 2)]
        pltpu.make_async_copy(ref, ref, psend.at[slot]).wait()

    def arrived(slot):
        for h in (0, 1):
            if slot == 0:
                wait_plane(h, -1, 0, 0, 64, 0)
                wait_plane(h, 1, 0, 0, 64, 1)
            elif slot == 2:
                wait_plane(h, 2, 0, 0, 32, 2)
                wait_plane(h, 2, 0, 32, 32, 3)
            elif slot in OWN_SLOTS:
                oi = OWN_SLOTS.index(slot)
                wait_plane(h, OFFS[oi], -1, 0, 64, 4 + 4 * oi)
                wait_plane(h, OFFS[oi], 1, 0, 64, 5 + 4 * oi)
            else:
                oi = FORWARD_SLOTS.index(slot)
                wait_plane(h, OFFS[oi], 2, 0, 32, 6 + 4 * oi)
                wait_plane(h, OFFS[oi], 2, 32, 32, 7 + 4 * oi)

    issue(0)
    send_line(0, 0, 128, xdev(1), 0)
    send_line(0, 0, 128, xdev(-1), 1)
    send_line(0, 0, 128, sibling, 4)
    issue(1)
    arrived(0)
    sent(0)
    issue(2)
    arrived(1)
    sent(1)
    issue(3)
    wait_line(xblk(-1), 0, 128, 0)
    send_line(-1, 0, 64, xdev(1), 2)
    send_line(-1, 0, 128, sibling, 5)
    wait_line(xblk(1), 0, 128, 1)
    send_line(1, 64, 64, xdev(-1), 3)
    send_line(1, 0, 128, sibling, 6)
    sent(2)
    issue(4)
    issue(5)
    sent(3)
    arrived(2)
    wait_line(xblk(2), 0, 64, 2)
    wait_line(xblk(2), 64, 64, 3)
    send_line(2, 0, 128, sibling, 7)
    for i, dx in enumerate((0, -1, 1, 2)):
        wait_line(lax.rem(x + dx + SIDE, SIDE) * 2 + (1 - core), 0, 128, 4 + i)
    own_c.wait()
    own_r.wait()
    sent(4)
    issue(6)

    eye = lax.broadcasted_iota(jnp.int32, (BLOCK, BLOCK), 0) == lax.broadcasted_iota(jnp.int32, (BLOCK, BLOCK), 1)
    low = jnp.full((8, BLOCK), -3e38, F32)
    zero = jnp.zeros((8, BLOCK), F32)
    steps = RROWS // CH

    def rows_at(i):
        return pl.ds(pl.multiple_of(i * CH, CH), CH)

    score_scale = LOG2E / math.sqrt(WIDTH)

    def score_tile(n):
        right = ec[pl.ds(2 * n, 2)].reshape(2 * BLOCK, WIDTH)
        cols = pl.ds(pl.multiple_of(n * 256, 256), 256)
        for m in range(LINE // SCORE_M):
            left = er[pl.ds(SCORE_M * m, SCORE_M)].reshape(SCORE_M * BLOCK, WIDTH)
            out = lax.dot_general(left, right, (((1,), (1,)), ((), ())), preferred_element_type=F32)
            s[pl.ds(m * SCORE_M * BLOCK, SCORE_M * BLOCK), cols] = out * score_scale

    def first_sums(n):
        two = [pl.ds(pl.multiple_of(n * 256 + k * BLOCK, BLOCK), BLOCK) for k in range(2)]

        def step(i, carry):
            rows = rows_at(i)
            v = [s[rows, c] for c in two]
            old = mr[rows, :]
            top = jnp.maximum(jnp.maximum(v[0], v[1]), old)
            mr[rows, :] = top
            accr[rows, :] = accr[rows, :] * jnp.exp2(old - top) + (jnp.exp2(v[0] - top) + jnp.exp2(v[1] - top))
            out = []
            for k in range(2):
                old, acc = carry[k]
                top = jnp.maximum(old, fold(v[k], jnp.maximum))
                p = [jnp.exp2(v[k][r : r + 8] - top) for r in range(0, CH, 8)]
                out.append((top, acc * jnp.exp2(old - top) + tree(p, jnp.add)))
            return tuple(out)

        sums = lax.fori_loop(0, steps, step, ((low, zero),) * 2)
        for k in range(2):
            each, acc = sums[k]
            top = jnp.max(each, axis=0, keepdims=True)
            cmsg[0, pl.ds(2 * n + k, 1), :] = top + log2(jnp.sum(acc * jnp.exp2(each - top), axis=0, keepdims=True))

    def tile_step(i, carry):
        @pl.when(i == 1)
        def _():
            arrived(3)

        @pl.when(i == 2)
        def _():
            arrived(4)
            sent(5)
            issue(7)
            arrived(5)

        @pl.when(i == 3)
        def _():
            sent(6)
            issue(8)

        @pl.when(i == 4)
        def _():
            arrived(6)
            sent(7)
            issue(9)
            arrived(7)

        @pl.when(i == 5)
        def _():
            arrived(8)

        @pl.when(i == 7)
        def _():
            arrived(9)

        def pick(values):
            out = values[0]
            for k in range(1, 8):
                out = jnp.where(i == k, values[k], out)
            return out

        half = z // 2
        other = pick((0, 1, 0, 0, 1, 1, 0, 1))
        n = lax.rem(y + pick((0, 0, 3, 1, 3, 1, 2, 2)), SIDE) * 2 + lax.rem(half + other, 2)
        score_tile(n)

        @pl.when(i == 0)
        def _():
            dr = pl.ds(pl.multiple_of(b * BLOCK, BLOCK), BLOCK)
            dc = pl.ds(pl.multiple_of(a * BLOCK, BLOCK), BLOCK)
            s[dr, dc] = jnp.where(eye, -30000.0 * LOG2E, s[dr, dc])

        first_sums(n)
        return carry

    mr[...] = jnp.full((RROWS, BLOCK), -3e38, F32)
    accr[...] = jnp.zeros((RROWS, BLOCK), F32)
    lax.fori_loop(0, 8, tile_step, 0)

    def lanes(k):
        return slice(k * BLOCK, (k + 1) * BLOCK)

    def to_rows(v, ref):
        for g in range(LINE):
            ref[pl.ds(g * BLOCK, BLOCK), :] = jnp.broadcast_to(v[g : g + 1], (BLOCK, BLOCK)).T

    def row_sums(ref):
        out = [jnp.sum(ref[pl.ds(g * BLOCK, BLOCK), :].T, axis=0, keepdims=True) for g in range(LINE)]
        return jnp.concatenate(out, axis=0)

    plane_ids = [dev_of(dy, dz, 0, core) for dy, dz in FAR_FIRST]
    line_ids = [
        dev_of(0, 0, dx, 1 - core if other else core)
        for dx, other in ((2, 1), (2, 0), (1, 1), (-1, 1), (1, 0), (-1, 0), (0, 1))
    ]

    def send_cols(e):
        for device in plane_ids:
            pltpu.make_async_remote_copy(
                src_ref=cmsg.at[e], dst_ref=crx.at[e, a], send_sem=csend.at[e], recv_sem=crecv.at[e],
                device_id=(device,), device_id_type=MESH,
            ).start()
        crx[e, a] = cmsg[e]

    def row_part(e):
        return pl.ds(0, LINE + 8 if e in (0, 3) else LINE)

    def send_rows(e):
        for device in line_ids:
            pltpu.make_async_remote_copy(
                src_ref=rmsg.at[e, row_part(e)], dst_ref=rrx.at[e, b, row_part(e)],
                send_sem=rsend.at[e], recv_sem=rrecv.at[e],
                device_id=(device,), device_id_type=MESH,
            ).start()
        rrx[e, b] = rmsg[e]

    def wait_cols(e):
        every = crx.at[e, pl.ds(0, PLANE - 1)]
        pltpu.make_async_copy(every, every, crecv.at[e]).wait()

    def wait_rows(e):
        every = rrx.at[e, pl.ds(0, LINE - 1), row_part(e)]
        pltpu.make_async_copy(every, every, rrecv.at[e]).wait()

    def send_loss():
        for device in plane_ids:
            pltpu.make_async_remote_copy(
                src_ref=lmsg, dst_ref=lrx.at[a], send_sem=losem.at[0], recv_sem=losem.at[1],
                device_id=(device,), device_id_type=MESH,
            ).start()
        lrx[a] = lmsg[...]

    def merge(v):
        top = jnp.max(v, axis=0)
        return top + log2(jnp.sum(jnp.exp2(v - top[None]), axis=0))

    def row_lse(t):
        pot_c = cvec.at[t - 2]

        def step(i, carry):
            rows = rows_at(i)
            best = tree([s[rows, lanes(k)] + pot_c[k : k + 1, :] for k in range(PLANE)], jnp.maximum)
            mr[rows, :] = best
            acc = None
            for k in range(PLANE):
                p = jnp.exp2(s[rows, lanes(k)] + pot_c[k : k + 1, :] - best)
                acc = p if acc is None else acc + p
            accr[rows, :] = acc
            return carry

        lax.fori_loop(0, steps, step, 0)
        send_row_lse(t)

    def send_row_lse(t):
        out = []
        for g in range(LINE):
            best = mr[pl.ds(g * BLOCK, BLOCK), :].T
            acc = accr[pl.ds(g * BLOCK, BLOCK), :].T
            top = jnp.max(best, axis=0, keepdims=True)
            out.append(top + log2(jnp.sum(acc * jnp.exp2(best - top), axis=0, keepdims=True)))
        rmsg[t - 1, 0:LINE, :] = jnp.concatenate(out, axis=0)
        send_rows(t - 1)

    def col_lse(t):
        pot_r = rvec.at[t - 2]

        def value(rows, k, pr):
            return s[rows, lanes(k)] + pr

        def top_step(i, tops):
            rows = rows_at(i)
            pr = pot_r[rows, :]
            return tuple(jnp.maximum(tops[k], fold(value(rows, k, pr), jnp.maximum)) for k in range(PLANE))

        tops = lax.fori_loop(0, steps, top_step, (low,) * PLANE)
        ctop = jnp.concatenate([jnp.max(v, axis=0, keepdims=True) for v in tops], axis=0)
        cvec[7] = ctop

        def sum_step(i, sums):
            rows = rows_at(i)
            pr = pot_r[rows, :]
            out = []
            for k in range(PLANE):
                p = jnp.exp2(value(rows, k, pr) - cvec[7, k : k + 1, :])
                if t == 3:
                    kept[rows, lanes(k)] = p
                out.append(sums[k] + fold(p, jnp.add))
            return tuple(out)

        sums = lax.fori_loop(0, steps, sum_step, (zero,) * PLANE)
        csum = jnp.concatenate([jnp.sum(v, axis=0, keepdims=True) for v in sums], axis=0)
        cmsg[t - 1] = ctop + log2(csum)
        send_cols(t - 1)

    def take_rows(e):
        wait_rows(e)
        return merge(rrx[e, :, 0:LINE, :])

    def take_cols(e):
        wait_cols(e)
        return merge(crx[e])

    rmsg[...] = jnp.zeros_like(rmsg)
    rmsg[0, LINE : LINE + 8, :] = jnp.broadcast_to(pos[...].astype(F32), (8, BLOCK))
    send_cols(0)
    send_row_lse(1)
    lse_r = take_rows(0)
    pot_r = -0.5 * lse_r
    to_rows(pot_r, rvec.at[0])
    col_lse(2)
    to_rows(lse_r, rvec.at[2])
    to_rows(jnp.concatenate([rrx[0, g, LINE : LINE + 1, :] for g in range(LINE)], axis=0), pr_ref)
    lse_c = take_cols(0)
    pot_c = -0.5 * lse_c
    cvec[2] = lse_c
    cvec[0] = pot_c
    row_lse(2)
    lse_c = take_cols(1)
    pot_c = (pot_c - lse_c) * 0.5
    cvec[3] = lse_c
    cvec[1] = pot_c
    row_lse(3)
    lse_r = take_rows(1)
    pot_r = (pot_r - lse_r) * 0.5
    to_rows(pot_r, rvec.at[1])
    col_lse(3)
    to_rows(lse_r, rvec.at[3])

    first_col = (lax.broadcasted_iota(jnp.int32, (8, BLOCK), 1) + b * BLOCK).astype(F32)
    first_col = jnp.broadcast_to(first_col[0:1], (CH, BLOCK))

    def add_term(t):
        def step(i, carry):
            sums, picked = carry
            rows = rows_at(i)
            if t < 3:
                qr = rvec[5, rows, :]
            else:
                lr = rvec[4, rows, :]
                partner = pr_ref[rows, :] - first_col
            out = []
            for k in range(PLANE):
                if t < 3:
                    term = term2[rows, lanes(k)] * qr
                    w[rows, lanes(k)] = w[rows, lanes(k)] + term
                else:
                    v = s[rows, lanes(k)]
                    term = jnp.exp2(v + cvec[1, k : k + 1, :] - lr)
                    hit = partner == float(k * RROWS)
                    picked = picked + fold(jnp.where(hit, v, 0.0), jnp.add)
                    w[rows, lanes(k)] = jnp.where(hit, term - 2.0, term)
                out.append(sums[k] + fold(term, jnp.add))
            return tuple(out), picked

        return lax.fori_loop(0, steps, step, ((zero,) * PLANE, zero))

    def add_mirror(factor):
        def step(i, carry):
            rows = rows_at(i)
            acc = None
            for k in range(PLANE):
                mirror = kept[rows, lanes(k)] * factor[k : k + 1, :]
                w[rows, lanes(k)] = w[rows, lanes(k)] + mirror
                acc = mirror if acc is None else acc + mirror
            accr[rows, :] = acc
            return carry

        lax.fori_loop(0, steps, step, 0)

    def keep_term():
        def step(i, carry):
            rows = rows_at(i)
            lr = rvec[3, rows, :]
            for k in range(PLANE):
                term2[rows, lanes(k)] = jnp.exp2(s[rows, lanes(k)] + cvec[0, k : k + 1, :] - lr)
            return carry

        lax.fori_loop(0, steps, step, 0)

    def keep_mirror(t):
        def step(i, carry):
            rows = rows_at(i)
            for k in range(PLANE):
                v = s[rows, lanes(k)]
                if t == 2:
                    v = v + rvec[0, rows, :]
                kept[rows, lanes(k)] = jnp.exp2(v - cvec[t + 1, k : k + 1, :])
            return carry

        lax.fori_loop(0, steps, step, 0)

    def keep_first_term():
        def step(i, carry):
            rows = rows_at(i)
            lr = rvec[2, rows, :]
            for k in range(PLANE):
                s[rows, lanes(k)] = jnp.exp2(s[rows, lanes(k)] - lr)
            return carry

        lax.fori_loop(0, steps, step, 0)

    def round_weights(start, count):
        def step(i, carry):
            rows = rows_at(start + i)
            qr = rvec[6, rows, :]
            for k in range(PLANE):
                total = w[rows, lanes(k)] + kept[rows, lanes(k)] * cvec[6, k : k + 1, :] + s[rows, lanes(k)] * qr
                wb[rows, lanes(k)] = total.astype(BF16)
            return carry

        lax.fori_loop(0, count, step, 0)

    def col_sums(e, sums):
        cmsg[e] = jnp.concatenate([jnp.sum(v, axis=0, keepdims=True) for v in sums], axis=0)
        send_cols(e)

    to_rows(take_rows(2), rvec.at[4])
    sums, picked = add_term(3)
    col_sums(3, sums)
    keep_term()
    lse_c = take_cols(2)
    pot_c = (pot_c - lse_c) * 0.5
    cvec[4] = jnp.exp2(cvec[7] - lse_c)
    add_mirror(cvec.at[4])
    rmsg[3, 0:LINE, :] = row_sums(accr)
    rmsg[3, LINE : LINE + 8, :] = picked + (2.0 / PLANE) * (pot_c[0:8] + pot_c[8:16])
    send_rows(3)
    keep_mirror(2)
    wait_cols(3)
    cot_c = -1.0 + jnp.sum(crx[3], axis=0)
    cvec[5] = -0.5 * cot_c
    add_mirror(cvec.at[5])
    rmsg[4, 0:LINE, :] = row_sums(accr)
    send_rows(4)
    wait_rows(3)
    cot_r = -1.0 + jnp.sum(rrx[3, :, 0:LINE, :], axis=0)
    to_rows(-0.5 * cot_r, rvec.at[5])
    sums, _ = add_term(2)
    col_sums(4, sums)
    lmsg[...] = jnp.sum(rrx[3, :, LINE : LINE + 8, :], axis=0)
    send_loss()
    keep_mirror(1)
    keep_first_term()
    wait_rows(4)
    cot_r = 0.5 * cot_r + jnp.sum(rrx[4, :, 0:LINE, :], axis=0)
    to_rows(-0.5 * cot_r, rvec.at[6])
    wait_cols(4)
    cot_c = 0.5 * cot_c + jnp.sum(crx[4], axis=0)
    cvec[6] = -0.5 * cot_c

    grad_scale = 1.0 / math.sqrt(WIDTH)

    def product(d, half_of):
        block = lax.rem(x + d, SIDE) * 2 + half_of
        round_weights(block * (BLOCK // CH), BLOCK // CH)
        left = wb[pl.ds(pl.multiple_of(block * BLOCK, BLOCK), BLOCK), :]
        for n in range(WIDTH // TILE):
            right = ec[:, :, pl.ds(n * TILE, TILE)].reshape(CCOLS, TILE)
            out = jnp.dot(left, right, preferred_element_type=F32) * grad_scale
            gp[d, half_of, :, n * TILE : (n + 1) * TILE] = out

    def chip_sum(d):
        pltpu.make_async_copy(rb.at[d], rb.at[d], grecv.at[d]).wait()
        return gp[d, core] + rb[d]

    def ring(n, i, dx):
        return pltpu.make_async_remote_copy(
            src_ref=xs.at[n, i], dst_ref=xr.at[i] if n == 0 else parts.at[n - 1, i],
            send_sem=hsend.at[2 * n + i], recv_sem=hrecv.at[2 * n + i],
            device_id=(xdev(dx),), device_id_type=MESH,
        )

    half = WIDTH // 2
    far, direct, near = [[ring(n, i, dx) for i, dx in ((0, 1), (1, -1))] for n in range(3)]

    def product_step(i, carry):
        step = i // 2
        d = jnp.where(step == 0, 2, jnp.where(step == 1, 1, jnp.where(step == 2, 3, 0)))
        product(d, lax.rem(i + 1 + core, 2))

        @pl.when(lax.rem(i, 2) == 0)
        def _():
            pltpu.make_async_remote_copy(
                src_ref=gp.at[d, 1 - core], dst_ref=rb.at[d], send_sem=gsend.at[d], recv_sem=grecv.at[d],
                device_id=(sibling,), device_id_type=MESH,
            ).start()

        @pl.when(i == 2)
        def _():
            v = chip_sum(2).astype(BF16)
            xs[0, 0] = v[:, :half]
            far[0].start()
            xs[0, 1] = v[:, half:]
            far[1].start()

        @pl.when(i == 4)
        def _():
            v = chip_sum(1)
            xs[1, 0] = v[:, half:].astype(BF16)
            direct[0].start()
            rb[1, :, :half] = v[:, :half]

        @pl.when(i == 6)
        def _():
            v = chip_sum(3)
            xs[1, 1] = v[:, :half].astype(BF16)
            direct[1].start()
            rb[3, :, half:] = v[:, half:]

        return carry

    lax.fori_loop(0, 2 * SIDE, product_step, 0)
    far[0].wait_recv()
    xs[2, 0] = (rb[1, :, :half] + xr[0].astype(F32)).astype(BF16)
    near[0].start()
    far[1].wait_recv()
    xs[2, 1] = (rb[3, :, half:] + xr[1].astype(F32)).astype(BF16)
    near[1].start()
    rb[0] = chip_sum(0)
    result = pltpu.make_async_copy(rb.at[0], own, lsem.at[2])
    result.start()
    every = lrx.at[pl.ds(0, PLANE - 1)]
    pltpu.make_async_copy(every, every, losem.at[1]).wait()
    loss[0, 0] = jnp.sum(lrx[...]) * (-LN2 / TOTAL)

    pltpu.make_async_copy(every, every, losem.at[0]).wait()
    sent(8)
    sent(9)
    every = er.at[pl.ds(0, LINE - 1)]
    pltpu.make_async_copy(every, every, xsend).wait()
    for e in range(5):
        every = rrx.at[e, pl.ds(0, LINE - 1), row_part(e)]
        pltpu.make_async_copy(every, every, rsend.at[e]).wait()
        every = crx.at[e, pl.ds(0, PLANE - 1)]
        pltpu.make_async_copy(every, every, csend.at[e]).wait()
    for d in range(SIDE):
        pltpu.make_async_copy(rb.at[d], rb.at[d], gsend.at[d]).wait()
    for c in far:
        c.wait_send()
    result.wait()
    for c in direct + near:
        c.wait()


def add_parts(own, parts, total, grad, loss):
    half = WIDTH // 2
    grad[:, :half] = own[:, :half] + parts[0, 1].astype(F32) + parts[1, 0].astype(F32)
    grad[:, half:] = own[:, half:] + parts[0, 0].astype(F32) + parts[1, 1].astype(F32)
    loss[0, 0] = total[0, 0]


def shards(embeddings, positives):
    vec = pltpu.VMEM
    dma = pltpu.SemaphoreType.DMA
    own, parts, total = pl.pallas_call(
        kernel,
        out_shape=(
            jax.ShapeDtypeStruct((BLOCK, WIDTH), F32),
            jax.ShapeDtypeStruct((2, 2, BLOCK, WIDTH // 2), BF16),
            jax.ShapeDtypeStruct((1, 1), F32),
        ),
        in_specs=[pl.BlockSpec(memory_space=pl.ANY), pl.BlockSpec(memory_space=pltpu.VMEM)],
        out_specs=(
            pl.BlockSpec(memory_space=pl.ANY),
            pl.BlockSpec(memory_space=pl.ANY),
            pl.BlockSpec(memory_space=pltpu.SMEM),
        ),
        scratch_shapes=[
            vec((PLANE, BLOCK, WIDTH), BF16),
            vec((LINE, BLOCK, WIDTH), BF16),
            vec((RROWS, CCOLS), F32),
            vec((RROWS, CCOLS), F32),
            vec((RROWS, CCOLS), BF16),
            vec((RROWS, CCOLS), F32),
            vec((RROWS, CCOLS), F32),
            vec((7, RROWS, BLOCK), F32),
            vec((8, PLANE, BLOCK), F32),
            vec((RROWS, BLOCK), F32),
            vec((RROWS, BLOCK), F32),
            vec((RROWS, BLOCK), F32),
            vec((5, PLANE, BLOCK), F32),
            vec((5, PLANE, PLANE, BLOCK), F32),
            vec((5, LINE + 8, BLOCK), F32),
            vec((5, LINE, LINE + 8, BLOCK), F32),
            vec((8, BLOCK), F32),
            vec((PLANE, 8, BLOCK), F32),
            vec((SIDE, 2, BLOCK, WIDTH), F32),
            vec((SIDE, BLOCK, WIDTH), F32),
            vec((3, 2, BLOCK, WIDTH // 2), BF16),
            vec((2, BLOCK, WIDTH // 2), BF16),
            dma((3,)),
            dma((10,)),
            dma((2, 20)),
            dma,
            dma((8,)),
            dma((5,)),
            dma((5,)),
            dma((5,)),
            dma((5,)),
            dma((2,)),
            dma((SIDE,)),
            dma((SIDE,)),
            dma((6,)),
            dma((6,)),
        ],
        compiler_params=pltpu.CompilerParams(
            collective_id=0, has_side_effects=True, vmem_limit_bytes=60 * 1024 * 1024
        ),
    )(embeddings, positives.reshape(1, BLOCK))
    grad, loss = pl.pallas_call(
        add_parts,
        out_shape=(jax.ShapeDtypeStruct((BLOCK, WIDTH), F32), jax.ShapeDtypeStruct((1, 1), F32)),
        grid=(2,),
        in_specs=[
            pl.BlockSpec((BLOCK // 2, WIDTH), lambda i: (i, 0)),
            pl.BlockSpec((2, 2, BLOCK // 2, WIDTH // 2), lambda i: (0, 0, i, 0)),
            pl.BlockSpec(memory_space=pltpu.SMEM),
        ],
        out_specs=(pl.BlockSpec((BLOCK // 2, WIDTH), lambda i: (i, 0)), pl.BlockSpec(memory_space=pltpu.SMEM)),
    )(own, parts, total)
    return loss.reshape(()), grad


def solution(mesh):
    placed = (P("dp", None), P("dp"))
    return jax.shard_map(
        shards, mesh=mesh, in_specs=placed, out_specs=(P(), P("dp", None)), check_vma=False
    )
```
